32 devices in a mesh: replica: 4 (over x, core), group: 8 (over z, y).
Axes of the slice: x: 2, y: 2, z: 4, core: 2. Of those that a mesh axis runs over, the one named last changes fastest.
Arguments:
- tokens: bfloat16 [32768, 1024], P(('replica', 'group')), may hold values from -6 to 6
- segment_ids: int32 [64, 512], P(('replica', 'group')), may hold values from 0 to 7, never falling along the last dimension, each value on 1 to 256 neighbouring positions
- w_query: bfloat16 [1024, 1024], P(('replica', 'group')), may hold values from -0.1875 to 0.1875
- b_query: bfloat16 [1024], P(('replica', 'group')), may hold values from -3 to 3
- w_key: bfloat16 [1024, 1024], P(('replica', 'group')), may hold values from -0.1875 to 0.1875
- w_value: bfloat16 [1024, 1024], P(('replica', 'group')), may hold values from -0.1875 to 0.1875
- b_value: bfloat16 [1024], P(('replica', 'group')), may hold values from -3 to 3
- w_out: bfloat16 [1024, 1024], P(('replica', 'group')), may hold values from -0.75 to 0.75
- b_out: bfloat16 [1024], P(('replica', 'group')), may hold values from -3 to 3
- gain_first: bfloat16 [1024], P(('replica', 'group')), may hold values from 0.099609375 to 1.8984375
- shift_first: bfloat16 [1024], P(('replica', 'group')), may hold values from -3 to 3
- w_inner: bfloat16 [1024, 4096], P(('replica', 'group')), may hold values from -0.1875 to 0.1875
- b_inner: bfloat16 [4096], P(('replica', 'group')), may hold values from -3 to 3
- w_outer: bfloat16 [4096, 1024], P(('replica', 'group')), may hold values from -0.1875 to 0.1875
- b_outer: bfloat16 [1024], P(('replica', 'group')), may hold values from -3 to 3
- gain_second: bfloat16 [1024], P(('replica', 'group')), may hold values from 0.099609375 to 1.8984375
- shift_second: bfloat16 [1024], P(('replica', 'group')), may hold values from -3 to 3
- cotangent: bfloat16 [32768, 1024], P(('replica', 'group')), may hold values from -6 to 6
Outputs:
- output: bfloat16 [32768, 1024], P(('replica', 'group'))
- grad_tokens: bfloat16 [32768, 1024], P(('replica', 'group'))
- grad_wquery: float32 [1024, 1024], P('group')
- grad_bquery: float32 [1024], P('group')
- grad_wkey: float32 [1024, 1024], P('group')
- grad_wvalue: float32 [1024, 1024], P('group')
- grad_bvalue: float32 [1024], P('group')
- grad_wout: float32 [1024, 1024], P('group')
- grad_bout: float32 [1024], P('group')
- grad_gainfirst: float32 [1024], P('group')
- grad_shiftfirst: float32 [1024], P('group')
- grad_winner: float32 [1024, 4096], P('group')
- grad_binner: float32 [4096], P('group')
- grad_wouter: float32 [4096, 1024], P('group')
- grad_bouter: float32 [1024], P('group')
- grad_gainsecond: float32 [1024], P('group')
- grad_shiftsecond: float32 [1024], P('group')
The draws below stay inside these ranges and needn't reach their ends.
Inputs may be any that keep to these rules, and one draw needn't show every extreme that they name: `segment_ids`: along each row of 512 positions the ids never fall; each of the 8 ids covers 1 to 256 consecutive positions, and some id exactly 256.
All inputs are finite; a program needn't handle non-finite values.
Results may differ from the reference program's by a relative error of at most 0.018.
Values may be sent and summed in bfloat16 or wider, within the bound.
No kernel may reach another device: no remote copies, remote signals or barrier semaphores. Data moves between devices by JAX's collectives and lax.ppermute only.
A program may use at most 256 MiB of HBM per device.

```python
import math
import jax
import jax.numpy as jnp
import numpy as np
from jax import lax

D = 1024
H = 16
HD = 64
FF = 4096
LEN = 512
SEGS = 8
SEQS = 64
TOKENS = 32768


def strengthened(entries, own_key, source, target, parts, factor):
    owner, partner = [(jnp.arange(entries.shape[axis_at]) // (entries.shape[axis_at] // parts)).reshape([-1 if axis == axis_at else 1 for axis in range(entries.ndim)]) for axis_at in (source, target)]
    chosen = jax.random.permutation(own_key, parts)[partner]
    strong = (owner == chosen) | (owner == (partner + parts // 2) % parts)
    return jnp.where(strong, factor * entries, entries)


def block_scale(rng, dims, split, smallest, high):
    loudness = 1.0
    for axis_at, blocks in split:
        draws = jax.random.uniform(jax.random.fold_in(jax.random.fold_in(rng, 6), axis_at), (blocks,), jnp.float32, smallest / len(split), high / len(split))
        loudness = loudness * jnp.repeat(jnp.exp(draws), dims[axis_at] // blocks).reshape((-1,) + (1,) * (len(dims) - 1 - axis_at))
    return loudness


def profile(amount, total, limit, slope):
    weights = [(1 << 20) // math.isqrt(rank ** slope) + 1 for rank in range(2, amount + 1)]
    spare, given = total - limit - (amount - 1), [1] * (amount - 1)
    while spare > 0:
        movable = [i for i in range(amount - 1) if given[i] < limit]
        whole, remaining = sum([weights[i] for i in movable]), spare
        for i in movable:
            extra = min(limit - given[i], max(1, remaining * weights[i] // whole), spare)
            given[i] = given[i] + extra
            spare = spare - extra
    return np.array([limit] + given)


def uneven_parts(own_key, count, total, most, skew):
    if count == 2:
        one = jax.random.randint(own_key, (), max(1, total - most), min(most, total - 1) + 1)
        return jnp.stack([one, total - one])
    sizes = jnp.asarray(profile(count, total, most, skew), jnp.int32)
    couples = (count - 1) // 2
    giver, receiver = sizes[1:1 + 2 * couples:2], sizes[2:2 + 2 * couples:2]
    slack = jnp.minimum(giver - 1, most - receiver)
    moved = jax.random.randint(jax.random.fold_in(own_key, 1), (couples,), 0, 1 << 20) % (slack + 1)
    sizes = sizes.at[1:1 + 2 * couples:2].set(giver - moved).at[2:2 + 2 * couples:2].set(receiver + moved)
    return sizes[jax.random.permutation(jax.random.fold_in(own_key, 2), count)]


def normal_values(key, dims, spread, reach, cuts=(), dtype=jnp.bfloat16):
    values = spread * jax.random.normal(key, dims, jnp.float32)
    if cuts:
        values = values * block_scale(key, dims, cuts, -0.22, 0.18)
    return jnp.clip(values, -reach, reach).astype(dtype)


def bell_draw_with(stream_key, dims, width, most, shards, heavy, dtype=jnp.bfloat16):
    array = width * jax.random.normal(stream_key, dims, jnp.float32)
    if shards:
        array = array * block_scale(stream_key, dims, shards, -0.22, 0.18)
    return jnp.clip(strengthened(array, jax.random.fold_in(stream_key, 3), *heavy), -most, most).astype(dtype)


def setup_inputs(seed: int = 0) -> dict:
    key_list = jax.random.split(jax.random.key(seed), 19)
    return {
        "tokens": normal_values(key_list[0], (TOKENS, D), 1.0, 6.0, ((0, 32),)),
        "segment_ids": jax.vmap(lambda own: jnp.searchsorted(jnp.cumsum(uneven_parts(own, SEGS, LEN, LEN // 2, 1)), jnp.arange(LEN), side="right"))(jax.random.split(key_list[1], SEQS)).reshape((SEQS, LEN)).astype(jnp.int32),
        "w_query": normal_values(key_list[2], (D, D), D ** -0.5, 0.1875, ((0, 32),)),
        "b_query": normal_values(key_list[3], (D,), 0.5, 3.0, ((0, 32),)),
        "w_key": normal_values(key_list[4], (D, D), D ** -0.5, 0.1875, ((0, 32),)),
        "w_value": normal_values(key_list[5], (D, D), D ** -0.5, 0.1875, ((0, 32),)),
        "b_value": normal_values(key_list[6], (D,), 0.5, 3.0, ((0, 32),)),
        "w_out": normal_values(key_list[7], (D, D), (D // 16) ** -0.5, 0.75, ((0, 32),)),
        "b_out": normal_values(key_list[8], (D,), 0.5, 3.0, ((0, 32),)),
        "gain_first": jnp.clip(1.0 + 0.18 * jax.random.normal(key_list[9], (D,), jnp.float32), 0.099609375, 1.8984375).astype(jnp.bfloat16),
        "shift_first": normal_values(key_list[10], (D,), 0.5, 3.0, ((0, 32),)),
        "w_inner": normal_values(key_list[11], (D, FF), D ** -0.5, 0.1875, ((0, 32),)),
        "b_inner": normal_values(key_list[12], (FF,), 0.5, 3.0, ((0, 32),)),
        "w_outer": normal_values(key_list[13], (FF, D), (FF // 4) ** -0.5, 0.1875, ((0, 32),)),
        "b_outer": normal_values(key_list[14], (D,), 0.5, 3.0, ((0, 32),)),
        "gain_second": jnp.clip(1.0 + 0.18 * jax.random.normal(key_list[15], (D,), jnp.float32), 0.099609375, 1.8984375).astype(jnp.bfloat16),
        "shift_second": normal_values(key_list[16], (D,), 0.5, 3.0, ((0, 32),)),
        "cotangent": bell_draw_with(key_list[17], (TOKENS, D), 1.0, 6.0, ((0, 32),), (0, 1, 32, 2.75)),
    }


@jax.custom_vjp
def low(v):
    return lax.optimization_barrier(v.astype(jnp.bfloat16)).astype(jnp.float32)

@jax.custom_vjp
def low_back(v):
    return v

def low_keep(v):
    return (low(v), None)

def low_pass(kept, grad):
    return (grad,)

def back_keep(v):
    return (v, None)

def back_low(kept, grad):
    return (low(grad),)
low.defvjp(low_keep, low_pass)
low_back.defvjp(back_keep, back_low)

def layer_norm(value, gain, shift):
    center = value - lax.optimization_barrier(jnp.mean(value, axis=-1, keepdims=True))
    scale = lax.rsqrt(lax.optimization_barrier(jnp.mean(center * center, axis=-1, keepdims=True)) + 1e-06)
    return center * scale * gain + shift

def gelu_exact(value):
    return 0.5 * value * (1.0 + lax.erf(value * (1.0 / math.sqrt(2.0))))

def matmul(left, right):
    return jnp.dot(left, right, precision=lax.Precision.HIGHEST, preferred_element_type=jnp.float32)

def forward(params, inputs, segments):
    w_query, b_query, w_key, w_value, b_value, w_out, b_out, gain_first, shift_first, w_inner, b_inner, w_outer, b_outer, gain_second, shift_second = params
    batch = inputs.shape[0]
    flat = inputs.reshape(-1, D)
    shape4 = (batch, LEN, H, HD)
    query = low(low_back(matmul(flat, w_query) + b_query)).reshape(shape4)
    keys = low(low_back(matmul(flat, w_key))).reshape(shape4)
    values = low(low_back(matmul(flat, w_value) + b_value)).reshape(shape4)
    scores = low_back(jnp.einsum('bqhd,bkhd->bhqk', query, keys, precision=lax.Precision.HIGHEST) * 0.125)
    same = segments[:, None, :, None] == segments[:, None, None, :]
    masked = jnp.where(same, scores, -1000000000.0)
    top = lax.optimization_barrier(jnp.max(masked, axis=-1, keepdims=True))
    expo = jnp.exp(masked - top)
    probs = expo / lax.optimization_barrier(jnp.sum(expo, axis=-1, keepdims=True))
    mixed = jnp.einsum('bhqk,bkhd->bqhd', low(probs), values, precision=lax.Precision.HIGHEST).reshape(-1, D)
    attended = low_back(matmul(low(low_back(mixed)), w_out) + b_out)
    hidden = layer_norm(flat + attended, gain_first, shift_first)
    inner = low_back(matmul(low(hidden), w_inner) + b_inner)
    outer = low_back(matmul(low(gelu_exact(inner)), w_outer) + b_outer)
    return layer_norm(hidden + outer, gain_second, shift_second).reshape(inputs.shape)

def reference(tokens, segment_ids, w_query, b_query, w_key, w_value, b_value, w_out, b_out, gain_first, shift_first, w_inner, b_inner, w_outer, b_outer, gain_second, shift_second, cotangent):
    params = tuple((item.astype(jnp.float32) for item in (w_query, b_query, w_key, w_value, b_value, w_out, b_out, gain_first, shift_first, w_inner, b_inner, w_outer, b_outer, gain_second, shift_second)))
    bundle = math.gcd(SEQS, 8)
    blocks = SEQS // bundle
    inputs = tokens.astype(jnp.float32).reshape(blocks, bundle, LEN, D)
    backs = cotangent.astype(jnp.float32).reshape(blocks, bundle, LEN, D)
    segments = segment_ids.reshape(blocks, bundle, LEN)
    zeros = tuple((jnp.zeros_like(item) for item in params))

    def advance(totals, block):
        data, ids, back = block

        def wrapped(weights, values):
            return forward(weights, values, ids)
        result, pullback = jax.vjp(wrapped, params, data)
        grad_params, grad_data = pullback(back)
        totals = tuple((total + grad for total, grad in zip(totals, grad_params)))
        return (totals, (result.astype(jnp.bfloat16), grad_data.astype(jnp.bfloat16)))
    totals, (results, grads) = lax.scan(advance, zeros, (inputs, segments, backs))
    return (results.reshape(TOKENS, D), grads.reshape(TOKENS, D), totals[0], totals[1], totals[2], totals[3], totals[4], totals[5], totals[6], totals[7], totals[8], totals[9], totals[10], totals[11], totals[12], totals[13], totals[14])
```

```python
import functools
import math

import jax
import jax.numpy as jnp
from jax import lax
from jax.experimental import pallas as pl
from jax.experimental.pallas import tpu as pltpu
from jax.sharding import PartitionSpec as P

F32 = jnp.float32
BF16 = jnp.bfloat16
VMEM_LIMIT = 56 * 1024 * 1024


def params(*semantics):
    return pltpu.CompilerParams(dimension_semantics=semantics, vmem_limit_bytes=VMEM_LIMIT)


def cost(flops, bytes_accessed, transcendentals=0):
    return pl.CostEstimate(flops=int(flops), bytes_accessed=int(bytes_accessed), transcendentals=int(transcendentals))


def dot(left, right):
    return lax.dot_general(left, right, (((1,), (0,)), ((), ())), preferred_element_type=F32)


def dot_nt(left, right):
    return lax.dot_general(left, right, (((1,), (1,)), ((), ())), preferred_element_type=F32)


def whole(shape):
    return pl.BlockSpec(shape, lambda *i: (0,) * len(shape))


def transpose_kernel(x_ref, out_ref):
    out_ref[...] = x_ref[...].T


def transposed(x, tile=256):
    rows, cols = x.shape
    return pl.pallas_call(
        transpose_kernel,
        out_shape=jax.ShapeDtypeStruct((cols, rows), x.dtype),
        grid=(rows // tile,),
        in_specs=[pl.BlockSpec((tile, cols), lambda i: (i, 0))],
        out_specs=pl.BlockSpec((cols, tile), lambda i: (0, i)),
        compiler_params=params("arbitrary"),
        cost_estimate=cost(0, 4 * rows * cols),
        name="transposed",
    )(x)


def project_kernel(order_ref, x_ref, w_ref, b_ref, out_ref, whole_ref, held, arrived, left, *, tile):
    step = pl.program_id(0)
    pieces, rows, _ = w_ref.shape
    cols = held.shape[1]
    write = pltpu.make_async_copy(held, whole_ref, left)

    @pl.when(step == 0)
    def _():
        def fetch(j):
            start = pl.multiple_of(order_ref[j] * rows, rows)
            return pltpu.make_async_copy(w_ref.at[j, :, pl.ds(0, cols)], held.at[pl.ds(start, rows)], arrived.at[j])

        for j in range(pieces):
            fetch(j).start()
        for j in range(pieces):
            fetch(j).wait()
        write.start()

    part = held[:, pl.ds(pl.multiple_of(step * tile, tile), tile)]
    out_ref[...] = (dot(x_ref[...], part) + b_ref[...]).astype(BF16)

    @pl.when(step == pl.num_programs(0) - 1)
    def _():
        write.wait()


def project(order, x, w, bias, tile=512):
    rows, depth = x.shape
    cols = bias.shape[1]
    return pl.pallas_call(
        functools.partial(project_kernel, tile=tile),
        out_shape=(jax.ShapeDtypeStruct((rows, cols), BF16), jax.ShapeDtypeStruct((depth, cols), BF16)),
        grid_spec=pltpu.PrefetchScalarGridSpec(
            num_scalar_prefetch=1,
            grid=(cols // tile,),
            in_specs=[
                pl.BlockSpec((rows, depth), lambda i, order: (0, 0)),
                pl.BlockSpec(memory_space=pl.ANY),
                pl.BlockSpec((1, tile), lambda i, order: (0, i)),
            ],
            out_specs=(pl.BlockSpec((rows, tile), lambda i, order: (0, i)), pl.BlockSpec(memory_space=pl.ANY)),
            scratch_shapes=[pltpu.VMEM((depth, cols), BF16), pltpu.SemaphoreType.DMA((w.shape[0],)), pltpu.SemaphoreType.DMA],
        ),
        compiler_params=params("arbitrary"),
        cost_estimate=cost(2 * rows * depth * cols, 2 * (rows * depth + depth * cols + rows * cols)),
        name="project",
    )(order, x, w, bias)


def attend_kernel(q_ref, k_ref, v_ref, row_ref, col_ref, o_ref, ot_ref, p_ref, bias_ref):
    @pl.when(pl.program_id(1) == 0)
    def _():
        bias_ref[...] = jnp.where(col_ref[0] == row_ref[0], 0.0, -1e9).astype(F32)

    qt = q_ref[...].T
    keys = k_ref[...]
    vt = v_ref[...].T
    half = qt.shape[0] // 2
    zero = jnp.zeros((half, qt.shape[1]), BF16)
    for head in range(2):
        own = qt[head * half : (head + 1) * half]
        qh = jnp.concatenate([own, zero] if head == 0 else [zero, own], axis=0)
        scores = dot(keys, qh) * 0.125 + bias_ref[...]
        top = jnp.max(scores, axis=0, keepdims=True)
        expo = jnp.exp(scores - top)
        total = jnp.sum(expo, axis=0, keepdims=True)
        probs = (expo * (1.0 / total)).astype(BF16)
        p_ref[0, head] = probs
        ot_ref[pl.ds(head * half, half), :] = dot(vt[head * half : (head + 1) * half], probs).astype(BF16)
    o_ref[...] = ot_ref[...].T


def attend(qkv, segment, pair=128):
    seqs, length = segment.shape
    width = qkv.shape[1] // 3
    pairs = width // pair
    row = segment.reshape(seqs, 1, length)
    col = segment.reshape(seqs, length, 1)
    spec = lambda part: pl.BlockSpec((length, pair), lambda s, p: (s, part * pairs + p))
    return pl.pallas_call(
        attend_kernel,
        out_shape=(
            jax.ShapeDtypeStruct((seqs * length, width), BF16),
            jax.ShapeDtypeStruct((width, seqs * length), BF16),
            jax.ShapeDtypeStruct((seqs, 2 * pairs, length, length), BF16),
        ),
        grid=(seqs, pairs),
        in_specs=[
            spec(0),
            spec(1),
            spec(2),
            pl.BlockSpec((1, 1, length), lambda s, p: (s, 0, 0)),
            pl.BlockSpec((1, length, 1), lambda s, p: (s, 0, 0)),
        ],
        out_specs=(
            pl.BlockSpec((length, pair), lambda s, p: (s, p)),
            pl.BlockSpec((pair, length), lambda s, p: (p, s)),
            pl.BlockSpec((1, 2, length, length), lambda s, p: (s, p, 0, 0)),
        ),
        scratch_shapes=[pltpu.VMEM((length, length), F32)],
        compiler_params=params("arbitrary", "arbitrary"),
        cost_estimate=cost(8 * seqs * length * length * width, 20e6, seqs * length * length * 16),
        name="attend",
    )(qkv, qkv, qkv, row, col)


def attend_back_kernel(q_ref, k_ref, v_ref, ot_ref, p_ref, do_ref, d_ref, bq_ref, bv_ref):
    pair = q_ref.shape[1]
    half = pair // 2
    length = q_ref.shape[0]
    do = do_ref[...]
    dot_t = do.T
    q = q_ref[...]
    kt = k_ref[...].T
    v = v_ref[...]
    product = dot_t.astype(F32) * ot_ref[...].astype(F32)
    zero = jnp.zeros((half, length), BF16)
    first = lax.broadcasted_iota(jnp.int32, (1, pair), 1) < half
    dk, dv, dqt = [], [], []
    for head in range(2):
        here = slice(head * half, (head + 1) * half)
        delta = jnp.sum(product[here], axis=0, keepdims=True)
        own = dot_t[here]
        dh = jnp.concatenate([own, zero] if head == 0 else [zero, own], axis=0)
        probs = p_ref[0, head]
        ds = (probs.astype(F32) * (dot(v, dh) - delta)).astype(BF16)
        dv.append(dot(probs, do))
        dk.append(dot(ds, q))
        dqt.append(dot(kt[here], ds))
    dv = jnp.where(first, dv[0], dv[1]).astype(BF16)
    dk = (jnp.where(first, dk[0], dk[1]) * 0.125).astype(BF16)
    dq = (jnp.concatenate(dqt, axis=0) * 0.125).astype(BF16).T
    d_ref[0] = dq
    d_ref[1] = dk
    d_ref[2] = dv
    sum_q = jnp.sum(dq.astype(F32), axis=0, keepdims=True)
    sum_v = jnp.sum(dv.astype(F32), axis=0, keepdims=True)
    bq_ref[0] = sum_q
    bv_ref[0] = sum_v


def attend_back(qkv, ot, probs, do, seqs, part, pair=128):
    tokens, width = do.shape[0], qkv.shape[1] // 3
    length = tokens // seqs
    pairs = width // pair
    spec = lambda part: pl.BlockSpec((length, pair), lambda s, p: (s, part * pairs + p))
    sums = pl.BlockSpec((1, 1, pair), lambda s, p: (s, 0, p))
    return pl.pallas_call(
        attend_back_kernel,
        out_shape=(jax.ShapeDtypeStruct((3, tokens, width), BF16),)
        + (jax.ShapeDtypeStruct((seqs, 1, width), F32),) * 2,
        grid=(seqs, pairs),
        in_specs=[
            spec(0),
            spec(1),
            spec(2),
            pl.BlockSpec((pair, length), lambda s, p: (p, s)),
            pl.BlockSpec((1, 2, length, length), lambda s, p: (s, p, 0, 0)),
            pl.BlockSpec((length, pair), lambda s, p: (s, part * pairs + p)),
        ],
        out_specs=(pl.BlockSpec((3, length, pair), lambda s, p: (0, s, p)), sums, sums),
        compiler_params=params("arbitrary", "arbitrary"),
        cost_estimate=cost(16 * seqs * length * length * width, 30e6),
        name="attend_back",
    )(qkv, qkv, qkv, ot, probs, do)


def normed(z):
    center = z - jnp.mean(z, axis=-1, keepdims=True)
    rstd = lax.rsqrt(jnp.mean(center * center, axis=-1, keepdims=True) + 1e-06)
    return center * rstd, rstd


def norm_back(dn, n, rstd):
    return rstd * (dn - jnp.mean(dn, axis=-1, keepdims=True) - n * jnp.mean(dn * n, axis=-1, keepdims=True))


def join_kernel(o0_ref, o1_ref, w_ref, x_ref, b_ref, g_ref, s_ref, n_ref, r_ref, h_ref, ht_ref):
    half = o0_ref.shape[1]
    mixed = dot(o0_ref[...], w_ref[:half]) + dot(o1_ref[...], w_ref[half:])
    z = x_ref[...].astype(F32) + (mixed + b_ref[...])
    n, rstd = normed(z)
    n_ref[...] = n
    r_ref[...] = rstd
    h = (n * g_ref[...] + s_ref[...]).astype(BF16)
    h_ref[...] = h
    ht_ref[...] = h.T


def join(o0, o1, w, x, bias, gain, shift, tile=256):
    rows, width = x.shape
    tok = pl.BlockSpec((tile, width), lambda i: (i, 0))
    half = pl.BlockSpec((tile, width // 2), lambda i: (i, 0))
    vec = whole((1, width))
    return pl.pallas_call(
        join_kernel,
        out_shape=(
            jax.ShapeDtypeStruct((rows, width), F32),
            jax.ShapeDtypeStruct((rows, 1), F32),
            jax.ShapeDtypeStruct((rows, width), BF16),
            jax.ShapeDtypeStruct((width, rows), BF16),
        ),
        grid=(rows // tile,),
        in_specs=[half, half, whole((width, width)), tok, vec, vec, vec],
        out_specs=(tok, pl.BlockSpec((tile, 1), lambda i: (i, 0)), tok, pl.BlockSpec((width, tile), lambda i: (0, i))),
        compiler_params=params("arbitrary"),
        cost_estimate=cost(2 * rows * width * width, 16 * rows * width),
        name="join",
    )(o0, o1, w, x, bias, gain, shift)


def gelu_pair(f):
    size = jnp.abs(f)
    t = 1.0 / (1.0 + (0.3275911 / math.sqrt(2.0)) * size)
    bell = jnp.exp(-0.5 * (f * f))
    poly = t * (0.127414796 + t * (-0.142248368 + t * (0.7107068705 + t * (-0.7265760135 + t * 0.5307027145))))
    tail = poly * bell
    weight = jnp.where(f < 0, tail, 1.0 - tail)
    return f * weight, weight + f * (bell * (1.0 / math.sqrt(2.0 * math.pi)))


def inner_kernel(h_ref, w_ref, b_ref, u_ref, g_ref):
    f = dot(h_ref[...], w_ref[...]) + b_ref[...]
    u, slope = gelu_pair(f)
    u_ref[...] = u.astype(BF16)
    g_ref[...] = slope.astype(BF16)


def inner(h, w, bias, tile=512):
    rows, depth = h.shape
    cols = w.shape[1]
    out = pl.BlockSpec((rows, tile), lambda i: (0, i))
    return pl.pallas_call(
        inner_kernel,
        out_shape=(jax.ShapeDtypeStruct((rows, cols), BF16),) * 2,
        grid=(cols // tile,),
        in_specs=[whole((rows, depth)), pl.BlockSpec((depth, tile), lambda i: (0, i)), pl.BlockSpec((1, tile), lambda i: (0, i))],
        out_specs=(out, out),
        compiler_params=params("arbitrary"),
        cost_estimate=cost(2 * rows * depth * cols, 2 * (depth * cols + 2 * rows * cols), 2 * rows * cols),
        name="inner",
    )(h, w, bias)


def outer_kernel(u_ref, w_ref, n_ref, c_ref, b_ref, g1_ref, s1_ref, g2_ref, s2_ref, out_ref, dz_ref, dm_ref, dmt_ref, sums_ref):
    @pl.when(pl.program_id(0) == 0)
    def _():
        sums_ref[...] = jnp.zeros_like(sums_ref)

    z = (n_ref[...] * g1_ref[...] + s1_ref[...]) + (dot(u_ref[...], w_ref[...]) + b_ref[...])
    n, rstd = normed(z)
    out_ref[...] = (n * g2_ref[...] + s2_ref[...]).astype(BF16)
    c = c_ref[...].astype(F32)
    dz = norm_back(c * g2_ref[...], n, rstd)
    dz_ref[...] = dz
    dm = dz.astype(BF16)
    dm_ref[...] = dm
    dmt_ref[...] = dm.T
    sums_ref[0:1, :] += jnp.sum(c * n, axis=0, keepdims=True)
    sums_ref[1:2, :] += jnp.sum(c, axis=0, keepdims=True)
    sums_ref[2:3, :] += jnp.sum(dm.astype(F32), axis=0, keepdims=True)


def outer(u, w, n1, cot, bias, gain1, shift1, gain2, shift2, tile=256):
    rows, depth = u.shape
    width = w.shape[1]
    tok = pl.BlockSpec((tile, width), lambda i: (i, 0))
    vec = whole((1, width))
    return pl.pallas_call(
        outer_kernel,
        out_shape=(
            jax.ShapeDtypeStruct((rows, width), BF16),
            jax.ShapeDtypeStruct((rows, width), F32),
            jax.ShapeDtypeStruct((rows, width), BF16),
            jax.ShapeDtypeStruct((width, rows), BF16),
            jax.ShapeDtypeStruct((8, width), F32),
        ),
        grid=(rows // tile,),
        in_specs=[pl.BlockSpec((tile, depth), lambda i: (i, 0)), whole((depth, width)), tok, tok, vec, vec, vec, vec, vec],
        out_specs=(tok, tok, tok, pl.BlockSpec((width, tile), lambda i: (0, i)), whole((8, width))),
        compiler_params=params("arbitrary"),
        cost_estimate=cost(2 * rows * depth * width, 2 * (rows * depth + depth * width) + 20 * rows * width),
        name="outer",
    )(u, w, n1, cot, bias, gain1, shift1, gain2, shift2)


def outer_grad_kernel(half_ref, left_ref, right_ref, out_ref):
    made = dot(left_ref[...], right_ref[...]).astype(BF16)
    halves, blocks, rows, part = out_ref.shape
    for i in range(blocks):
        out_ref[:, i] = made[:, i * part : (i + 1) * part].reshape(halves, rows, part)


def outer_grad(half, dmt, u, groups):
    width, rows = dmt.shape
    cols = u.shape[1]
    part = cols // groups
    blocks = max(1, 512 // part)
    return pl.pallas_call(
        outer_grad_kernel,
        out_shape=jax.ShapeDtypeStruct((2, groups, width // 4, part), BF16),
        grid_spec=pltpu.PrefetchScalarGridSpec(
            num_scalar_prefetch=1,
            grid=(groups // blocks,),
            in_specs=[
                pl.BlockSpec((width // 2, rows), lambda i, half: (half[0], 0)),
                pl.BlockSpec((rows, blocks * part), lambda i, half: (0, i)),
            ],
            out_specs=pl.BlockSpec((2, blocks, width // 4, part), lambda i, half: (0, i, 0, 0)),
        ),
        compiler_params=params("arbitrary"),
        cost_estimate=cost(rows * width * cols, 2 * rows * (width + cols) + width * cols),
        name="outer_grad",
    )(half, dmt, u)


def inner_back_kernel(half_ref, dm_ref, w2_ref, g_ref, ht_ref, w1_ref, dh0_ref, dw_ref, dh_ref, sum_ref):
    @pl.when(pl.program_id(0) == 0)
    def _():
        dh_ref[...] = dh0_ref[...]

    df = (dot_nt(dm_ref[...], w2_ref[...]) * g_ref[...].astype(F32)).astype(BF16)
    sum_ref[...] = jnp.sum(df.astype(F32), axis=0, keepdims=True)
    dw_ref[...] = dot(ht_ref[...], df).astype(BF16).reshape(dw_ref.shape)
    dh_ref[...] += dot_nt(df, w1_ref[...])


def inner_back(half, dm, w2, slope, ht, w1, dh, groups, tile=512):
    rows, width = dm.shape
    cols = slope.shape[1]
    steps = cols // 2 // tile
    per = steps // 2
    at = lambda i, half: half[0] * steps + i
    return pl.pallas_call(
        inner_back_kernel,
        out_shape=(
            jax.ShapeDtypeStruct((2, groups, width // groups, cols // 4), BF16),
            jax.ShapeDtypeStruct((rows, width), F32),
            jax.ShapeDtypeStruct((1, cols // 2), F32),
        ),
        grid_spec=pltpu.PrefetchScalarGridSpec(
            num_scalar_prefetch=1,
            grid=(steps,),
            in_specs=[
                pl.BlockSpec((rows, width), lambda i, half: (0, 0)),
                pl.BlockSpec((tile, width), lambda i, half: (at(i, half), 0)),
                pl.BlockSpec((rows, tile), lambda i, half: (0, at(i, half))),
                pl.BlockSpec((width, rows), lambda i, half: (0, 0)),
                pl.BlockSpec((width, tile), lambda i, half: (0, at(i, half))),
                pl.BlockSpec((rows, width), lambda i, half: (0, 0)),
            ],
            out_specs=(
                pl.BlockSpec((1, groups, width // groups, tile), lambda i, half: (i // per, 0, 0, i % per)),
                pl.BlockSpec((rows, width), lambda i, half: (0, 0)),
                pl.BlockSpec((1, tile), lambda i, half: (0, i)),
            ),
        ),
        compiler_params=params("arbitrary"),
        cost_estimate=cost(3 * rows * width * cols, 3 * width * cols + rows * cols + 12 * rows * width),
        name="inner_back",
    )(half, dm, w2, slope, ht, w1, dh)


def mix_grad_kernel(half_ref, left0_ref, left1_ref, right_ref, out_ref):
    for i, left_ref in enumerate((left0_ref, left1_ref)):
        made = dot(left_ref[...], right_ref[...]).astype(BF16)
        groups = out_ref.shape[1] // 2
        shape = (groups,) + out_ref.shape[2:]
        for x in range(2):
            cols = out_ref.shape[3]
            out_ref[x, i * groups : (i + 1) * groups] = made[:, x * cols : (x + 1) * cols].reshape(shape)


def mix_grad(half, ot0, ot1, da, groups):
    rows, width = da.shape
    left = pl.BlockSpec((width // 2, rows), lambda i, half: (0, 0))
    return pl.pallas_call(
        mix_grad_kernel,
        out_shape=jax.ShapeDtypeStruct((2, groups, width // groups, width // 4), BF16),
        grid_spec=pltpu.PrefetchScalarGridSpec(
            num_scalar_prefetch=1,
            grid=(1,),
            in_specs=[left, left, pl.BlockSpec((rows, width // 2), lambda i, half: (0, half[0]))],
            out_specs=pl.BlockSpec((2, groups, width // groups, width // 4), lambda i, half: (0, 0, 0, 0)),
        ),
        compiler_params=params("arbitrary"),
        cost_estimate=cost(rows * width * width, 5 * width * width),
        name="mix_grad",
    )(half, ot0, ot1, da)


def token_weights_grad_kernel(half_ref, left_ref, right_ref, *refs):
    out_ref = refs[-1]
    rows = left_ref.shape[0] // out_ref.shape[1]
    cols = right_ref.shape[2] // 2
    shape = (out_ref.shape[1], rows, cols)
    for which in range(3):
        made = dot(left_ref[...], right_ref[which]).astype(BF16)
        for x in range(2):
            out_ref[x, :, :rows, which * cols : (which + 1) * cols] = made[:, x * cols : (x + 1) * cols].reshape(shape)
    for extra_ref in refs[:-1]:
        for x in range(2):
            out_ref[x, :, rows:, :] = extra_ref[...]


def token_weights_grad(half, xt, d, groups, *extra):
    width, rows = xt.shape
    part = d.shape[2] // 2
    cols = 3 * part // 2
    more = sum(e.shape[1] for e in extra)
    return pl.pallas_call(
        token_weights_grad_kernel,
        out_shape=jax.ShapeDtypeStruct((2, groups, width // groups + more, cols), BF16),
        grid_spec=pltpu.PrefetchScalarGridSpec(
            num_scalar_prefetch=1,
            grid=(1,),
            in_specs=[
                pl.BlockSpec((width, rows), lambda i, half: (0, 0)),
                pl.BlockSpec((3, rows, part), lambda i, half: (0, 0, half[0])),
            ]
            + [pl.BlockSpec(e.shape, lambda i, half: (0, 0, 0)) for e in extra],
            out_specs=pl.BlockSpec((2, groups, width // groups + more, cols), lambda i, half: (0, 0, 0, 0)),
        ),
        compiler_params=params("arbitrary"),
        cost_estimate=cost(6 * rows * width * part, 2 * width * rows + 12 * rows * part),
        name="token_weights_grad",
    )(half, xt, d, *extra)


def join_back_kernel(dz2_ref, dh_ref, n_ref, r_ref, g_ref, w_ref, dz_ref, da_ref, do_ref, sums_ref):
    @pl.when(pl.program_id(0) == 0)
    def _():
        sums_ref[...] = jnp.zeros_like(sums_ref)

    dh = dz2_ref[...] + dh_ref[...]
    n = n_ref[...]
    dz = norm_back(dh * g_ref[...], n, r_ref[...])
    dz_ref[...] = dz
    da = dz.astype(BF16)
    da_ref[...] = da
    do_ref[...] = dot_nt(da, w_ref[...]).astype(BF16)
    sums_ref[0:1, :] += jnp.sum(dh * n, axis=0, keepdims=True)
    sums_ref[1:2, :] += jnp.sum(dh, axis=0, keepdims=True)
    sums_ref[2:3, :] += jnp.sum(da.astype(F32), axis=0, keepdims=True)


def join_back(dz2, dh, n1, rstd, gain, w, tile=256):
    rows, width = dz2.shape
    tok = pl.BlockSpec((tile, width), lambda i: (i, 0))
    return pl.pallas_call(
        join_back_kernel,
        out_shape=(
            jax.ShapeDtypeStruct((rows, width), F32),
            jax.ShapeDtypeStruct((rows, width), BF16),
            jax.ShapeDtypeStruct((rows, width), BF16),
            jax.ShapeDtypeStruct((8, width), F32),
        ),
        grid=(rows // tile,),
        in_specs=[tok, tok, tok, pl.BlockSpec((tile, 1), lambda i: (i, 0)), whole((1, width)), whole((width, width))],
        out_specs=(tok, tok, tok, whole((8, width))),
        compiler_params=params("arbitrary"),
        cost_estimate=cost(2 * rows * width * width, 22 * rows * width),
        name="join_back",
    )(dz2, dh, n1, rstd, gain, w)


def token_grad_kernel(dz_ref, d0_ref, d1_ref, w0_ref, w1_ref, out_ref):
    width = d0_ref.shape[2]
    total = dz_ref[...]
    for d_ref, w_ref in ((d0_ref, w0_ref), (d1_ref, w1_ref)):
        for i in range(3):
            total = total + dot_nt(d_ref[i], w_ref[:, i * width : (i + 1) * width])
    out_ref[...] = total.astype(BF16)


def token_grad(dz, d0, d1, w0, w1, tile=256):
    rows, width = dz.shape
    tok = pl.BlockSpec((tile, width), lambda i: (i, 0))
    part = pl.BlockSpec((3, tile, width // 2), lambda i: (0, i, 0))
    weight = whole((width, 3 * width // 2))
    return pl.pallas_call(
        token_grad_kernel,
        out_shape=jax.ShapeDtypeStruct((rows, width), BF16),
        grid=(rows // tile,),
        in_specs=[tok, part, part, weight, weight],
        out_specs=tok,
        compiler_params=params("arbitrary"),
        cost_estimate=cost(6 * rows * width * width, 18 * rows * width),
        name="token_grad",
    )(dz, d0, d1, w0, w1)


def digits_of(axis, total, base):
    digits, stride = [], total
    while stride > 1:
        size = base if stride % base == 0 else 2
        stride //= size
        digits.append((axis, stride, size))
    return digits


class Layout:
    def __init__(self, mesh):
        self.replicas, self.groups = mesh.shape["replica"], mesh.shape["group"]
        self.group = digits_of("group", self.groups, 4)
        replica = digits_of("replica", self.replicas, 2)
        self.core, self.over = replica[-1], replica[:-1]
        self.sizes = {"replica": self.replicas, "group": self.groups}
        self.devices = self.replicas * self.groups

    def place(self, digit):
        axis, stride, size = digit
        return (lax.axis_index(axis) // stride) % size

    def send(self, value, digit, shift):
        axis, stride, size = digit
        pairs = []
        for i in range(self.sizes[axis]):
            own = (i // stride) % size
            pairs.append((i, i + ((own + shift) % size - own) * stride))
        return lax.ppermute(value, axis, pairs)

    def gather(self, value, order):
        value = value[None]
        for digit in order:
            value = jnp.concatenate([value] + [self.send(value, digit, k) for k in range(1, digit[2])], axis=0)
        return value

    def places(self, order):
        total = jnp.zeros((1,), jnp.int32)
        for axis, stride, size in order:
            own = self.place((axis, stride, size))
            weight = stride * (self.groups if axis == "replica" else 1)
            source = (own - jnp.arange(size, dtype=jnp.int32) + size) % size
            total = (source[:, None] * weight + total[None, :]).reshape(-1)
        return total

    def scatter(self, terms, order):
        dims = self.over + self.group
        for digit in order:
            axis = dims.index(digit)
            dims = dims[:axis] + dims[axis + 1 :]
            size, own = digit[2], self.place(digit)
            pick = lambda at: [lax.dynamic_index_in_dim(t, at, axis, keepdims=False) for t in terms]
            came = [self.send(total_of(pick((own + k) % size)), digit, k) for k in range(1, size)]
            terms = pick(own) + came
        return total_of(terms)

    def spread(self, block):
        for digit in self.over[::-1] + [self.core]:
            came = self.send(block, digit, 1)
            own = self.place(digit)
            block = jnp.where(own == 0, jnp.stack([block, came]), jnp.stack([came, block]))
        return block


def total_of(terms):
    total = terms[0].astype(F32)
    for term in terms[1:]:
        total = total + term.astype(F32)
    return total.astype(BF16)


def local(layout, tokens, segment_ids, w_query, b_query, w_key, w_value, b_value, w_out, b_out, gain_first, shift_first, w_inner, b_inner, w_outer, b_outer, gain_second, shift_second, cotangent):
    groups, devices = layout.groups, layout.devices
    seqs = segment_ids.shape[0]
    width = tokens.shape[1]
    rows = w_query.shape[0]
    each = b_query.shape[0]
    lanes = 128
    half_width = width // 2
    core = layout.place(layout.core).astype(jnp.int32)
    mine, theirs = core.reshape(1), (1 - core).reshape(1)

    both = ("replica", "group")
    whole_wouter = lax.all_gather(w_outer, both, axis=0, tiled=True)
    whole_rest = lax.all_gather(jnp.concatenate([w_inner, w_out], axis=1), both, axis=0, tiled=True)
    whole_winner, whole_wout = whole_rest[:, : w_inner.shape[1]], whole_rest[:, w_inner.shape[1] :]
    vectors = (b_query, b_value, b_out, gain_first, shift_first, b_outer, gain_second, shift_second)
    small = jnp.concatenate(vectors + (b_inner,))
    small = jnp.pad(small, (0, rows * lanes - small.shape[0])).reshape(rows, lanes)
    parts = [jnp.concatenate([w[:, i * half_width : (i + 1) * half_width] for w in (w_query, w_key, w_value)], axis=1) for i in range(2)]
    z_first = layout.group[:1] + layout.over + layout.group[1:] + [layout.core]
    z_last = layout.group[:1] + layout.group[1:] + layout.over + [layout.core]
    came0 = layout.gather(jnp.concatenate([parts[0], small], axis=1), z_first)
    came1 = layout.gather(parts[1], z_last)
    place0, place1 = layout.places(z_first), layout.places(z_last)
    count = sum(v.shape[0] for v in vectors) + b_inner.shape[0]
    chosen = (place0[None, :] == jnp.arange(devices, dtype=jnp.int32)[:, None]).astype(BF16)
    small = dot(chosen, came0[:, :, 3 * half_width :].reshape(devices, -1)[:, :count])
    vec = small[:, : 8 * each].reshape(devices, 8, each).transpose(1, 0, 2).reshape(8, 1, width)
    whole_binner = small[:, 8 * each :].reshape(1, -1)
    bias = [jnp.concatenate([vec[0, :, at], jnp.zeros((1, half_width), F32), vec[1, :, at]], axis=1) for at in (slice(0, half_width), slice(half_width, None))]
    if rows % 16:
        came0, came1 = came0[jnp.argsort(place0)].reshape(1, width, -1), came1[jnp.argsort(place1)].reshape(1, width, -1)
        place0 = place1 = jnp.zeros((1,), jnp.int32)

    xt = transposed(tokens)
    qkv0, wqkv0 = project(place0, tokens, came0, bias[0])
    o0, ot0, probs0 = attend(qkv0, segment_ids)
    qkv1, wqkv1 = project(place1, tokens, came1, bias[1])
    o1, ot1, probs1 = attend(qkv1, segment_ids)
    n1, rstd1, h, ht = join(o0, o1, whole_wout, tokens, vec[2], vec[3], vec[4])
    u, slope = inner(h, whole_winner, whole_binner)
    out, dz2, dm, dmt, sums2 = outer(u, whole_wouter, n1, cotangent, vec[5], vec[3], vec[4], vec[6], vec[7])

    digits = tuple(d[2] for d in layout.group)
    unfold = lambda a: a.reshape((2,) * len(layout.over) + digits + a.shape[2:])

    def reduced(own, other, order):
        came = layout.send(other, layout.core, 1)
        return layout.spread(layout.scatter([unfold(own), unfold(came)], order))

    x_first = layout.over + layout.group[1:] + layout.group[:1]
    y_first = layout.group[1:] + layout.over + layout.group[:1]
    other = outer_grad(theirs, dmt, u, groups)
    own = outer_grad(mine, dmt, u, groups)
    got_wouter = reduced(own, other, x_first)
    other, dh, sum_other = inner_back(theirs, dm, whole_wouter, slope, ht, whole_winner, jnp.zeros_like(dz2), groups)
    own, dh, sum_own = inner_back(mine, dm, whole_wouter, slope, ht, whole_winner, dh, groups)
    got_winner = reduced(own, other, y_first)
    sum_inner = jnp.where(core == 0, jnp.concatenate([sum_own, sum_other], axis=1), jnp.concatenate([sum_other, sum_own], axis=1))
    dz1, da, do, sums1 = join_back(dz2, dh, n1, rstd1, vec[3], whole_wout)
    other = mix_grad(theirs, ot0, ot1, da, groups)
    own = mix_grad(mine, ot0, ot1, da, groups)
    got_wout = reduced(own, other, x_first)
    d0, sq0, sv0 = attend_back(qkv0, ot0, probs0, do, seqs, 0)
    other = token_weights_grad(theirs, xt, d0, groups)
    own = token_weights_grad(mine, xt, d0, groups)
    got_first = reduced(own, other, x_first)
    d1, sq1, sv1 = attend_back(qkv1, ot1, probs1, do, seqs, 1)
    bq = jnp.concatenate([jnp.sum(s, axis=0) for s in (sq0, sq1)], axis=1)
    bv = jnp.concatenate([jnp.sum(s, axis=0) for s in (sv0, sv1)], axis=1)
    sums = jnp.concatenate([bq, bv, sums1[2:3], sums1[0:1], sums1[1:2], sums2[2:3], sums2[0:1], sums2[1:2]], axis=0)
    sums = sums.reshape(8, groups, -1).transpose(1, 0, 2).reshape(groups, -1)
    sums = jnp.concatenate([sums, sum_inner.reshape(groups, -1)], axis=1)
    used = sums.shape[1]
    cols = 3 * width // 8
    extra = jnp.pad(sums.astype(BF16), ((0, 0), (0, 16 * cols - used))).reshape(groups, 16, cols)
    other = token_weights_grad(theirs, xt, d1, groups, extra)
    own = token_weights_grad(mine, xt, d1, groups, extra)
    got_second = reduced(own, other, y_first)
    grad_tokens = token_grad(dz1, d0, d1, wqkv0, wqkv1)

    joined = lambda got: jnp.moveaxis(got, -2, 0).reshape(got.shape[-2], -1).astype(F32)
    grad_wouter = got_wouter.reshape(width, -1).T.astype(F32)
    grad_winner, grad_wout = joined(got_winner), joined(got_wout)
    keep = width // groups
    quarter = half_width // 4
    both_parts = [got_first, got_second[..., :keep, :]]
    wqkv = [jnp.concatenate([joined(g[..., i * quarter : (i + 1) * quarter]) for g in both_parts], axis=1) for i in range(3)]
    sums = got_second[(0,) * (got_second.ndim - 2)][keep:].reshape(-1)[:used].astype(F32)
    bq, bv, bout, gain1, shift1, bouter, gain2, shift2 = (sums[i * keep : (i + 1) * keep] for i in range(8))
    binner = sums[8 * keep :]
    return (out, grad_tokens, wqkv[0], bq, wqkv[1], wqkv[2], bv, grad_wout, bout, gain1, shift1, grad_winner, binner, grad_wouter, bouter, gain2, shift2)


def solution(mesh):
    layout = Layout(mesh)
    both = ("replica", "group")
    rows, vector = P(both, None), P(both)
    in_specs = (rows, rows, rows, vector, rows, rows, vector, rows, vector, vector, vector, rows, vector, rows, vector, vector, vector, rows)
    kept, kept_vector = P("group", None), P("group")
    out_specs = (rows, rows, kept, kept_vector, kept, kept, kept_vector, kept, kept_vector, kept_vector, kept_vector, kept, kept_vector, kept, kept_vector, kept_vector, kept_vector)
    return jax.shard_map(functools.partial(local, layout), mesh=mesh, in_specs=in_specs, out_specs=out_specs, check_vma=False)
```

```python
import functools
import math

import jax
import jax.numpy as jnp
from jax import lax
from jax.experimental import pallas as pl
from jax.experimental.pallas import tpu as pltpu
from jax.sharding import PartitionSpec as P

F32 = jnp.float32
BF16 = jnp.bfloat16
VMEM_LIMIT = 56 * 1024 * 1024
ANY = pl.BlockSpec(memory_space=pl.ANY)
BQ, BV, BOUT, GAIN1, SHIFT1, BOUTER, GAIN2, SHIFT2 = range(8)


LAST = []


def call(kernel, name, operands, in_specs, out_shape, out_specs, *, grid=(1,), scalars=(), after=(), carry=(), scratch=(), room=None):
    single = not isinstance(out_shape, (tuple, list))
    shapes, specs = ([out_shape], [out_specs]) if single else (list(out_shape), list(out_specs))
    first, made = len(scalars) + len(operands), len(shapes)
    unread = list(carry) + list(after) + LAST

    limit = VMEM_LIMIT
    if room is not None:
        pairs = list(zip(specs, shapes)) + list(zip(in_specs, operands))
        blocks = [math.prod(spec.block_shape) * array.dtype.itemsize for spec, array in pairs if spec.block_shape is not None]
        limit = min(VMEM_LIMIT, 2 * sum(blocks) + room)

    def body(*refs):
        outs = first + len(unread)
        kernel(*refs[:first], *refs[outs : outs + made], *refs[outs + made + len(carry) :])

    outs = pl.pallas_call(
        body,
        out_shape=shapes + [jax.ShapeDtypeStruct(c.shape, c.dtype) for c in carry],
        grid_spec=pltpu.PrefetchScalarGridSpec(
            num_scalar_prefetch=len(scalars),
            grid=grid,
            in_specs=list(in_specs) + [ANY] * len(unread),
            out_specs=specs + [ANY] * len(carry),
            scratch_shapes=list(scratch),
        ),
        input_output_aliases={first + i: made + i for i in range(len(carry))},
        compiler_params=pltpu.CompilerParams(dimension_semantics=("arbitrary",) * len(grid), vmem_limit_bytes=limit),
        cost_estimate=pl.CostEstimate(flops=1, bytes_accessed=1, transcendentals=0),
        name=name,
    )(*scalars, *operands, *unread)
    LAST[:] = outs[made - 1 : made]
    result = outs[0] if single else tuple(outs[:made])
    return (result, outs[made:]) if carry else result


def like(shape, dtype=BF16):
    return jax.ShapeDtypeStruct(shape, dtype)


def dot(left, right):
    return lax.dot_general(left, right, (((1,), (0,)), ((), ())), preferred_element_type=F32)


def dot_nt(left, right):
    return lax.dot_general(left, right, (((1,), (1,)), ((), ())), preferred_element_type=F32)


def whole(shape):
    return pl.BlockSpec(shape, lambda *i: (0,) * len(shape))


def column_sum(value):
    return jnp.sum(value.astype(F32), axis=0, keepdims=True)


def pack(operands, makes, vectors=()):
    lanes = 128 if vectors else 0

    def kernel(*refs):
        outs = refs[len(operands) + len(vectors) :]
        for out_ref, pieces in zip(outs, makes):
            at = 0
            for which, start, size in pieces:
                out_ref[:, at : at + size] = refs[which][:, start : start + size]
                at += size
        if vectors:
            rows, cols = outs[0].shape
            outs[0][:, cols - lanes :] = jnp.zeros((rows, lanes), BF16)
            for ref, (row, lane) in zip(refs[len(operands) :], vector_places(vectors, rows)):
                size = ref.shape[0]
                start = cols - lanes + lane
                outs[0][row : row + 1, start : start + size] = ref[...].astype(F32).reshape(1, size).astype(BF16)

    shapes = [(operands[pieces[0][0]].shape[0], sum(p[2] for p in pieces)) for pieces in makes]
    if vectors:
        shapes[0] = (shapes[0][0], shapes[0][1] + lanes)
    everything = list(operands) + list(vectors)
    return call(kernel, "pack", everything, [whole(o.shape) for o in everything], [like(s) for s in shapes], [whole(s) for s in shapes], room=4 << 20)


def vector_places(vectors, rows):
    size = vectors[0].shape[0]
    places = [(i % rows, i // rows * size) for i in range(len(vectors) - 1)]
    return places + [(8, 0) if rows > 8 else (0, 64)]


def stack(jobs, carry=()):
    flat = [array for arrays, *_ in jobs for array in arrays]
    shapes = []
    for arrays, _, axis, _, cols in jobs:
        shape = arrays[0].shape
        shapes.append(shape[:axis] + (len(arrays),) + shape[axis:-1] + (cols,))

    def kernel(*refs):
        place_refs, refs = refs[: len(jobs)], refs[len(jobs) :]
        ins, outs, arrived = refs[: len(flat)], refs[len(flat) : -1], refs[-1]
        copies = []
        for (arrays, _, axis, first, cols), place_ref, out_ref in zip(jobs, place_refs, outs):
            count = len(arrays)
            for k in range(count):
                ref = ins[len(copies)]
                source = ref.at[(slice(None),) * (len(ref.shape) - 1) + (pl.ds(first, cols),)]
                target = out_ref.at[(slice(None),) * axis + (lax.rem(place_ref[0] + count - k, count),)]
                copies.append(pltpu.make_async_copy(source, target, arrived.at[len(copies)]))
        for copy in copies:
            copy.start()
        for copy in copies:
            copy.wait()

    return call(
        kernel,
        "stack",
        flat,
        [ANY] * len(flat),
        [like(shape) for shape in shapes],
        [whole(shape) for shape in shapes],
        scalars=[job[1] for job in jobs],
        carry=carry,
        scratch=[pltpu.SemaphoreType.DMA((len(flat),))],
        room=4 << 20,
    )


def combine(jobs, carry=(), after=()):
    n = jobs[0][1][0][0].shape[1]
    sizes = []
    for _, terms in jobs:
        before, _, behind, _, _ = terms[0][0].shape
        sizes.append((before, behind) + terms[0][2])
    flat = [t for _, terms in jobs for t in terms]

    def kernel(*refs):
        refs = refs[len(jobs) :]
        outs = refs[len(flat) :]
        i = 0
        for job, (_, terms) in enumerate(jobs):
            total = refs[i][:, 0].astype(F32)
            for ref in refs[i + 1 : i + len(terms)]:
                total = total + ref[:, 0].astype(F32)
            total = total.astype(BF16)
            i += len(terms)
            for j, out_ref in enumerate(outs[job * n : (job + 1) * n]):

                @pl.when(pl.program_id(0) == j)
                def _():
                    out_ref[...] = total

    def at(job, block):
        before, behind, rows, cols = sizes[job]
        return pl.BlockSpec((before, 1, behind, rows, cols), lambda i, *own: (0, lax.rem(own[job][0] + i + 1, n), 0) + block)

    made = call(
        kernel,
        "combine",
        [t[0] for t in flat],
        [at(job, t[1]) for job, (_, terms) in enumerate(jobs) for t in terms],
        [like(size) for size in sizes for _ in range(n)],
        [whole(size) for size in sizes for _ in range(n)],
        grid=(n,),
        scalars=[own for own, _ in jobs],
        carry=carry,
        after=after,
        room=12 << 20,
    )
    made, carried = made if carry else (made, ())
    return [made[job * n : (job + 1) * n] for job in range(len(jobs))], carried


def gather_sums(own, lists):
    flat = [t for terms in lists for t in terms]
    n = flat[0].shape[0]
    rows = max(t.shape[1] for t in flat)
    cols = sum(terms[0].shape[2] for terms in lists)

    def kernel(own_ref, *refs):
        outs = refs[len(flat) :]
        parts, i = [], 0
        for terms in lists:
            total = refs[i][0].astype(F32)
            for ref in refs[i + 1 : i + len(terms)]:
                total = total + ref[0].astype(F32)
            parts.append(total.astype(BF16))
            i += len(terms)
        for j, out_ref in enumerate(outs):

            @pl.when(pl.program_id(0) == j)
            def _():
                at = 0
                for part in parts:
                    high, wide = part.shape
                    out_ref[:high, at : at + wide] = part
                    if high < rows:
                        out_ref[high:, at : at + wide] = jnp.zeros((rows - high, wide), BF16)
                    at += wide

    return call(
        kernel,
        "gather_sums",
        flat,
        [pl.BlockSpec((1,) + t.shape[1:], lambda i, own: (lax.rem(own[0] + i + 1, n), 0, 0)) for t in flat],
        [like((rows, cols))] * n,
        [whole((rows, cols))] * n,
        grid=(n,),
        scalars=[own],
        room=6 << 20,
    )


def add_up(lists, after=()):
    flat = [a for arrays in lists for a in arrays]

    def kernel(*refs):
        at, i = 0, 0
        for arrays in lists:
            total = refs[i][...].astype(F32)
            for ref in refs[i + 1 : i + len(arrays)]:
                total = total + ref[...].astype(F32)
            rows, cols = total.shape
            refs[-1][:rows, at : at + cols] = total.astype(BF16)
            if rows < refs[-1].shape[0]:
                refs[-1][rows:, at : at + cols] = jnp.zeros((refs[-1].shape[0] - rows, cols), BF16)
            at += cols
            i += len(arrays)

    shape = (max(a.shape[0] for a in flat), sum(arrays[0].shape[1] for arrays in lists))
    return call(kernel, "add_up", flat, [whole(a.shape) for a in flat], like(shape), whole(shape), after=after, room=12 << 20)


def outer_result(got, order, runs=2):
    count, cols, rows = got.shape
    rows //= runs

    def kernel(got_ref, out_ref):
        for i, j in enumerate(order):
            for run in range(runs):
                at = (j * runs + run) * cols
                out_ref[:, at : at + cols] = got_ref[i, :, run * rows : (run + 1) * rows].astype(F32).T

    shape = (rows, count * runs * cols)
    return call(kernel, "outer_result", [got], [whole(got.shape)], like(shape, F32), whole(shape), room=8 << 20)


def inner_result(got, order):
    count, rows, cols = got.shape

    def kernel(got_ref, out_ref):
        for i, j in enumerate(order):
            out_ref[:, j * cols : (j + 1) * cols] = got_ref[i].astype(F32)

    shape = (rows, count * cols)
    return call(kernel, "inner_result", [got], [whole(got.shape)], like(shape, F32), whole(shape), room=8 << 20)


def token_weights_result(pieces, places, keep, size, last):
    count = len(pieces)
    rows = pieces[0].shape[0]
    second = 3 * size + last

    def kernel(place_ref, *refs):
        outs = refs[count:]
        for i in range(count):
            at = lambda j, wide: pl.ds(pl.multiple_of(j * wide, wide), wide)
            piece = refs[i][:keep].astype(F32)
            for which in range(3):
                outs[which][:, at(place_ref[i], size)] = piece[:, which * size : (which + 1) * size]
                outs[which][:, at(count + place_ref[i], size)] = piece[:, second + which * size : second + (which + 1) * size]
            outs[3][:, at(place_ref[i], last)] = piece[:, 3 * size : second]
        outs[4][...] = refs[0][keep:, second:].astype(F32)

    shapes = [(keep, 2 * count * size)] * 3 + [(keep, count * last), (rows - keep, 3 * size)]
    return call(
        kernel,
        "token_weights_result",
        pieces,
        [whole(p.shape) for p in pieces],
        [like(s, F32) for s in shapes],
        [whole(s) for s in shapes],
        scalars=[places],
        room=8 << 20,
    )


def transposed(x, tile=256):
    rows, cols = x.shape

    def kernel(x_ref, out_ref):
        out_ref[...] = x_ref[...].T

    return call(
        kernel,
        "transposed",
        [x],
        [pl.BlockSpec((tile, cols), lambda i: (i, 0))],
        like((cols, rows)),
        pl.BlockSpec((cols, tile), lambda i: (0, i)),
        grid=(rows // tile,),
    )


class Pieces:
    def __init__(self, cores, buffers, spans, shape):
        self.cores, self.buffers, self.spans, self.shape = cores, buffers, spans, shape
        self.count = sum(b.shape[0] for b in buffers)

    def part(self, start, cols):
        kept = []
        for buffer, (first, size, to) in zip(self.buffers, self.spans):
            low, high = max(to, start), min(to + size, start + cols)
            kept.append((buffer, (first + low - to, high - low, low - start)))
        buffers, spans = zip(*(k for k in kept if k[1][1] > 0))
        return Pieces(self.cores, list(buffers), list(spans), (self.shape[0], cols))

    def scratch(self):
        return [pltpu.VMEM(self.shape, BF16), pltpu.SemaphoreType.DMA((self.count,)), pltpu.SemaphoreType.DMA]

    def fetch(self, cores_ref, refs, held, arrived):
        copies = []
        for i, (ref, (first, cols, to)) in enumerate(zip(refs, self.spans)):
            blocks, rows, _ = ref.shape
            for j in range(blocks):
                target = held.at[pl.ds(pl.multiple_of((2 * j + cores_ref[i % 2]) * rows, rows), rows), pl.ds(to, cols)]
                copies.append(pltpu.make_async_copy(ref.at[j, :, pl.ds(first, cols)], target, arrived.at[len(copies)]))
        for copy in copies:
            copy.start()
        for copy in copies:
            copy.wait()


def project(pieces, x, vec, half, after=()):
    rows, depth = x.shape
    cols = pieces.shape[1]
    tile = cols // 3
    count = len(pieces.buffers)

    def kernel(*refs):
        (cores_ref,), (x_ref, vec_ref), refs = refs[:1], refs[1 : 3], refs[3:]
        buffer_refs, (out_ref, whole_ref, held, arrived, left) = refs[:count], refs[count:]
        step = pl.program_id(0)
        write = pltpu.make_async_copy(held, whole_ref, left)

        @pl.when(step == 0)
        def _():
            pieces.fetch(cores_ref, buffer_refs, held, arrived)
            write.start()

        at = slice(half * tile, (half + 1) * tile)
        for i, row in enumerate((BQ, None, BV)):

            @pl.when(step == i)
            def _():
                made = dot(x_ref[...], held[:, i * tile : (i + 1) * tile])
                out_ref[...] = (made if row is None else made + vec_ref[row : row + 1, at]).astype(BF16)

        @pl.when(step == 2)
        def _():
            write.wait()

    return call(
        kernel,
        "project",
        [x, vec] + list(pieces.buffers),
        [whole(x.shape), whole(vec.shape)] + [ANY] * count,
        (like((rows, cols)), like((depth, cols))),
        (pl.BlockSpec((rows, tile), lambda i, *_: (0, i)), ANY),
        grid=(3,),
        scalars=[pieces.cores],
        scratch=pieces.scratch(),
        after=after,
    )


def attend(qkv, row, col, heads=4, size=64, after=()):
    seqs, _, length = row.shape
    width = qkv.shape[1] // 3
    block = heads * size
    blocks = width // block

    def kernel(q_ref, k_ref, v_ref, row_ref, col_ref, o_ref, ot_ref, p_ref, r_ref, bias_ref):
        @pl.when(pl.program_id(1) == 0)
        def _():
            bias_ref[...] = jnp.where(col_ref[0] == row_ref[0], 0.0, -1e9).astype(F32)

        qt = (q_ref[...] * jnp.asarray(0.125, BF16)).T
        vt = v_ref[...].T
        zero = jnp.zeros((size, length), BF16)
        for head in range(heads):
            here = slice(head * size, (head + 1) * size)
            pair = slice(head // 2 * 2 * size, (head // 2 + 1) * 2 * size)
            own = [qt[here], zero] if head % 2 == 0 else [zero, qt[here]]
            scores = dot(k_ref[:, pair], jnp.concatenate(own, axis=0)) + bias_ref[...]
            expo = jnp.exp(scores - jnp.max(scores, axis=0, keepdims=True))
            share = 1.0 / jnp.sum(expo, axis=0, keepdims=True)
            expo = expo.astype(BF16)
            p_ref[0, head] = expo
            r_ref[0, 0, head : head + 1] = share
            ot_ref[here, :] = (dot(vt[here], expo) * share).astype(BF16)
        o_ref[...] = ot_ref[...].T

    spec = lambda part: pl.BlockSpec((length, block), lambda s, p: (s, part * blocks + p))
    return call(
        kernel,
        "attend",
        [qkv, qkv, qkv, row, col],
        [spec(0), spec(1), spec(2), pl.BlockSpec((1, 1, length), lambda s, p: (s, 0, 0)), pl.BlockSpec((1, length, 1), lambda s, p: (s, 0, 0))],
        (like((seqs * length, width)), like((width, seqs * length)), like((seqs, heads * blocks, length, length)), like((seqs, blocks, heads, length), F32)),
        (
            pl.BlockSpec((length, block), lambda s, p: (s, p)),
            pl.BlockSpec((block, length), lambda s, p: (p, s)),
            pl.BlockSpec((1, heads, length, length), lambda s, p: (s, p, 0, 0)),
            pl.BlockSpec((1, 1, heads, length), lambda s, p: (s, p, 0, 0)),
        ),
        grid=(seqs, blocks),
        scratch=[pltpu.VMEM((length, length), F32)],
        after=after,
    )


def attend_back(qkv, ot, probs, share, do, part, after=()):
    seqs, blocks, heads, length = share.shape
    tokens, width = ot.shape[1], ot.shape[0]
    block = width // blocks
    size = block // heads

    def kernel(q_ref, k_ref, v_ref, ot_ref, p_ref, r_ref, do_ref, d_ref, bq_ref, bv_ref):
        dot_t = do_ref[...].T.astype(F32)
        shares = jnp.concatenate([jnp.broadcast_to(r_ref[0, 0, h : h + 1], (size, length)) for h in range(heads)], axis=0)
        dot_t = (dot_t * shares).astype(BF16)
        do = dot_t.T
        kt = k_ref[...].T
        product = dot_t.astype(F32) * ot_ref[...].astype(F32)
        zero = jnp.zeros((size, length), BF16)
        first = lax.broadcasted_iota(jnp.int32, (1, 2 * size), 1) < size
        dk, dv, dqt = [], [], []
        for head in range(heads):
            here = slice(head * size, (head + 1) * size)
            pair = slice(head // 2 * 2 * size, (head // 2 + 1) * 2 * size)
            delta = jnp.sum(product[here], axis=0, keepdims=True)
            own = [dot_t[here], zero] if head % 2 == 0 else [zero, dot_t[here]]
            expo = p_ref[0, head]
            ds = (expo.astype(F32) * (dot(v_ref[:, pair], jnp.concatenate(own, axis=0)) - delta)).astype(BF16)
            dv.append(dot(expo, do[:, pair]))
            dk.append(dot(ds, q_ref[:, pair]))
            dqt.append(dot(kt[here], ds))
        paired = lambda parts: jnp.concatenate([jnp.where(first, parts[i], parts[i + 1]) for i in range(0, heads, 2)], axis=1)
        dq = (jnp.concatenate(dqt, axis=0) * 0.125).astype(BF16).T
        dv = paired(dv).astype(BF16)
        d_ref[0] = dq
        d_ref[1] = (paired(dk) * 0.125).astype(BF16)
        d_ref[2] = dv
        bq_ref[0] = column_sum(dq)
        bv_ref[0] = column_sum(dv)

    spec = lambda which: pl.BlockSpec((length, block), lambda s, p: (s, which * blocks + p))
    sums = pl.BlockSpec((1, 1, block), lambda s, p: (s, 0, p))
    return call(
        kernel,
        "attend_back",
        [qkv, qkv, qkv, ot, probs, share, do],
        [
            spec(0),
            spec(1),
            spec(2),
            pl.BlockSpec((block, length), lambda s, p: (p, s)),
            pl.BlockSpec((1, heads, length, length), lambda s, p: (s, p, 0, 0)),
            pl.BlockSpec((1, 1, heads, length), lambda s, p: (s, p, 0, 0)),
            spec(part),
        ],
        (like((3, tokens, width)), like((seqs, 1, width), F32), like((seqs, 1, width), F32)),
        (pl.BlockSpec((3, length, block), lambda s, p: (0, s, p)), sums, sums),
        grid=(seqs, blocks),
        after=after,
    )


def normed(z):
    center = z - jnp.mean(z, axis=-1, keepdims=True)
    rstd = lax.rsqrt(jnp.mean(center * center, axis=-1, keepdims=True) + 1e-06)
    return center * rstd, rstd


def norm_back(dn, n, rstd):
    return rstd * (dn - jnp.mean(dn, axis=-1, keepdims=True) - n * jnp.mean(dn * n, axis=-1, keepdims=True))


def join(pieces, o0, o1, x, vec, tile=256, after=()):
    rows, width = x.shape
    count = len(pieces.buffers)

    def kernel(*refs):
        (cores_ref,), (o0_ref, o1_ref, x_ref, vec_ref), refs = refs[:1], refs[1 : 5], refs[5:]
        buffer_refs, (n_ref, r_ref, h_ref, ht_ref, whole_ref, held, arrived, left) = refs[:count], refs[count:]
        write = pltpu.make_async_copy(held, whole_ref, left)

        @pl.when(pl.program_id(0) == 0)
        def _():
            pieces.fetch(cores_ref, buffer_refs, held, arrived)
            write.start()

        half = o0_ref.shape[1]
        mixed = dot(o0_ref[...], held[:half]) + dot(o1_ref[...], held[half:])
        z = x_ref[...].astype(F32) + (mixed + vec_ref[BOUT : BOUT + 1])
        n, rstd = normed(z)
        n_ref[...] = n
        r_ref[...] = rstd
        h = (n * vec_ref[GAIN1 : GAIN1 + 1] + vec_ref[SHIFT1 : SHIFT1 + 1]).astype(BF16)
        h_ref[...] = h
        ht_ref[...] = h.T

        @pl.when(pl.program_id(0) == pl.num_programs(0) - 1)
        def _():
            write.wait()

    tok = pl.BlockSpec((tile, width), lambda i, *_: (i, 0))
    half = pl.BlockSpec((tile, width // 2), lambda i, *_: (i, 0))
    return call(
        kernel,
        "join",
        [o0, o1, x, vec] + list(pieces.buffers),
        [half, half, tok, whole(vec.shape)] + [ANY] * count,
        (like((rows, width), F32), like((rows, 1), F32), like((rows, width)), like((width, rows)), like((width, width))),
        (tok, pl.BlockSpec((tile, 1), lambda i, *_: (i, 0)), tok, pl.BlockSpec((width, tile), lambda i, *_: (0, i)), ANY),
        grid=(rows // tile,),
        scalars=[pieces.cores],
        scratch=pieces.scratch(),
        after=after,
    )


def inner(h, rest, bias, tile=512, after=()):
    rows, depth = h.shape
    cols = bias.shape[1]

    def kernel(h_ref, w_ref, b_ref, u_ref, g_ref):
        f = dot(h_ref[...], w_ref[...]) + b_ref[...]
        weight = 0.5 + 0.5 * lax.erf(f * math.sqrt(0.5))
        u_ref[...] = (f * weight).astype(BF16)
        bell = jnp.exp2((f * f) * (-0.5 * math.log2(math.e)))
        g_ref[...] = (weight + (f * (1.0 / math.sqrt(2.0 * math.pi))) * bell).astype(BF16)

    out = pl.BlockSpec((rows, tile), lambda i: (0, i))
    return call(
        kernel,
        "inner",
        [h, rest, bias],
        [whole(h.shape), pl.BlockSpec((depth, tile), lambda i: (0, i)), pl.BlockSpec((1, tile), lambda i: (0, i))],
        (like((rows, cols)), like((rows, cols))),
        (out, out),
        grid=(cols // tile,),
        after=after,
    )


def outer(pieces, u, n1, cot, vec, tile=256, after=()):
    rows, depth = u.shape
    width = n1.shape[1]
    count = len(pieces.buffers)

    def kernel(*refs):
        (cores_ref,), (u_ref, n_ref, c_ref, vec_ref), refs = refs[:1], refs[1 : 5], refs[5:]
        buffer_refs, (out_ref, dz_ref, dm_ref, dmt_ref, sums_ref, whole_ref, held, arrived, left) = refs[:count], refs[count:]
        write = pltpu.make_async_copy(held, whole_ref, left)

        @pl.when(pl.program_id(0) == 0)
        def _():
            sums_ref[...] = jnp.zeros_like(sums_ref)
            pieces.fetch(cores_ref, buffer_refs, held, arrived)
            write.start()

        row = lambda i: vec_ref[i : i + 1]
        z = (n_ref[...] * row(GAIN1) + row(SHIFT1)) + (dot(u_ref[...], held[...]) + row(BOUTER))
        n, rstd = normed(z)
        out_ref[...] = (n * row(GAIN2) + row(SHIFT2)).astype(BF16)
        c = c_ref[...].astype(F32)
        dz = norm_back(c * row(GAIN2), n, rstd)
        dz_ref[...] = dz
        dm = dz.astype(BF16)
        dm_ref[...] = dm
        dmt_ref[...] = dm.T
        sums_ref[0:1, :] += column_sum(dm)
        sums_ref[1:2, :] += column_sum(c * n)
        sums_ref[2:3, :] += column_sum(c)

        @pl.when(pl.program_id(0) == pl.num_programs(0) - 1)
        def _():
            write.wait()

    tok = pl.BlockSpec((tile, width), lambda i, *_: (i, 0))
    return call(
        kernel,
        "outer",
        [u, n1, cot, vec] + list(pieces.buffers),
        [pl.BlockSpec((tile, depth), lambda i, *_: (i, 0)), tok, tok, whole(vec.shape)] + [ANY] * count,
        (like((rows, width)), like((rows, width), F32), like((rows, width)), like((width, rows)), like((8, width), F32), like((depth, width))),
        (tok, tok, tok, pl.BlockSpec((width, tile), lambda i, *_: (0, i)), whole((8, width)), ANY),
        grid=(rows // tile,),
        scalars=[pieces.cores],
        scratch=pieces.scratch(),
        after=after,
    )


def outer_grad(half, dmt, u, groups, after=()):
    width, rows = dmt.shape
    cols = u.shape[1]
    part = cols // groups
    blocks = 2048 // part

    def kernel(half_ref, left_ref, right_ref, out_ref):
        made = dot(left_ref[...], right_ref[...]).astype(BF16)
        for i in range(blocks):
            out_ref[:, i] = made[:, i * part : (i + 1) * part].reshape(2, width // 4, part)

    return call(
        kernel,
        "outer_grad",
        [dmt, u],
        [pl.BlockSpec((width // 2, rows), lambda i, half: (half[0], 0)), pl.BlockSpec((rows, blocks * part), lambda i, half: (0, i))],
        like((2, groups, width // 4, part)),
        pl.BlockSpec((2, blocks, width // 4, part), lambda i, half: (0, i, 0, 0)),
        grid=(groups // blocks,),
        scalars=[half],
        after=after,
    )


def inner_back(halves, dm, w2, slope, ht, w1, groups, tile=512, after=()):
    rows, width = dm.shape
    cols = slope.shape[1]
    steps = cols // 2 // tile
    per = steps // 2

    def kernel(halves_ref, dm_ref, w2_ref, g_ref, ht_ref, w1_ref, first_ref, second_ref, dh_ref, sum_ref):
        step = pl.program_id(0)

        @pl.when(step == 0)
        def _():
            dh_ref[...] = jnp.zeros_like(dh_ref)

        df = (dot_nt(dm_ref[...], w2_ref[...]) * g_ref[...].astype(F32)).astype(BF16)
        sum_ref[...] = column_sum(df)
        made = dot(ht_ref[...], df).astype(BF16).reshape(first_ref.shape)

        @pl.when(step < steps)
        def _():
            first_ref[...] = made

        @pl.when(step >= steps)
        def _():
            second_ref[...] = made

        dh_ref[...] += dot_nt(df, w1_ref[...])

    at = lambda i, halves: halves[i // steps] * steps + i % steps
    grad = like((2, groups, width // groups, cols // 4))
    block = (1, groups, width // groups, tile)
    kept = lambda step: (step // per, 0, 0, step % per)
    return call(
        kernel,
        "inner_back",
        [dm, w2, slope, ht, w1],
        [
            whole(dm.shape),
            pl.BlockSpec((tile, width), lambda i, halves: (at(i, halves), 0)),
            pl.BlockSpec((rows, tile), lambda i, halves: (0, at(i, halves))),
            whole(ht.shape),
            pl.BlockSpec((width, tile), lambda i, halves: (0, at(i, halves))),
        ],
        (grad, grad, like((rows, width), F32), like((1, cols), F32)),
        (
            pl.BlockSpec(block, lambda i, halves: kept(jnp.minimum(i, steps - 1))),
            pl.BlockSpec(block, lambda i, halves: kept(jnp.maximum(i - steps, 0))),
            whole((rows, width)),
            pl.BlockSpec((1, tile), lambda i, halves: (0, at(i, halves))),
        ),
        grid=(2 * steps,),
        scalars=[halves],
        after=after,
    )


def join_back(dz2, dh, n1, rstd, vec, w, tile=256, after=()):
    rows, width = dz2.shape

    def kernel(dz2_ref, dh_ref, n_ref, r_ref, vec_ref, w_ref, dz_ref, da_ref, do_ref, sums_ref):
        @pl.when(pl.program_id(0) == 0)
        def _():
            sums_ref[...] = jnp.zeros_like(sums_ref)

        dh = dz2_ref[...] + dh_ref[...]
        n = n_ref[...]
        dz = norm_back(dh * vec_ref[GAIN1 : GAIN1 + 1], n, r_ref[...])
        dz_ref[...] = dz
        da = dz.astype(BF16)
        da_ref[...] = da
        do_ref[...] = dot_nt(da, w_ref[...]).astype(BF16)
        sums_ref[0:1, :] += column_sum(da)
        sums_ref[1:2, :] += column_sum(dh * n)
        sums_ref[2:3, :] += column_sum(dh)

    tok = pl.BlockSpec((tile, width), lambda i: (i, 0))
    return call(
        kernel,
        "join_back",
        [dz2, dh, n1, rstd, vec, w],
        [tok, tok, tok, pl.BlockSpec((tile, 1), lambda i: (i, 0)), whole(vec.shape), whole(w.shape)],
        (like((rows, width), F32), like((rows, width)), like((rows, width)), like((8, width), F32)),
        (tok, tok, tok, whole((8, width))),
        grid=(rows // tile,),
        after=after,
    )


def token_weights_grad(halves, xt, d, groups, mixed=None, extra=None, after=()):
    width, rows = xt.shape
    part = d.shape[2] // 2
    last = width // 4
    mixed_at = -(-3 * part // (2 * last)) * last
    cols = mixed_at + last if mixed else 3 * part // 2
    more = 0 if extra is None else extra.shape[1]
    keep = width // groups

    def kernel(halves_ref, left_ref, d_ref, *refs):
        refs, first_ref, second_ref = refs[:-2], refs[-2], refs[-1]

        def fill(out_ref):
            def store(made, start, group, blocks):
                size = made.shape[1] // 2
                for x in range(2):
                    piece = made[:, x * size : (x + 1) * size].reshape(blocks, keep, size)
                    out_ref[x, group : group + blocks, :keep, start : start + size] = piece

            for which in range(3):
                store(dot(left_ref[...], d_ref[which]).astype(BF16), which * (part // 2), 0, groups)
            if mixed:
                for i in range(2):
                    store(dot(refs[i][...], refs[2][...]).astype(BF16), mixed_at, i * groups // 2, groups // 2)
                if mixed_at > 3 * part // 2:
                    out_ref[:, :, :, 3 * part // 2 : mixed_at] = jnp.zeros((2, groups, keep, mixed_at - 3 * part // 2), BF16)
            if more:
                for x in range(2):
                    out_ref[x, :, keep:, :] = refs[-1][...]

        @pl.when(pl.program_id(0) == 0)
        def _():
            fill(first_ref)

        @pl.when(pl.program_id(0) == 1)
        def _():
            fill(second_ref)

    operands = [xt, d]
    specs = [whole(xt.shape), pl.BlockSpec((3, rows, part), lambda i, halves: (0, 0, halves[i]))]
    if mixed:
        operands += mixed
        specs += [whole(mixed[0].shape), whole(mixed[1].shape), pl.BlockSpec((rows, width // 2), lambda i, halves: (0, halves[i]))]
    if more:
        operands.append(extra)
        specs.append(whole(extra.shape))
    shape = (2, groups, keep + more, cols)
    return call(
        kernel,
        "token_weights_grad",
        operands,
        specs,
        (like(shape), like(shape)),
        (whole(shape), whole(shape)),
        grid=(2,),
        scalars=[halves],
        after=after,
    )


def token_grad(base, d, w, dtype, tile=256, after=()):
    rows, width = base.shape
    part = d.shape[2]

    def kernel(base_ref, d_ref, w_ref, out_ref):
        total = base_ref[...]
        for i in range(3):
            total = total + dot_nt(d_ref[i], w_ref[:, i * part : (i + 1) * part])
        out_ref[...] = total.astype(dtype)

    tok = pl.BlockSpec((tile, width), lambda i: (i, 0))
    return call(
        kernel,
        "token_grad",
        [base, d, w],
        [tok, pl.BlockSpec((3, tile, part), lambda i: (0, i, 0)), whole(w.shape)],
        like((rows, width), dtype),
        tok,
        grid=(rows // tile,),
        after=after,
    )


def digits_of(axis, total, base):
    digits, stride = [], total
    while stride > 1:
        size = base if stride % base == 0 else 2
        stride //= size
        digits.append((axis, stride, size))
    return digits


def total_of(terms):
    total = terms[0].astype(F32)
    for term in terms[1:]:
        total = total + term.astype(F32)
    return total.astype(BF16)


class Layout:
    def __init__(self, mesh):
        self.replicas, self.groups = mesh.shape["replica"], mesh.shape["group"]
        self.group = digits_of("group", self.groups, 4)
        replica = digits_of("replica", self.replicas, 2)
        self.core, self.over = replica[-1], replica[:-1]
        self.sizes = {"replica": self.replicas, "group": self.groups}
        self.devices = self.replicas * self.groups
        cores = self.core[2]
        self.same_core = [
            [r * self.groups + g for r in range(c, self.replicas, cores) for g in range(self.groups)] for c in range(cores)
        ]

    def place(self, digit):
        axis, stride, size = digit
        return (lax.axis_index(axis) // stride) % size

    def send(self, value, digit, shift=1):
        axis, stride, size = digit
        pairs = []
        for i in range(self.sizes[axis]):
            own = (i // stride) % size
            pairs.append((i, i + ((own + shift) % size - own) * stride))
        return lax.ppermute(value, axis, pairs)

    def sends(self, value, digit):
        return [self.send(value, digit, k) for k in range(1, digit[2])]

    def pieces(self, parts, shape):
        core = self.place(self.core).astype(jnp.int32)
        cores = jnp.stack([core, 1 - core])
        buffers, spans, start = [], [], 0
        for chain, cols in parts:
            came = self.send(chain.value, self.core)
            blocks = math.prod(d[2] for d in self.over)
            for buffer in (chain.value, came):
                buffers.append(buffer.reshape(blocks, -1, buffer.shape[-1]))
                spans.append((0, cols, start))
            start += cols
        return Pieces(cores, buffers, spans, shape)

    def along(self, digit):
        axis, stride, size = digit
        stride *= self.groups if axis == "replica" else 1
        starts = [d for d in range(self.devices) if d // stride % size == 0]
        return [[d + k * stride for k in range(size)] for d in starts]


class Chain:
    def __init__(self, layout, value, order, done=()):
        self.layout, self.value, self.order, self.done = layout, value, list(order), list(done)
        self.came = layout.sends(value, self.order[0]) if self.order else []

    def job(self, first=0, cols=None):
        digits = self.layout.over + self.layout.group
        axis = sum(digits.index(d) < digits.index(self.order[0]) for d in self.done)
        place = self.layout.place(self.order[0]).astype(jnp.int32).reshape(1)
        return [self.value] + self.came, place, axis, first, self.value.shape[-1] if cols is None else cols

    def after(self, value, order=None):
        return Chain(self.layout, value, (self.order if order is None else order)[1:], self.done + self.order[:1])


def move(*chains, carry=()):
    values = stack([c.job() for c in chains], carry)
    values, carried = values if carry else (values, ())
    moved = [c.after(v) for c, v in zip(chains, values)]
    return moved + list(carried)


class Reduction:
    def __init__(self, layout, terms, order):
        self.layout, self.dims, self.terms, self.order = layout, layout.over + layout.group, terms, list(order)

    def job(self):
        digit = self.digit = self.order.pop(0)
        axis = self.dims.index(digit)
        count = lambda dims: math.prod(d[2] for d in dims)
        shape = (count(self.dims[:axis]), digit[2], count(self.dims[axis + 1 :]))
        self.dims = self.dims[:axis] + self.dims[axis + 1 :]
        terms = [(t.reshape(shape + t.shape[-2:]), block, cols) for t, block, cols in self.terms]
        return self.layout.place(digit).astype(jnp.int32).reshape(1), terms

    def take(self, made):
        came = [self.layout.send(s, self.digit, k + 1) for k, s in enumerate(made[:-1])]
        self.terms = [(t, (0, 0), t.shape[-2:]) for t in [made[-1]] + came]

    def came(self):
        return [t for t, _, _ in self.terms[1:]]

    def last(self):
        return [t.reshape((-1,) + t.shape[-2:]) for t, _, _ in self.terms]


def step(*reductions, carry=(), after=()):
    jobs = [r.job() for r in reductions]
    if len({r.digit[2] for r in reductions}) == 1:
        made, carry = combine(jobs, carry, after)
    else:
        made = []
        for job in jobs:
            one, carry = combine([job], carry, after)
            made += one
    for reduction, one in zip(reductions, made):
        reduction.take(one)
    return carry


def local(layout, tokens, segment_ids, w_query, b_query, w_key, w_value, b_value, w_out, b_out, gain_first, shift_first, w_inner, b_inner, w_outer, b_outer, gain_second, shift_second, cotangent):
    LAST.clear()
    groups, devices = layout.groups, layout.devices
    seqs, length = segment_ids.shape
    width = tokens.shape[1]
    hidden = w_inner.shape[1]
    each = b_query.shape[0]
    half = width // 2
    core = layout.place(layout.core).astype(jnp.int32)
    mine, theirs = core.reshape(1), (1 - core).reshape(1)
    halves = jnp.concatenate([theirs, mine])
    z_digit, y_digits = layout.group[:1], layout.group[1:]
    zxy, zyx = z_digit + layout.over + y_digits, z_digit + y_digits + layout.over
    xyz, yxz = layout.over + y_digits + z_digit, y_digits + layout.over + z_digit

    vectors = (b_query, b_value, b_out, gain_first, shift_first, b_outer, gain_second, shift_second, b_inner)
    lanes, cut, wide = 128, 3 * half // 2, (3 * half + width) // 2
    (first,) = pack([w_query, w_key, w_value], [[(0, 0, half), (1, 0, half), (2, 0, half)]], vectors)
    high = first.shape[0]
    first = Chain(layout, first, zxy)
    xt = transposed(tokens)
    a, b = stack([first.job(0, cut), first.job(cut, cut + lanes)])
    a, b = first.after(a), first.after(b, zyx)
    second, last, inner_rows = pack(
        [w_query, w_key, w_value, w_out, w_outer, w_inner],
        [[(0, half, half), (1, half, half), (2, half, half), (3, 0, width)], [(4, 0, width)], [(5, 0, hidden)]],
    )
    second = Chain(layout, second, zxy)
    (va, vb, vc, vd), (inner_rows,) = stack([a.job(), b.job(), second.job(0, wide), second.job(wide, wide)], carry=[inner_rows])
    a, b, c, d = a.after(va), b.after(vb), second.after(vc), second.after(vd, zyx)
    whole_winner = lax.all_gather(inner_rows, ("replica", "group"), axis=0, tiled=True)
    while a.order:
        a, b, c, d = move(a, b, c, d)
    pieces0 = layout.pieces([(a, cut), (b, cut)], (width, 3 * half))
    spots = vector_places(vectors, high)
    used = max(r for r, _ in spots) + 1
    both = [v.reshape(-1, groups, high, v.shape[-1])[:, :, :used, cut:].astype(F32) for v in pieces0.buffers[-2:]]
    small = jnp.stack([jnp.where(core == k, both[0], both[1]) for k in range(2)], axis=1).reshape(devices, used, lanes)
    vec = jnp.stack([small[:, r, l : l + each].reshape(width) for r, l in spots[:-1]])
    r, l = spots[-1]
    whole_binner = small[:, r, l : l + b_inner.shape[0]].reshape(1, -1)
    row, col = segment_ids.reshape(seqs, 1, length), segment_ids.reshape(seqs, length, 1)

    qkv0, wqkv0 = project(pieces0, tokens, vec, 0)
    while c.order:
        c, d, last = move(c, d, carry=[last])
    pieces1 = layout.pieces([(c, wide), (d, wide)], (width, 3 * half + width))
    last = Chain(layout, last, zxy)
    o0, ot0, probs0, share0 = attend(qkv0, row, col)
    qkv1, wqkv1 = project(pieces1.part(0, 3 * half), tokens, vec, 1)
    e, f = stack([last.job(0, half), last.job(half, half)])
    e, f = last.after(e), last.after(f, zyx)
    o1, ot1, probs1, share1 = attend(qkv1, row, col)
    while len(e.order) > 1:
        e, f = move(e, f)
    n1, rstd1, h, ht, whole_wout = join(pieces1.part(3 * half, width), o0, o1, tokens, vec)
    u, slope = inner(h, whole_winner, whole_binner)
    e, f = move(e, f)
    pieces2 = layout.pieces([(e, half), (f, half)], (w_outer.shape[0] * devices, width))
    out, dz2, dm, dmt, sums2, whole_wouter = outer(pieces2, u, n1, cotangent, vec)

    def reduction(other, own, *orders, by_rows=False, runs=None):
        came = layout.send(other, layout.core)
        rows, cols = own.shape[2:]
        if by_rows:
            parts = [((i, 0), (rows // len(orders), cols)) for i in range(len(orders))]
        else:
            runs = runs or [(i * cols // len(orders), cols // len(orders)) for i in range(len(orders))]
            parts = [((0, start // size), (rows, size)) for start, size in runs]
        return [Reduction(layout, [(own,) + part, (came,) + part], order) for part, order in zip(parts, orders)]

    def along_z(reductions):
        sums = add_up([[t.reshape(-1, t.shape[-1]) for t in r.last()] for r in reductions])
        return lax.psum_scatter(sums, ("replica", "group"), scatter_dimension=0, axis_index_groups=layout.along(z_digit[0]), tiled=True)

    def across_z(reductions):
        made = gather_sums(layout.place(z_digit[0]).astype(jnp.int32).reshape(1), [r.last() for r in reductions])
        return [made[-1]] + [layout.send(s, z_digit[0], k + 1) for k, s in enumerate(made[:-1])]

    spread = lambda block: lax.all_gather(block, "replica", axis=0, tiled=False)
    other = outer_grad(theirs, dmt, u, groups)
    own = outer_grad(mine, dmt, u, groups)
    outers = reduction(other, own, xyz, yxz, by_rows=True)
    step(*outers)
    other, own, dh, sum_inner = inner_back(halves, dm, whole_wouter, slope, ht, whole_winner, groups)
    for _ in range(len(xyz) - 2):
        (other,) = step(*outers, carry=[other])
    inners = reduction(other, own, xyz, yxz)
    dz1, da, do, sums1 = join_back(dz2, dh, n1, rstd1, vec, whole_wout)
    got_wouter = along_z(outers)
    step(*inners)
    d0, sq0, sv0 = attend_back(qkv0, ot0, probs0, share0, do, 0)
    other, own = token_weights_grad(halves, xt, d0, groups, mixed=[ot0, ot1, da])
    for _ in range(len(xyz) - 2):
        (other,) = step(*inners, carry=[other])
    runs = ((0, 3 * half // 4), (other.shape[3] - width // 4, width // 4))
    firsts = reduction(other, own, xyz, yxz, runs=runs)
    d1, sq1, sv1 = attend_back(qkv1, ot1, probs1, share1, do, 1)
    bq = jnp.concatenate([jnp.sum(s, axis=0) for s in (sq0, sq1)], axis=1)
    bv = jnp.concatenate([jnp.sum(s, axis=0) for s in (sv0, sv1)], axis=1)
    sums = jnp.concatenate([bq, bv, sums1[:3], sums2[:3]], axis=0)
    sums = sums.reshape(8, groups, -1).transpose(1, 0, 2).reshape(groups, -1)
    sums = jnp.concatenate([sums, sum_inner.reshape(groups, -1)], axis=1)
    used, cols = sums.shape[1], 3 * half // 4
    extra = jnp.pad(sums.astype(BF16), ((0, 0), (0, 16 * cols - used))).reshape(groups, 16, cols)
    got_winner = along_z(inners)
    step(*firsts)
    partial = token_grad(dz1, d0, wqkv0, F32)
    other, own = token_weights_grad(halves, xt, d1, groups, extra=extra)
    for _ in range(len(xyz) - 2):
        (other,) = step(*firsts, carry=[other])
    seconds = reduction(other, own, xyz, yxz, runs=((0, 2 * cols // 3), (2 * cols // 3, cols // 3)))
    grad_tokens = token_grad(partial, d1, wqkv1, BF16)
    step(*seconds, after=[t for r in firsts for t in r.came()])
    first_sums = across_z(firsts)
    for _ in range(len(xyz) - 2):
        step(*seconds, after=first_sums[1:])
    second_sums = across_z(seconds)
    got_wouter, got_winner = spread(got_wouter), spread(got_winner)
    cores = layout.core[2]
    order = [r % cores * (layout.replicas // cores) + r // cores for r in range(layout.replicas)]
    grad_wouter = outer_result(got_wouter, order)
    grad_winner = inner_result(got_winner, order)
    got = [add_up([first_sums, second_sums])]
    places = jnp.zeros((1,), jnp.int32)
    weight = 1
    for digit in layout.over[::-1] + [layout.core]:
        own = layout.place(digit).astype(jnp.int32)
        places = jnp.concatenate([places + own * weight, places + (1 - own) * weight])
        got = got + [layout.send(g, digit) for g in got]
        weight *= digit[2]
    keep = width // groups
    wq, wk, wv, grad_wout, sums = token_weights_result(got, places, keep, half // 4, width // 4)
    sums = sums.reshape(-1)[:used]
    bq, bv, bout, gain1, shift1, bouter, gain2, shift2 = (sums[i * keep : (i + 1) * keep] for i in range(8))
    binner = sums[8 * keep :]
    return (out, grad_tokens, wq, bq, wk, wv, bv, grad_wout, bout, gain1, shift1, grad_winner, binner, grad_wouter, bouter, gain2, shift2)


def solution(mesh):
    layout = Layout(mesh)
    both = ("replica", "group")
    rows, vector = P(both, None), P(both)
    in_specs = (rows, rows, rows, vector, rows, rows, vector, rows, vector, vector, vector, rows, vector, rows, vector, vector, vector, rows)
    kept, kept_vector = P("group", None), P("group")
    out_specs = (rows, rows, kept, kept_vector, kept, kept, kept_vector, kept, kept_vector, kept_vector, kept_vector, kept, kept_vector, kept, kept_vector, kept_vector, kept_vector)
    return jax.shard_map(functools.partial(local, layout), mesh=mesh, in_specs=in_specs, out_specs=out_specs, check_vma=False)
```

```python
import functools
import math

import jax
import jax.numpy as jnp
from jax import lax
from jax.experimental import pallas as pl
from jax.experimental.pallas import tpu as pltpu
from jax.sharding import PartitionSpec as P

F32 = jnp.float32
BF16 = jnp.bfloat16
VMEM_LIMIT = 48 * 1024 * 1024
ANY = pl.BlockSpec(memory_space=pl.ANY)
ALL_VMEM = 62 * 1024 * 1024
HBM = pl.BlockSpec(memory_space=pltpu.HBM)
BQ, BV, BOUT, GAIN1, SHIFT1, BOUTER, GAIN2, SHIFT2 = range(8)


LAST = []


def call(kernel, name, operands, in_specs, out_shape, out_specs, *, grid=(1,), scalars=(), after=(), carry=(), into=(), scratch=(), time=0, room=10 << 20):
    single = not isinstance(out_shape, (tuple, list))
    shapes, specs = ([out_shape], [out_specs]) if single else (list(out_shape), list(out_specs))
    first, made = len(scalars) + len(operands), len(shapes)
    ends = made + len(carry)
    unread = list(carry) + list(into) + list(after) + LAST

    pairs = list(zip(specs, shapes)) + list(zip(in_specs, operands))
    blocks = [math.prod(spec.block_shape) * array.dtype.itemsize for spec, array in pairs if spec.block_shape is not None]
    held = [math.prod(s.shape) * jnp.dtype(s.dtype).itemsize for s in scratch if getattr(s, "dtype", None) in (BF16, F32)]
    limit = ALL_VMEM if room is None else min(VMEM_LIMIT, 2 * sum(blocks) + sum(held) + room)

    def body(*refs):
        outs = first + len(unread)
        kernel(*refs[:first], *refs[outs : outs + made], *refs[outs + ends + 1 :])

    outs = pl.pallas_call(
        body,
        out_shape=shapes + [jax.ShapeDtypeStruct(c.shape, c.dtype) for c in carry] + [jax.ShapeDtypeStruct((8, 128), F32)],
        grid_spec=pltpu.PrefetchScalarGridSpec(
            num_scalar_prefetch=len(scalars),
            grid=grid,
            in_specs=list(in_specs) + [HBM] * len(carry) + [ANY] * (len(unread) - len(carry) - len(LAST)) + [HBM] * len(LAST),
            out_specs=specs + [HBM] * (len(carry) + 1),
            scratch_shapes=list(scratch),
        ),
        input_output_aliases={first + i: made + i for i in range(len(carry))} | {first + len(carry) + i: i for i in range(len(into))},
        compiler_params=pltpu.CompilerParams(dimension_semantics=("arbitrary",) * len(grid), vmem_limit_bytes=limit),
        cost_estimate=pl.CostEstimate(flops=int(1 + time * 1e9), bytes_accessed=int(1 + time * 1e6), transcendentals=0),
        name=name,
    )(*scalars, *operands, *unread)
    LAST[:] = outs[ends:]
    result = outs[0] if single else tuple(outs[:made])
    return (result, outs[made:ends]) if carry else result


def like(shape, dtype=BF16):
    return jax.ShapeDtypeStruct(shape, dtype)


def dot(left, right):
    return lax.dot_general(left, right, (((1,), (0,)), ((), ())), preferred_element_type=F32)


def dot_nt(left, right):
    return lax.dot_general(left, right, (((1,), (1,)), ((), ())), preferred_element_type=F32)


def whole(shape):
    return pl.BlockSpec(shape, lambda *i: (0,) * len(shape))


def column_sum(value):
    return jnp.sum(value.astype(F32), axis=0, keepdims=True)


def pack(operands, makes, vectors=()):
    lanes = 128 if vectors else 0

    def kernel(*refs):
        outs = refs[len(operands) + len(vectors) :]
        for out_ref, pieces in zip(outs, makes):
            at = 0
            for which, start, size in pieces:
                out_ref[:, at : at + size] = refs[which][:, start : start + size]
                at += size
        if vectors:
            rows, cols = outs[0].shape
            outs[0][:, cols - lanes :] = jnp.zeros((rows, lanes), BF16)
            for ref, (row, lane) in zip(refs[len(operands) :], vector_places(vectors, rows)):
                size = ref.shape[0]
                start = cols - lanes + lane
                outs[0][row : row + 1, start : start + size] = ref[...].astype(F32).reshape(1, size).astype(BF16)

    shapes = [(operands[pieces[0][0]].shape[0], sum(p[2] for p in pieces)) for pieces in makes]
    if vectors:
        shapes[0] = (shapes[0][0], shapes[0][1] + lanes)
    everything = list(operands) + list(vectors)
    return call(kernel, "pack", everything, [whole(o.shape) for o in everything], [like(s) for s in shapes], [whole(s) for s in shapes], room=None)


def vector_places(vectors, rows):
    size = vectors[0].shape[0]
    places = [(i % rows, i // rows * size) for i in range(len(vectors) - 1)]
    return places + [(8, 0) if rows > 8 else (0, 64)]


def stack(jobs, carry=()):
    flat = [array for arrays, *_ in jobs for array in arrays]
    shapes = []
    for arrays, _, axis, _, cols in jobs:
        shape = arrays[0].shape
        shapes.append(shape[:axis] + (len(arrays),) + shape[axis:-1] + (cols,))

    def kernel(*refs):
        place_refs, refs = refs[: len(jobs)], refs[len(jobs) :]
        ins, outs, arrived = refs[: len(flat)], refs[len(flat) : -1], refs[-1]
        copies = []
        for (arrays, _, axis, first, cols), place_ref, out_ref in zip(jobs, place_refs, outs):
            count = len(arrays)
            for k in range(count):
                ref = ins[len(copies)]
                source = ref.at[(slice(None),) * (len(ref.shape) - 1) + (pl.ds(first, cols),)]
                target = out_ref.at[(slice(None),) * axis + (lax.rem(place_ref[0] + count - k, count),)]
                copies.append(pltpu.make_async_copy(source, target, arrived.at[len(copies)]))
        for copy in copies:
            copy.start()
        for copy in copies:
            copy.wait()

    return call(
        kernel,
        "stack",
        flat,
        [ANY] * len(flat),
        [like(shape) for shape in shapes],
        [whole(shape) for shape in shapes],
        scalars=[job[1] for job in jobs],
        carry=carry,
        scratch=[pltpu.SemaphoreType.DMA((len(flat),))],
        room=4 << 20,
    )


def combine(jobs, carry=(), after=()):
    n = jobs[0][1][0][0].shape[1]
    sizes = []
    for _, terms in jobs:
        before, _, behind, _, _ = terms[0][0].shape
        sizes.append((before, behind) + terms[0][2])
    flat = [t for _, terms in jobs for t in terms]

    def kernel(*refs):
        refs = refs[len(jobs) :]
        outs = refs[len(flat) :]
        i = 0
        for job, (_, terms) in enumerate(jobs):
            total = refs[i][:, 0].astype(F32)
            for ref in refs[i + 1 : i + len(terms)]:
                total = total + ref[:, 0].astype(F32)
            total = total.astype(BF16)
            i += len(terms)
            for j, out_ref in enumerate(outs[job * n : (job + 1) * n]):

                @pl.when(pl.program_id(0) == j)
                def _():
                    out_ref[...] = total

    def at(job, block):
        before, behind, rows, cols = sizes[job]
        return pl.BlockSpec((before, 1, behind, rows, cols), lambda i, *own: (0, lax.rem(own[job][0] + i + 1, n), 0) + block)

    made = call(
        kernel,
        "combine",
        [t[0] for t in flat],
        [at(job, t[1]) for job, (_, terms) in enumerate(jobs) for t in terms],
        [like(size) for size in sizes for _ in range(n)],
        [whole(size) for size in sizes for _ in range(n)],
        grid=(n,),
        scalars=[own for own, _ in jobs],
        carry=carry,
        after=after,
        room=12 << 20,
    )
    made, carried = made if carry else (made, ())
    return [made[job * n : (job + 1) * n] for job in range(len(jobs))], carried


def gather_sums(own, lists, carry=()):
    flat = [t for terms in lists for t in terms]
    n = flat[0].shape[0]
    rows = max(t.shape[1] for t in flat)
    cols = sum(terms[0].shape[2] for terms in lists)

    def kernel(own_ref, *refs):
        outs = refs[len(flat) :]
        parts, i = [], 0
        for terms in lists:
            total = refs[i][0].astype(F32)
            for ref in refs[i + 1 : i + len(terms)]:
                total = total + ref[0].astype(F32)
            parts.append(total.astype(BF16))
            i += len(terms)
        for j, out_ref in enumerate(outs):

            @pl.when(pl.program_id(0) == j)
            def _():
                at = 0
                for part in parts:
                    high, wide = part.shape
                    out_ref[:high, at : at + wide] = part
                    if high < rows:
                        out_ref[high:, at : at + wide] = jnp.zeros((rows - high, wide), BF16)
                    at += wide

    return call(
        kernel,
        "gather_sums",
        flat,
        [pl.BlockSpec((1,) + t.shape[1:], lambda i, own: (lax.rem(own[0] + i + 1, n), 0, 0)) for t in flat],
        [like((rows, cols))] * n,
        [whole((rows, cols))] * n,
        grid=(n,),
        scalars=[own],
        carry=carry,
        room=6 << 20,
    )


def add_up(lists, carry=()):
    flat = [a for arrays in lists for a in arrays]

    def kernel(*refs):
        at, i = 0, 0
        for arrays in lists:
            total = refs[i][...].astype(F32)
            for ref in refs[i + 1 : i + len(arrays)]:
                total = total + ref[...].astype(F32)
            rows, cols = total.shape
            refs[-1][:rows, at : at + cols] = total.astype(BF16)
            if rows < refs[-1].shape[0]:
                refs[-1][rows:, at : at + cols] = jnp.zeros((refs[-1].shape[0] - rows, cols), BF16)
            at += cols
            i += len(arrays)

    shape = (max(a.shape[0] for a in flat), sum(arrays[0].shape[1] for arrays in lists))
    return call(kernel, "add_up", flat, [whole(a.shape) for a in flat], like(shape), whole(shape), carry=carry, room=12 << 20)


def outer_result(got, order, runs=2):
    count, cols, rows = got.shape
    rows //= runs

    def kernel(got_ref, out_ref):
        for i, j in enumerate(order):
            for run in range(runs):
                at = (j * runs + run) * cols
                out_ref[:, at : at + cols] = got_ref[i, :, run * rows : (run + 1) * rows].astype(F32).T

    shape = (rows, count * runs * cols)
    return call(kernel, "outer_result", [got], [whole(got.shape)], like(shape, F32), whole(shape), room=8 << 20)


def inner_result(got, order):
    count, rows, cols = got.shape

    def kernel(got_ref, out_ref):
        for i, j in enumerate(order):
            out_ref[:, j * cols : (j + 1) * cols] = got_ref[i].astype(F32)

    shape = (rows, count * cols)
    return call(kernel, "inner_result", [got], [whole(got.shape)], like(shape, F32), whole(shape), room=8 << 20)


def token_weights_result(pieces, places, keep, size, last):
    count = len(pieces)
    rows = pieces[0].shape[0]
    second = 3 * size + last

    def kernel(place_ref, *refs):
        outs = refs[count:]
        for i in range(count):
            at = lambda j, wide: pl.ds(pl.multiple_of(j * wide, wide), wide)
            piece = refs[i][:keep].astype(F32)
            for which in range(3):
                outs[which][:, at(place_ref[i], size)] = piece[:, which * size : (which + 1) * size]
                outs[which][:, at(count + place_ref[i], size)] = piece[:, second + which * size : second + (which + 1) * size]
            outs[3][:, at(place_ref[i], last)] = piece[:, 3 * size : second]
        outs[4][...] = refs[0][keep:, second:].astype(F32)

    shapes = [(keep, 2 * count * size)] * 3 + [(keep, count * last), (rows - keep, 3 * size)]
    return call(
        kernel,
        "token_weights_result",
        pieces,
        [whole(p.shape) for p in pieces],
        [like(s, F32) for s in shapes],
        [whole(s) for s in shapes],
        scalars=[places],
        room=8 << 20,
    )


def transposed(x, tile=256):
    rows, cols = x.shape

    def kernel(x_ref, out_ref):
        out_ref[...] = x_ref[...].T

    return call(
        kernel,
        "transposed",
        [x],
        [pl.BlockSpec((tile, cols), lambda i: (i, 0))],
        like((cols, rows)),
        pl.BlockSpec((cols, tile), lambda i: (0, i)),
        grid=(rows // tile,),
        time=3,
    )


class Pieces:
    def __init__(self, cores, buffers, spans, shape):
        self.cores, self.buffers, self.spans, self.shape = cores, buffers, spans, shape
        self.count = sum(b.shape[0] for b in buffers)

    def part(self, start, cols):
        kept = []
        for buffer, (first, size, to) in zip(self.buffers, self.spans):
            low, high = max(to, start), min(to + size, start + cols)
            kept.append((buffer, (first + low - to, high - low, low - start)))
        buffers, spans = zip(*(k for k in kept if k[1][1] > 0))
        return Pieces(self.cores, list(buffers), list(spans), (self.shape[0], cols))

    def scratch(self):
        return [pltpu.VMEM(self.shape, BF16), pltpu.SemaphoreType.DMA((self.count,)), pltpu.SemaphoreType.DMA]

    def fetch(self, cores_ref, refs, held, arrived):
        copies = []
        for i, (ref, (first, cols, to)) in enumerate(zip(refs, self.spans)):
            blocks, rows, _ = ref.shape
            for j in range(blocks):
                target = held.at[pl.ds(pl.multiple_of((2 * j + cores_ref[i % 2]) * rows, rows), rows), pl.ds(to, cols)]
                copies.append(pltpu.make_async_copy(ref.at[j, :, pl.ds(first, cols)], target, arrived.at[len(copies)]))
        for copy in copies:
            copy.start()
        for copy in copies:
            copy.wait()


def project(pieces, x, vec, half, carry=()):
    rows, depth = x.shape
    cols = pieces.shape[1]
    tile = cols // 3
    count = len(pieces.buffers)

    def kernel(*refs):
        (cores_ref,), (x_ref, vec_ref), refs = refs[:1], refs[1 : 3], refs[3:]
        buffer_refs, (out_ref, whole_ref, held, arrived, left) = refs[:count], refs[count:]
        step = pl.program_id(0)
        write = pltpu.make_async_copy(held, whole_ref, left)

        @pl.when(step == 0)
        def _():
            pieces.fetch(cores_ref, buffer_refs, held, arrived)
            write.start()

        at = slice(half * tile, (half + 1) * tile)
        for i, row in enumerate((BQ, None, BV)):

            @pl.when(step == i)
            def _():
                made = dot(x_ref[...], held[:, i * tile : (i + 1) * tile])
                out_ref[...] = (made if row is None else made + vec_ref[row : row + 1, at]).astype(BF16)

        @pl.when(step == 2)
        def _():
            write.wait()

    return call(
        kernel,
        "project",
        [x, vec] + list(pieces.buffers),
        [whole(x.shape), whole(vec.shape)] + [ANY] * count,
        (like((rows, cols)), like((depth, cols))),
        (pl.BlockSpec((rows, tile), lambda i, *_: (0, i)), HBM),
        grid=(3,),
        scalars=[pieces.cores],
        scratch=pieces.scratch(),
        carry=carry,
        time=6,
    )


def attend(qkv, row, col, heads=4, size=64, carry=()):
    seqs, _, length = row.shape
    width = qkv.shape[1] // 3
    block = heads * size
    blocks = width // block

    def kernel(q_ref, k_ref, v_ref, row_ref, col_ref, o_ref, ot_ref, p_ref, r_ref, bias_ref):
        @pl.when(pl.program_id(1) == 0)
        def _():
            bias_ref[...] = jnp.where(col_ref[0] == row_ref[0], 0.0, -1e9).astype(F32)

        qt = (q_ref[...] * jnp.asarray(0.125, BF16)).T
        vt = v_ref[...].T
        zero = jnp.zeros((size, length), BF16)
        for head in range(heads):
            here = slice(head * size, (head + 1) * size)
            pair = slice(head // 2 * 2 * size, (head // 2 + 1) * 2 * size)
            own = [qt[here], zero] if head % 2 == 0 else [zero, qt[here]]
            scores = dot(k_ref[:, pair], jnp.concatenate(own, axis=0)) + bias_ref[...]
            expo = jnp.exp(scores - jnp.max(scores, axis=0, keepdims=True))
            share = 1.0 / jnp.sum(expo, axis=0, keepdims=True)
            expo = expo.astype(BF16)
            p_ref[0, head] = expo
            r_ref[0, 0, head : head + 1] = share
            ot_ref[here, :] = (dot(vt[here], expo) * share).astype(BF16)
        o_ref[...] = ot_ref[...].T

    spec = lambda part: pl.BlockSpec((length, block), lambda s, p: (s, part * blocks + p))
    return call(
        kernel,
        "attend",
        [qkv, qkv, qkv, row, col],
        [spec(0), spec(1), spec(2), pl.BlockSpec((1, 1, length), lambda s, p: (s, 0, 0)), pl.BlockSpec((1, length, 1), lambda s, p: (s, 0, 0))],
        (like((seqs * length, width)), like((width, seqs * length)), like((seqs, heads * blocks, length, length)), like((seqs, blocks, heads, length), F32)),
        (
            pl.BlockSpec((length, block), lambda s, p: (s, p)),
            pl.BlockSpec((block, length), lambda s, p: (p, s)),
            pl.BlockSpec((1, heads, length, length), lambda s, p: (s, p, 0, 0)),
            pl.BlockSpec((1, 1, heads, length), lambda s, p: (s, p, 0, 0)),
        ),
        grid=(seqs, blocks),
        scratch=[pltpu.VMEM((length, length), F32)],
        carry=carry,
        time=11,
    )


def attend_back(qkv, ot, probs, share, do, part, carry=()):
    seqs, blocks, heads, length = share.shape
    tokens, width = ot.shape[1], ot.shape[0]
    block = width // blocks
    size = block // heads

    def kernel(q_ref, k_ref, v_ref, ot_ref, p_ref, r_ref, do_ref, d_ref, bq_ref, bv_ref):
        dot_t = do_ref[...].T.astype(F32)
        shares = jnp.concatenate([jnp.broadcast_to(r_ref[0, 0, h : h + 1], (size, length)) for h in range(heads)], axis=0)
        dot_t = (dot_t * shares).astype(BF16)
        do = dot_t.T
        kt = k_ref[...].T
        product = dot_t.astype(F32) * ot_ref[...].astype(F32)
        zero = jnp.zeros((size, length), BF16)
        first = lax.broadcasted_iota(jnp.int32, (1, 2 * size), 1) < size
        dk, dv, dqt = [], [], []
        for head in range(heads):
            here = slice(head * size, (head + 1) * size)
            pair = slice(head // 2 * 2 * size, (head // 2 + 1) * 2 * size)
            delta = jnp.sum(product[here], axis=0, keepdims=True)
            own = [dot_t[here], zero] if head % 2 == 0 else [zero, dot_t[here]]
            expo = p_ref[0, head]
            ds = (expo.astype(F32) * (dot(v_ref[:, pair], jnp.concatenate(own, axis=0)) - delta)).astype(BF16)
            dv.append(dot(expo, do[:, pair]))
            dk.append(dot(ds, q_ref[:, pair]))
            dqt.append(dot(kt[here], ds))
        paired = lambda parts: jnp.concatenate([jnp.where(first, parts[i], parts[i + 1]) for i in range(0, heads, 2)], axis=1)
        dq = (jnp.concatenate(dqt, axis=0) * 0.125).astype(BF16).T
        dv = paired(dv).astype(BF16)
        d_ref[0] = dq
        d_ref[1] = (paired(dk) * 0.125).astype(BF16)
        d_ref[2] = dv
        bq_ref[0] = column_sum(dq)
        bv_ref[0] = column_sum(dv)

    spec = lambda which: pl.BlockSpec((length, block), lambda s, p: (s, which * blocks + p))
    sums = pl.BlockSpec((1, 1, block), lambda s, p: (s, 0, p))
    return call(
        kernel,
        "attend_back",
        [qkv, qkv, qkv, ot, probs, share, do],
        [
            spec(0),
            spec(1),
            spec(2),
            pl.BlockSpec((block, length), lambda s, p: (p, s)),
            pl.BlockSpec((1, heads, length, length), lambda s, p: (s, p, 0, 0)),
            pl.BlockSpec((1, 1, heads, length), lambda s, p: (s, p, 0, 0)),
            spec(part),
        ],
        (like((3, tokens, width)), like((seqs, 1, width), F32), like((seqs, 1, width), F32)),
        (pl.BlockSpec((3, length, block), lambda s, p: (0, s, p)), sums, sums),
        grid=(seqs, blocks),
        carry=carry,
        time=11,
    )


def normed(z):
    center = z - jnp.mean(z, axis=-1, keepdims=True)
    rstd = lax.rsqrt(jnp.mean(center * center, axis=-1, keepdims=True) + 1e-06)
    return center * rstd, rstd


def norm_back(dn, n, rstd):
    return rstd * (dn - jnp.mean(dn, axis=-1, keepdims=True) - n * jnp.mean(dn * n, axis=-1, keepdims=True))


def join(pieces, o0, o1, x, vec, tile=256, after=()):
    rows, width = x.shape
    count = len(pieces.buffers)

    def kernel(*refs):
        (cores_ref,), (o0_ref, o1_ref, x_ref, vec_ref), refs = refs[:1], refs[1 : 5], refs[5:]
        buffer_refs, (n_ref, r_ref, h_ref, ht_ref, whole_ref, held, arrived, left) = refs[:count], refs[count:]
        write = pltpu.make_async_copy(held, whole_ref, left)

        @pl.when(pl.program_id(0) == 0)
        def _():
            pieces.fetch(cores_ref, buffer_refs, held, arrived)
            write.start()

        half = o0_ref.shape[1]
        mixed = dot(o0_ref[...], held[:half]) + dot(o1_ref[...], held[half:])
        z = x_ref[...].astype(F32) + (mixed + vec_ref[BOUT : BOUT + 1])
        n, rstd = normed(z)
        n_ref[...] = n
        r_ref[...] = rstd
        h = (n * vec_ref[GAIN1 : GAIN1 + 1] + vec_ref[SHIFT1 : SHIFT1 + 1]).astype(BF16)
        h_ref[...] = h
        ht_ref[...] = h.T

        @pl.when(pl.program_id(0) == pl.num_programs(0) - 1)
        def _():
            write.wait()

    tok = pl.BlockSpec((tile, width), lambda i, *_: (i, 0))
    half = pl.BlockSpec((tile, width // 2), lambda i, *_: (i, 0))
    return call(
        kernel,
        "join",
        [o0, o1, x, vec] + list(pieces.buffers),
        [half, half, tok, whole(vec.shape)] + [ANY] * count,
        (like((rows, width), F32), like((rows, 1), F32), like((rows, width)), like((width, rows)), like((width, width))),
        (tok, pl.BlockSpec((tile, 1), lambda i, *_: (i, 0)), tok, pl.BlockSpec((width, tile), lambda i, *_: (0, i)), HBM),
        grid=(rows // tile,),
        scalars=[pieces.cores],
        scratch=pieces.scratch(),
        after=after,
        time=7,
    )


def inner(h, rest, bias, run=0, runs=1, into=(), tile=512):
    rows, depth = h.shape
    cols = bias.shape[1]
    steps = cols // tile // runs

    def kernel(h_ref, w_ref, b_ref, u_ref, g_ref):
        f = dot(h_ref[...], w_ref[...]) + b_ref[...]
        weight = 0.5 + 0.5 * lax.erf(f * math.sqrt(0.5))
        u_ref[...] = (f * weight).astype(BF16)
        bell = jnp.exp2((f * f) * (-0.5 * math.log2(math.e)))
        g_ref[...] = (weight + (f * (1.0 / math.sqrt(2.0 * math.pi))) * bell).astype(BF16)

    at = lambda i: (0, run * steps + i)
    out = pl.BlockSpec((rows, tile), at)
    return call(
        kernel,
        "inner",
        [h, rest, bias],
        [whole(h.shape), pl.BlockSpec((depth, tile), at), pl.BlockSpec((1, tile), at)],
        (like((rows, cols)), like((rows, cols))),
        (out, out),
        grid=(steps,),
        into=into,
        time=9,
    )


def outer(pieces, u, n1, cot, vec, tile=256, after=()):
    rows, depth = u.shape
    width = n1.shape[1]
    count = len(pieces.buffers)

    def kernel(*refs):
        (cores_ref,), (u_ref, n_ref, c_ref, vec_ref), refs = refs[:1], refs[1 : 5], refs[5:]
        buffer_refs, (out_ref, dz_ref, dm_ref, dmt_ref, sums_ref, whole_ref, held, arrived, left) = refs[:count], refs[count:]
        write = pltpu.make_async_copy(held, whole_ref, left)

        @pl.when(pl.program_id(0) == 0)
        def _():
            sums_ref[...] = jnp.zeros_like(sums_ref)
            pieces.fetch(cores_ref, buffer_refs, held, arrived)
            write.start()

        row = lambda i: vec_ref[i : i + 1]
        z = (n_ref[...] * row(GAIN1) + row(SHIFT1)) + (dot(u_ref[...], held[...]) + row(BOUTER))
        n, rstd = normed(z)
        out_ref[...] = (n * row(GAIN2) + row(SHIFT2)).astype(BF16)
        c = c_ref[...].astype(F32)
        dz = norm_back(c * row(GAIN2), n, rstd)
        dz_ref[...] = dz
        dm = dz.astype(BF16)
        dm_ref[...] = dm
        dmt_ref[...] = dm.T
        sums_ref[0:1, :] += column_sum(dm)
        sums_ref[1:2, :] += column_sum(c * n)
        sums_ref[2:3, :] += column_sum(c)

        @pl.when(pl.program_id(0) == pl.num_programs(0) - 1)
        def _():
            write.wait()

    tok = pl.BlockSpec((tile, width), lambda i, *_: (i, 0))
    return call(
        kernel,
        "outer",
        [u, n1, cot, vec] + list(pieces.buffers),
        [pl.BlockSpec((tile, depth), lambda i, *_: (i, 0)), tok, tok, whole(vec.shape)] + [ANY] * count,
        (like((rows, width)), like((rows, width), F32), like((rows, width)), like((width, rows)), like((8, width), F32), like((depth, width))),
        (tok, tok, tok, pl.BlockSpec((width, tile), lambda i, *_: (0, i)), whole((8, width)), HBM),
        grid=(rows // tile,),
        scalars=[pieces.cores],
        scratch=pieces.scratch(),
        after=after,
        time=19,
    )


def outer_grad(half, dmt, u, groups, after=()):
    width, rows = dmt.shape
    cols = u.shape[1]
    part = cols // groups
    blocks = 2048 // part

    def kernel(half_ref, left_ref, right_ref, out_ref):
        made = dot(left_ref[...], right_ref[...]).astype(BF16)
        for i in range(blocks):
            out_ref[:, i] = made[:, i * part : (i + 1) * part].reshape(2, width // 4, part)

    return call(
        kernel,
        "outer_grad",
        [dmt, u],
        [pl.BlockSpec((width // 2, rows), lambda i, half: (half[0], 0)), pl.BlockSpec((rows, blocks * part), lambda i, half: (0, i))],
        like((2, groups, width // 4, part)),
        pl.BlockSpec((2, blocks, width // 4, part), lambda i, half: (0, i, 0, 0)),
        grid=(groups // blocks,),
        scalars=[half],
        after=after,
        time=6,
    )


def inner_back(halves, dm, w2, slope, ht, w1, groups, tile=512, after=()):
    rows, width = dm.shape
    cols = slope.shape[1]
    steps = cols // 2 // tile
    per = steps // 2

    def kernel(halves_ref, dm_ref, w2_ref, g_ref, ht_ref, w1_ref, first_ref, second_ref, dh_ref, sum_ref):
        step = pl.program_id(0)

        @pl.when(step == 0)
        def _():
            dh_ref[...] = jnp.zeros_like(dh_ref)

        df = (dot_nt(dm_ref[...], w2_ref[...]) * g_ref[...].astype(F32)).astype(BF16)
        sum_ref[...] = column_sum(df)
        made = dot(ht_ref[...], df).astype(BF16).reshape(first_ref.shape)

        @pl.when(step < steps)
        def _():
            first_ref[...] = made

        @pl.when(step >= steps)
        def _():
            second_ref[...] = made

        dh_ref[...] += dot_nt(df, w1_ref[...])

    at = lambda i, halves: halves[i // steps] * steps + i % steps
    grad = like((2, groups, width // groups, cols // 4))
    block = (1, groups, width // groups, tile)
    kept = lambda step: (step // per, 0, 0, step % per)
    return call(
        kernel,
        "inner_back",
        [dm, w2, slope, ht, w1],
        [
            whole(dm.shape),
            pl.BlockSpec((tile, width), lambda i, halves: (at(i, halves), 0)),
            pl.BlockSpec((rows, tile), lambda i, halves: (0, at(i, halves))),
            whole(ht.shape),
            pl.BlockSpec((width, tile), lambda i, halves: (0, at(i, halves))),
        ],
        (grad, grad, like((rows, width), F32), like((1, cols), F32)),
        (
            pl.BlockSpec(block, lambda i, halves: kept(jnp.minimum(i, steps - 1))),
            pl.BlockSpec(block, lambda i, halves: kept(jnp.maximum(i - steps, 0))),
            whole((rows, width)),
            pl.BlockSpec((1, tile), lambda i, halves: (0, at(i, halves))),
        ),
        grid=(2 * steps,),
        scalars=[halves],
        after=after,
        time=35,
    )


def join_back(dz2, dh, n1, rstd, vec, w, tile=256, after=()):
    rows, width = dz2.shape

    def kernel(dz2_ref, dh_ref, n_ref, r_ref, vec_ref, w_ref, dz_ref, da_ref, do_ref, sums_ref):
        @pl.when(pl.program_id(0) == 0)
        def _():
            sums_ref[...] = jnp.zeros_like(sums_ref)

        dh = dz2_ref[...] + dh_ref[...]
        n = n_ref[...]
        dz = norm_back(dh * vec_ref[GAIN1 : GAIN1 + 1], n, r_ref[...])
        dz_ref[...] = dz
        da = dz.astype(BF16)
        da_ref[...] = da
        do_ref[...] = dot_nt(da, w_ref[...]).astype(BF16)
        sums_ref[0:1, :] += column_sum(da)
        sums_ref[1:2, :] += column_sum(dh * n)
        sums_ref[2:3, :] += column_sum(dh)

    tok = pl.BlockSpec((tile, width), lambda i: (i, 0))
    return call(
        kernel,
        "join_back",
        [dz2, dh, n1, rstd, vec, w],
        [tok, tok, tok, pl.BlockSpec((tile, 1), lambda i: (i, 0)), whole(vec.shape), whole(w.shape)],
        (like((rows, width), F32), like((rows, width)), like((rows, width)), like((8, width), F32)),
        (tok, tok, tok, whole((8, width))),
        grid=(rows // tile,),
        after=after,
        time=8,
    )


def token_weights_grad(halves, xt, d, groups, mixed=None, vectors=(), carry=()):
    width, rows = xt.shape
    part = d.shape[2] // 2
    size, last = part // 2, width // 4
    keep = width // groups
    mixed_at = -(-3 * size // last) * last
    cols = mixed_at + last if mixed else 3 * size
    more = 16 if vectors else 0
    arrays = [a for group, _ in vectors for a in group]

    def kernel(halves_ref, left_ref, d_ref, *refs):
        def put(out_ref):
            at, read = keep, list(refs)
            for group, row in vectors:
                here, read = read[: len(group)], read[len(group) :]
                values = [jnp.sum(ref[...], axis=0) if len(ref.shape) == 3 else ref[row : row + 1] for ref in here]
                wide = values[0].shape[1]
                many = wide * len(group) // groups
                for g in range(groups):
                    for i in range(many // keep):
                        start = g * many + i * keep
                        piece = values[start // wide][:, start % wide : start % wide + keep].astype(BF16)
                        for x in range(2):
                            out_ref[x, g, at + i : at + i + 1, :keep] = piece
                at += many // keep

        def store(out_ref, made, start, group, blocks):
            wide = made.shape[1] // 2
            for x in range(2):
                piece = made[:, x * wide : (x + 1) * wide].reshape(blocks, keep, wide)
                out_ref[x, group : group + blocks, :keep, start : start + wide] = piece

        for step, out_ref in enumerate(refs[-2:]):

            @pl.when(pl.program_id(0) == step)
            def _():
                for which in range(3):
                    store(out_ref, dot(left_ref[...], d_ref[which]).astype(BF16), which * size, 0, groups)
                if mixed:
                    for i in range(2):
                        made = dot(refs[i][...], refs[2][...]).astype(BF16)
                        store(out_ref, made, mixed_at, i * groups // 2, groups // 2)
                    if mixed_at > 3 * size:
                        out_ref[:, :, :, 3 * size : mixed_at] = jnp.zeros((2, groups, keep, mixed_at - 3 * size), BF16)
                if more:
                    out_ref[:, :, keep:, :] = jnp.zeros((2, groups, more, cols), BF16)
                    put(out_ref)

    operands = [xt, d] + list(mixed or ()) + arrays
    specs = [whole(xt.shape), pl.BlockSpec((3, rows, part), lambda i, halves: (0, 0, halves[i]))]
    if mixed:
        specs += [whole(mixed[0].shape), whole(mixed[1].shape), pl.BlockSpec((rows, width // 2), lambda i, halves: (0, halves[i]))]
    specs += [whole(a.shape) for a in arrays]
    shape = (2, groups, keep + more, cols)
    return call(
        kernel,
        "token_weights_grad",
        operands,
        specs,
        (like(shape), like(shape)),
        (whole(shape), whole(shape)),
        grid=(2,),
        scalars=[halves],
        carry=carry,
        time=8,
    )


def token_grad(base, d, w, dtype, tile=256, after=()):
    rows, width = base.shape
    part = d.shape[2]

    def kernel(base_ref, d_ref, w_ref, out_ref):
        total = base_ref[...]
        for i in range(3):
            total = total + dot_nt(d_ref[i], w_ref[:, i * part : (i + 1) * part])
        out_ref[...] = total.astype(dtype)

    tok = pl.BlockSpec((tile, width), lambda i: (i, 0))
    return call(
        kernel,
        "token_grad",
        [base, d, w],
        [tok, pl.BlockSpec((3, tile, part), lambda i: (0, i, 0)), whole(w.shape)],
        like((rows, width), dtype),
        tok,
        grid=(rows // tile,),
        after=after,
        time=6,
    )


def digits_of(axis, total, base):
    digits, stride = [], total
    while stride > 1:
        size = base if stride % base == 0 else 2
        stride //= size
        digits.append((axis, stride, size))
    return digits


def total_of(terms):
    total = terms[0].astype(F32)
    for term in terms[1:]:
        total = total + term.astype(F32)
    return total.astype(BF16)


class Layout:
    def __init__(self, mesh):
        self.replicas, self.groups = mesh.shape["replica"], mesh.shape["group"]
        self.group = digits_of("group", self.groups, 4)
        replica = digits_of("replica", self.replicas, 2)
        self.core, self.over = replica[-1], replica[:-1]
        self.sizes = {"replica": self.replicas, "group": self.groups}
        self.devices = self.replicas * self.groups
        cores = self.core[2]
        self.same_core = [
            [r * self.groups + g for r in range(c, self.replicas, cores) for g in range(self.groups)] for c in range(cores)
        ]

    def place(self, digit):
        axis, stride, size = digit
        return (lax.axis_index(axis) // stride) % size

    def send(self, value, digit, shift=1):
        axis, stride, size = digit
        pairs = []
        for i in range(self.sizes[axis]):
            own = (i // stride) % size
            pairs.append((i, i + ((own + shift) % size - own) * stride))
        return lax.ppermute(value, axis, pairs)

    def sends(self, value, digit):
        return [self.send(value, digit, k) for k in range(1, digit[2])]

    def pieces(self, parts, shape):
        core = self.place(self.core).astype(jnp.int32)
        cores = jnp.stack([core, 1 - core])
        buffers, spans, start = [], [], 0
        for chain, cols in parts:
            came = self.send(chain.value, self.core)
            blocks = math.prod(d[2] for d in self.over)
            for buffer in (chain.value, came):
                buffers.append(buffer.reshape(blocks, -1, buffer.shape[-1]))
                spans.append((0, cols, start))
            start += cols
        return Pieces(cores, buffers, spans, shape)

    def along(self, digit):
        axis, stride, size = digit
        stride *= self.groups if axis == "replica" else 1
        starts = [d for d in range(self.devices) if d // stride % size == 0]
        return [[d + k * stride for k in range(size)] for d in starts]


class Chain:
    def __init__(self, layout, value, order, done=()):
        self.layout, self.value, self.order, self.done = layout, value, list(order), list(done)
        self.came = layout.sends(value, self.order[0]) if self.order else []

    def job(self, first=0, cols=None):
        digits = self.layout.over + self.layout.group
        axis = sum(digits.index(d) < digits.index(self.order[0]) for d in self.done)
        place = self.layout.place(self.order[0]).astype(jnp.int32).reshape(1)
        return [self.value] + self.came, place, axis, first, self.value.shape[-1] if cols is None else cols

    def after(self, value, order=None):
        return Chain(self.layout, value, (self.order if order is None else order)[1:], self.done + self.order[:1])


def move(*chains, carry=()):
    values = stack([c.job() for c in chains], carry)
    values, carried = values if carry else (values, ())
    moved = [c.after(v) for c, v in zip(chains, values)]
    return moved + list(carried)


class Reduction:
    def __init__(self, layout, terms, order):
        self.layout, self.dims, self.terms, self.order = layout, layout.over + layout.group, terms, list(order)

    def job(self):
        digit = self.digit = self.order.pop(0)
        axis = self.dims.index(digit)
        count = lambda dims: math.prod(d[2] for d in dims)
        shape = (count(self.dims[:axis]), digit[2], count(self.dims[axis + 1 :]))
        self.dims = self.dims[:axis] + self.dims[axis + 1 :]
        terms = [(t.reshape(shape + t.shape[-2:]), block, cols) for t, block, cols in self.terms]
        return self.layout.place(digit).astype(jnp.int32).reshape(1), terms

    def take(self, made):
        came = [self.layout.send(s, self.digit, k + 1) for k, s in enumerate(made[:-1])]
        self.terms = [(t, (0, 0), t.shape[-2:]) for t in [made[-1]] + came]

    def came(self):
        return [t for t, _, _ in self.terms[1:]]

    def last(self):
        return [t.reshape((-1,) + t.shape[-2:]) for t, _, _ in self.terms]


def step(*reductions, carry=(), after=()):
    jobs = [r.job() for r in reductions]
    if len({r.digit[2] for r in reductions}) == 1:
        made, carry = combine(jobs, carry, after)
    else:
        made = []
        for job in jobs:
            one, carry = combine([job], carry, after)
            made += one
    for reduction, one in zip(reductions, made):
        reduction.take(one)
    return carry


def local(layout, tokens, segment_ids, w_query, b_query, w_key, w_value, b_value, w_out, b_out, gain_first, shift_first, w_inner, b_inner, w_outer, b_outer, gain_second, shift_second, cotangent):
    LAST.clear()
    groups, devices = layout.groups, layout.devices
    seqs, length = segment_ids.shape
    width = tokens.shape[1]
    hidden = w_inner.shape[1]
    each = b_query.shape[0]
    half = width // 2
    core = layout.place(layout.core).astype(jnp.int32)
    mine, theirs = core.reshape(1), (1 - core).reshape(1)
    halves = jnp.concatenate([theirs, mine])
    z_digit, y_digits = layout.group[:1], layout.group[1:]
    zxy, zyx = z_digit + layout.over + y_digits, z_digit + y_digits + layout.over
    xyz, yxz = layout.over + y_digits + z_digit, y_digits + layout.over + z_digit

    vectors = (b_query, b_value, b_out, gain_first, shift_first, b_outer, gain_second, shift_second, b_inner)
    lanes, cut, wide = 128, 3 * half // 2, (3 * half + width) // 2
    (first,) = pack([w_query, w_key, w_value], [[(0, 0, half), (1, 0, half), (2, 0, half)]], vectors)
    high = first.shape[0]
    first = Chain(layout, first, zxy)
    xt = transposed(tokens)
    a, b = stack([first.job(0, cut), first.job(cut, cut + lanes)])
    a, b = first.after(a), first.after(b, zyx)
    second, last, inner_rows = pack(
        [w_query, w_key, w_value, w_out, w_outer, w_inner],
        [[(0, half, half), (1, half, half), (2, half, half), (3, 0, width)], [(4, 0, width)], [(5, 0, hidden)]],
    )
    whole_winner = lax.all_gather(inner_rows, ("replica", "group"), axis=0, tiled=True)
    a, b, second = move(a, b, carry=[second])
    second = Chain(layout, second, zxy)
    while a.order[1:]:
        a, b = move(a, b)
    va, vb, c, d = stack([a.job(), b.job(), second.job(0, wide), second.job(wide, wide)])
    a, b = a.after(va), b.after(vb)
    pieces0 = layout.pieces([(a, cut), (b, cut)], (width, 3 * half))
    c, d = second.after(c), second.after(d, zyx)
    spots = vector_places(vectors, high)
    used = max(r for r, _ in spots) + 1
    both = [v.reshape(-1, groups, high, v.shape[-1])[:, :, :used, cut:].astype(F32) for v in pieces0.buffers[-2:]]
    small = jnp.stack([jnp.where(core == k, both[0], both[1]) for k in range(2)], axis=1).reshape(devices, used, lanes)
    vec = jnp.stack([small[:, r, l : l + each].reshape(width) for r, l in spots[:-1]])
    r, l = spots[-1]
    whole_binner = small[:, r, l : l + b_inner.shape[0]].reshape(1, -1)
    row, col = segment_ids.reshape(seqs, 1, length), segment_ids.reshape(seqs, length, 1)

    (qkv0, wqkv0), (last,) = project(pieces0, tokens, vec, 0, carry=[last])
    last = Chain(layout, last, zxy)
    while c.order[1:]:
        c, d = move(c, d)
    o0, ot0, probs0, share0 = attend(qkv0, row, col)
    c_value, d_value, e, f = stack([c.job(), d.job(), last.job(0, half), last.job(half, half)])
    c, d = c.after(c_value), d.after(d_value)
    pieces1 = layout.pieces([(c, wide), (d, wide)], (width, 3 * half + width))
    e, f = last.after(e), last.after(f, zyx)
    qkv1, wqkv1 = project(pieces1.part(0, 3 * half), tokens, vec, 1)
    o1, ot1, probs1, share1 = attend(qkv1, row, col)
    while len(e.order) > 1:
        e, f = move(e, f)
    n1, rstd1, h, ht, whole_wout = join(pieces1.part(3 * half, width), o0, o1, tokens, vec)
    made = inner(h, whole_winner, whole_binner, 0, 2)
    e, f = move(e, f)
    pieces2 = layout.pieces([(e, half), (f, half)], (w_outer.shape[0] * devices, width))
    u, slope = inner(h, whole_winner, whole_binner, 1, 2, made)
    out, dz2, dm, dmt, sums2, whole_wouter = outer(pieces2, u, n1, cotangent, vec)

    def reduction(other, own, *orders, by_rows=False, runs=None):
        came = layout.send(other, layout.core)
        rows, cols = own.shape[2:]
        if by_rows:
            parts = [((i, 0), (rows // len(orders), cols)) for i in range(len(orders))]
        else:
            runs = runs or [(i * cols // len(orders), cols // len(orders)) for i in range(len(orders))]
            parts = [((0, start // size), (rows, size)) for start, size in runs]
        return [Reduction(layout, [(own,) + part, (came,) + part], order) for part, order in zip(parts, orders)]

    def along_z(reductions, carry=()):
        sums = add_up([[t.reshape(-1, t.shape[-1]) for t in r.last()] for r in reductions], carry)
        sums, carry = sums if carry else (sums, ())
        sums = lax.psum_scatter(sums, ("replica", "group"), scatter_dimension=0, axis_index_groups=layout.along(z_digit[0]), tiled=True)
        return [sums] + list(carry)

    def across_z(reductions, carry=()):
        made = gather_sums(layout.place(z_digit[0]).astype(jnp.int32).reshape(1), [r.last() for r in reductions], carry)
        made, carry = made if carry else (made, ())
        return [[made[-1]] + [layout.send(s, z_digit[0], k + 1) for k, s in enumerate(made[:-1])]] + list(carry)

    spread = lambda block: lax.all_gather(block, "replica", axis=0, tiled=False)
    middle = range(len(xyz) - 2)
    cols = 3 * half // 4
    other = outer_grad(theirs, dmt, u, groups)
    own = outer_grad(mine, dmt, u, groups)
    outers = reduction(other, own, xyz, yxz, by_rows=True)
    step(*outers)
    other, own, dh, sum_inner = inner_back(halves, dm, whole_wouter, slope, ht, whole_winner, groups)
    for _ in middle:
        (other,) = step(*outers, carry=[other])
    inners = reduction(other, own, xyz, yxz)
    dz1, da, do, sums1 = join_back(dz2, dh, n1, rstd1, vec, whole_wout)
    (got_wouter,) = along_z(outers)
    step(*inners)
    d0, sq0, sv0 = attend_back(qkv0, ot0, probs0, share0, do, 0)
    other, own = token_weights_grad(halves, xt, d0, groups, mixed=(ot0, ot1, da))
    for _ in middle:
        (other,) = step(*inners, carry=[other])
    firsts = reduction(other, own, xyz, yxz, runs=((0, cols), (other.shape[3] - width // 4, width // 4)))
    d1, sq1, sv1 = attend_back(qkv1, ot1, probs1, share1, do, 1)
    (got_winner,) = along_z(inners)
    step(*firsts)
    partial = token_grad(dz1, d0, wqkv0, F32)
    vectors = [((sq0, sq1), 0), ((sv0, sv1), 0)] + [((sums,), i) for sums in (sums1, sums2) for i in range(3)] + [((sum_inner,), 0)]
    (other, own), (got_wouter,) = token_weights_grad(halves, xt, d1, groups, vectors=vectors, carry=[got_wouter])
    got_wouter = spread(got_wouter)
    for _ in middle:
        (other,) = step(*firsts, carry=[other])
    seconds = reduction(other, own, xyz, yxz, runs=((0, 2 * cols // 3), (2 * cols // 3, cols // 3)))
    cores = layout.core[2]
    order = [r % cores * (layout.replicas // cores) + r // cores for r in range(layout.replicas)]
    step(*seconds)
    (first_sums,) = across_z(firsts)
    grad_tokens = token_grad(partial, d1, wqkv1, BF16)
    for _ in middle:
        (got_winner,) = step(*seconds, carry=[got_winner])
    got_winner = spread(got_winner)
    (second_sums,) = across_z(seconds)
    grad_wouter = outer_result(got_wouter, order)
    got = [add_up([first_sums, second_sums])]
    places = jnp.zeros((1,), jnp.int32)
    weight = 1
    for digit in layout.over[::-1] + [layout.core]:
        own = layout.place(digit).astype(jnp.int32)
        places = jnp.concatenate([places + own * weight, places + (1 - own) * weight])
        got = got + [layout.send(g, digit) for g in got]
        weight *= digit[2]
    grad_winner = inner_result(got_winner, order)
    keep = width // groups
    wq, wk, wv, grad_wout, sums = token_weights_result(got, places, keep, half // 4, width // 4)
    bq, bv, bout, gain1, shift1, bouter, gain2, shift2 = (sums[i, :keep] for i in range(8))
    binner = sums[8 : 8 + hidden // width, :keep].reshape(-1)
    return (out, grad_tokens, wq, bq, wk, wv, bv, grad_wout, bout, gain1, shift1, grad_winner, binner, grad_wouter, bouter, gain2, shift2)


def solution(mesh):
    layout = Layout(mesh)
    both = ("replica", "group")
    rows, vector = P(both, None), P(both)
    in_specs = (rows, rows, rows, vector, rows, rows, vector, rows, vector, vector, vector, rows, vector, rows, vector, vector, vector, rows)
    kept, kept_vector = P("group", None), P("group")
    out_specs = (rows, rows, kept, kept_vector, kept, kept, kept_vector, kept, kept_vector, kept_vector, kept_vector, kept, kept_vector, kept, kept_vector, kept_vector, kept_vector)
    return jax.shard_map(functools.partial(local, layout), mesh=mesh, in_specs=in_specs, out_specs=out_specs, check_vma=False)
```

```python
import functools
import math

import jax
import jax.numpy as jnp
from jax import lax
from jax.experimental import pallas as pl
from jax.experimental.pallas import tpu as pltpu
from jax.sharding import PartitionSpec as P

F32 = jnp.float32
BF16 = jnp.bfloat16
VMEM_LIMIT = 46 * 1024 * 1024
ANY = pl.BlockSpec(memory_space=pl.ANY)
ALL_VMEM = 62 * 1024 * 1024
HBM = pl.BlockSpec(memory_space=pltpu.HBM)
BQ, BV, BOUT, GAIN1, SHIFT1, BOUTER, GAIN2, SHIFT2 = range(8)


LAST = []


def call(kernel, name, operands, in_specs, out_shape, out_specs, *, grid=(1,), scalars=(), after=(), carry=(), into=(), scratch=(), time=0, room=None):
    single = not isinstance(out_shape, (tuple, list))
    shapes, specs = ([out_shape], [out_specs]) if single else (list(out_shape), list(out_specs))
    first, made = len(scalars) + len(operands), len(shapes)
    ends = made + len(carry)
    unread = list(carry) + list(into) + list(after) + LAST

    limit = VMEM_LIMIT
    if room is not None:
        pairs = list(zip(specs, shapes)) + list(zip(in_specs, operands))
        blocks = [math.prod(spec.block_shape) * array.dtype.itemsize for spec, array in pairs if spec.block_shape is not None]
        limit = ALL_VMEM if room < 0 else min(VMEM_LIMIT, 2 * sum(blocks) + room)

    def body(*refs):
        outs = first + len(unread)
        kernel(*refs[:first], *refs[outs : outs + made], *refs[outs + ends + 1 :])

    outs = pl.pallas_call(
        body,
        out_shape=shapes + [jax.ShapeDtypeStruct(c.shape, c.dtype) for c in carry] + [jax.ShapeDtypeStruct((8, 128), F32)],
        grid_spec=pltpu.PrefetchScalarGridSpec(
            num_scalar_prefetch=len(scalars),
            grid=grid,
            in_specs=list(in_specs) + [HBM] * len(carry) + [ANY] * (len(unread) - len(carry) - len(LAST)) + [HBM] * len(LAST),
            out_specs=specs + [HBM] * (len(carry) + 1),
            scratch_shapes=list(scratch),
        ),
        input_output_aliases={first + i: made + i for i in range(len(carry))} | {first + len(carry) + i: i for i in range(len(into))},
        compiler_params=pltpu.CompilerParams(dimension_semantics=("arbitrary",) * len(grid), vmem_limit_bytes=limit),
        cost_estimate=pl.CostEstimate(flops=int(1 + time * 1e9), bytes_accessed=int(1 + time * 1e6), transcendentals=0),
        name=name,
    )(*scalars, *operands, *unread)
    LAST[:] = outs[ends:]
    result = outs[0] if single else tuple(outs[:made])
    return (result, outs[made:ends]) if carry else result


def like(shape, dtype=BF16):
    return jax.ShapeDtypeStruct(shape, dtype)


def dot(left, right):
    return lax.dot_general(left, right, (((1,), (0,)), ((), ())), preferred_element_type=F32)


def dot_nt(left, right):
    return lax.dot_general(left, right, (((1,), (1,)), ((), ())), preferred_element_type=F32)


def whole(shape):
    return pl.BlockSpec(shape, lambda *i: (0,) * len(shape))


def column_sum(value):
    return jnp.sum(value.astype(F32), axis=0, keepdims=True)


def pack(operands, makes, vectors=()):
    lanes = 128 if vectors else 0

    def kernel(*refs):
        outs = refs[len(operands) + len(vectors) :]
        for out_ref, pieces in zip(outs, makes):
            at = 0
            for which, start, size in pieces:
                out_ref[:, at : at + size] = refs[which][:, start : start + size]
                at += size
        if vectors:
            rows, cols = outs[0].shape
            outs[0][:, cols - lanes :] = jnp.zeros((rows, lanes), BF16)
            for ref, (row, lane) in zip(refs[len(operands) :], vector_places(vectors, rows)):
                size = ref.shape[0]
                start = cols - lanes + lane
                outs[0][row : row + 1, start : start + size] = ref[...].astype(F32).reshape(1, size).astype(BF16)

    shapes = [(operands[pieces[0][0]].shape[0], sum(p[2] for p in pieces)) for pieces in makes]
    if vectors:
        shapes[0] = (shapes[0][0], shapes[0][1] + lanes)
    everything = list(operands) + list(vectors)
    return call(kernel, "pack", everything, [whole(o.shape) for o in everything], [like(s) for s in shapes], [whole(s) for s in shapes], room=-1)


def vector_places(vectors, rows):
    size = vectors[0].shape[0]
    places = [(i % rows, i // rows * size) for i in range(len(vectors) - 1)]
    return places + [(8, 0) if rows > 8 else (0, 64)]


def stack(jobs, carry=()):
    flat = [array for arrays, *_ in jobs for array in arrays]
    shapes = []
    for arrays, _, axis, _, cols in jobs:
        shape = arrays[0].shape
        shapes.append(shape[:axis] + (len(arrays),) + shape[axis:-1] + (cols,))

    def kernel(*refs):
        place_refs, refs = refs[: len(jobs)], refs[len(jobs) :]
        ins, outs, arrived = refs[: len(flat)], refs[len(flat) : -1], refs[-1]
        copies = []
        for (arrays, _, axis, first, cols), place_ref, out_ref in zip(jobs, place_refs, outs):
            count = len(arrays)
            for k in range(count):
                ref = ins[len(copies)]
                source = ref.at[(slice(None),) * (len(ref.shape) - 1) + (pl.ds(first, cols),)]
                target = out_ref.at[(slice(None),) * axis + (lax.rem(place_ref[0] + count - k, count),)]
                copies.append(pltpu.make_async_copy(source, target, arrived.at[len(copies)]))
        for copy in copies:
            copy.start()
        for copy in copies:
            copy.wait()

    return call(
        kernel,
        "stack",
        flat,
        [ANY] * len(flat),
        [like(shape) for shape in shapes],
        [whole(shape) for shape in shapes],
        scalars=[job[1] for job in jobs],
        carry=carry,
        scratch=[pltpu.SemaphoreType.DMA((len(flat),))],
        room=4 << 20,
    )


def combine(jobs, carry=(), after=()):
    n = jobs[0][1][0][0].shape[1]
    sizes = []
    for _, terms in jobs:
        before, _, behind, _, _ = terms[0][0].shape
        sizes.append((before, behind) + terms[0][2])
    flat = [t for _, terms in jobs for t in terms]

    def kernel(*refs):
        refs = refs[len(jobs) :]
        outs = refs[len(flat) :]
        i = 0
        for job, (_, terms) in enumerate(jobs):
            total = refs[i][:, 0].astype(F32)
            for ref in refs[i + 1 : i + len(terms)]:
                total = total + ref[:, 0].astype(F32)
            total = total.astype(BF16)
            i += len(terms)
            for j, out_ref in enumerate(outs[job * n : (job + 1) * n]):

                @pl.when(pl.program_id(0) == j)
                def _():
                    out_ref[...] = total

    def at(job, block):
        before, behind, rows, cols = sizes[job]
        return pl.BlockSpec((before, 1, behind, rows, cols), lambda i, *own: (0, lax.rem(own[job][0] + i + 1, n), 0) + block)

    made = call(
        kernel,
        "combine",
        [t[0] for t in flat],
        [at(job, t[1]) for job, (_, terms) in enumerate(jobs) for t in terms],
        [like(size) for size in sizes for _ in range(n)],
        [whole(size) for size in sizes for _ in range(n)],
        grid=(n,),
        scalars=[own for own, _ in jobs],
        carry=carry,
        after=after,
        room=12 << 20,
    )
    made, carried = made if carry else (made, ())
    return [made[job * n : (job + 1) * n] for job in range(len(jobs))], carried


def gather_sums(own, lists, carry=()):
    flat = [t for terms in lists for t in terms]
    n = flat[0].shape[0]
    rows = max(t.shape[1] for t in flat)
    cols = sum(terms[0].shape[2] for terms in lists)

    def kernel(own_ref, *refs):
        outs = refs[len(flat) :]
        parts, i = [], 0
        for terms in lists:
            total = refs[i][0].astype(F32)
            for ref in refs[i + 1 : i + len(terms)]:
                total = total + ref[0].astype(F32)
            parts.append(total.astype(BF16))
            i += len(terms)
        for j, out_ref in enumerate(outs):

            @pl.when(pl.program_id(0) == j)
            def _():
                at = 0
                for part in parts:
                    high, wide = part.shape
                    out_ref[:high, at : at + wide] = part
                    if high < rows:
                        out_ref[high:, at : at + wide] = jnp.zeros((rows - high, wide), BF16)
                    at += wide

    return call(
        kernel,
        "gather_sums",
        flat,
        [pl.BlockSpec((1,) + t.shape[1:], lambda i, own: (lax.rem(own[0] + i + 1, n), 0, 0)) for t in flat],
        [like((rows, cols))] * n,
        [whole((rows, cols))] * n,
        grid=(n,),
        scalars=[own],
        carry=carry,
        room=6 << 20,
    )


def add_up(lists, carry=()):
    flat = [a for arrays in lists for a in arrays]

    def kernel(*refs):
        at, i = 0, 0
        for arrays in lists:
            total = refs[i][...].astype(F32)
            for ref in refs[i + 1 : i + len(arrays)]:
                total = total + ref[...].astype(F32)
            rows, cols = total.shape
            refs[-1][:rows, at : at + cols] = total.astype(BF16)
            if rows < refs[-1].shape[0]:
                refs[-1][rows:, at : at + cols] = jnp.zeros((refs[-1].shape[0] - rows, cols), BF16)
            at += cols
            i += len(arrays)

    shape = (max(a.shape[0] for a in flat), sum(arrays[0].shape[1] for arrays in lists))
    return call(kernel, "add_up", flat, [whole(a.shape) for a in flat], like(shape), whole(shape), carry=carry, room=12 << 20)


def outer_result(got, order, runs=2):
    count, cols, rows = got.shape
    rows //= runs

    def kernel(got_ref, out_ref):
        for i, j in enumerate(order):
            for run in range(runs):
                at = (j * runs + run) * cols
                out_ref[:, at : at + cols] = got_ref[i, :, run * rows : (run + 1) * rows].astype(F32).T

    shape = (rows, count * runs * cols)
    return call(kernel, "outer_result", [got], [whole(got.shape)], like(shape, F32), whole(shape), room=8 << 20)


def inner_result(got, order):
    count, rows, cols = got.shape

    def kernel(got_ref, out_ref):
        for i, j in enumerate(order):
            out_ref[:, j * cols : (j + 1) * cols] = got_ref[i].astype(F32)

    shape = (rows, count * cols)
    return call(kernel, "inner_result", [got], [whole(got.shape)], like(shape, F32), whole(shape), room=8 << 20)


def token_weights_result(pieces, places, keep, size, last):
    count = len(pieces)
    rows = pieces[0].shape[0]
    second = 3 * size + last

    def kernel(place_ref, *refs):
        outs = refs[count:]
        for i in range(count):
            at = lambda j, wide: pl.ds(pl.multiple_of(j * wide, wide), wide)
            piece = refs[i][:keep].astype(F32)
            for which in range(3):
                outs[which][:, at(place_ref[i], size)] = piece[:, which * size : (which + 1) * size]
                outs[which][:, at(count + place_ref[i], size)] = piece[:, second + which * size : second + (which + 1) * size]
            outs[3][:, at(place_ref[i], last)] = piece[:, 3 * size : second]
        outs[4][...] = refs[0][keep:, second:].astype(F32)

    shapes = [(keep, 2 * count * size)] * 3 + [(keep, count * last), (rows - keep, 3 * size)]
    return call(
        kernel,
        "token_weights_result",
        pieces,
        [whole(p.shape) for p in pieces],
        [like(s, F32) for s in shapes],
        [whole(s) for s in shapes],
        scalars=[places],
        room=8 << 20,
    )


def transposed(x, tile=256):
    rows, cols = x.shape

    def kernel(x_ref, out_ref):
        out_ref[...] = x_ref[...].T

    return call(
        kernel,
        "transposed",
        [x],
        [pl.BlockSpec((tile, cols), lambda i: (i, 0))],
        like((cols, rows)),
        pl.BlockSpec((cols, tile), lambda i: (0, i)),
        grid=(rows // tile,),
        time=3,
    )


class Pieces:
    def __init__(self, cores, buffers, spans, shape):
        self.cores, self.buffers, self.spans, self.shape = cores, buffers, spans, shape
        self.count = sum(b.shape[0] for b in buffers)

    def part(self, start, cols):
        kept = []
        for buffer, (first, size, to) in zip(self.buffers, self.spans):
            low, high = max(to, start), min(to + size, start + cols)
            kept.append((buffer, (first + low - to, high - low, low - start)))
        buffers, spans = zip(*(k for k in kept if k[1][1] > 0))
        return Pieces(self.cores, list(buffers), list(spans), (self.shape[0], cols))

    def scratch(self):
        return [pltpu.VMEM(self.shape, BF16), pltpu.SemaphoreType.DMA((self.count,)), pltpu.SemaphoreType.DMA]

    def fetch(self, cores_ref, refs, held, arrived):
        copies = []
        for i, (ref, (first, cols, to)) in enumerate(zip(refs, self.spans)):
            blocks, rows, _ = ref.shape
            for j in range(blocks):
                target = held.at[pl.ds(pl.multiple_of((2 * j + cores_ref[i % 2]) * rows, rows), rows), pl.ds(to, cols)]
                copies.append(pltpu.make_async_copy(ref.at[j, :, pl.ds(first, cols)], target, arrived.at[len(copies)]))
        for copy in copies:
            copy.start()
        for copy in copies:
            copy.wait()


def project(pieces, x, vec, half, carry=()):
    rows, depth = x.shape
    cols = pieces.shape[1]
    tile = cols // 3
    count = len(pieces.buffers)

    def kernel(*refs):
        (cores_ref,), (x_ref, vec_ref), refs = refs[:1], refs[1 : 3], refs[3:]
        buffer_refs, (out_ref, whole_ref, held, arrived, left) = refs[:count], refs[count:]
        step = pl.program_id(0)
        write = pltpu.make_async_copy(held, whole_ref, left)

        @pl.when(step == 0)
        def _():
            pieces.fetch(cores_ref, buffer_refs, held, arrived)
            write.start()

        at = slice(half * tile, (half + 1) * tile)
        for i, row in enumerate((BQ, None, BV)):

            @pl.when(step == i)
            def _():
                made = dot(x_ref[...], held[:, i * tile : (i + 1) * tile])
                out_ref[...] = (made if row is None else made + vec_ref[row : row + 1, at]).astype(BF16)

        @pl.when(step == 2)
        def _():
            write.wait()

    return call(
        kernel,
        "project",
        [x, vec] + list(pieces.buffers),
        [whole(x.shape), whole(vec.shape)] + [ANY] * count,
        (like((rows, cols)), like((depth, cols))),
        (pl.BlockSpec((rows, tile), lambda i, *_: (0, i)), HBM),
        grid=(3,),
        scalars=[pieces.cores],
        scratch=pieces.scratch(),
        carry=carry,
        time=6,
    )


def attend(qkv, row, col, heads=4, size=64, carry=()):
    seqs, _, length = row.shape
    width = qkv.shape[1] // 3
    block = heads * size
    blocks = width // block

    def kernel(q_ref, k_ref, v_ref, row_ref, col_ref, o_ref, ot_ref, p_ref, r_ref, bias_ref):
        @pl.when(pl.program_id(1) == 0)
        def _():
            bias_ref[...] = jnp.where(col_ref[0] == row_ref[0], 0.0, -1e9).astype(F32)

        qt = (q_ref[...] * jnp.asarray(0.125, BF16)).T
        vt = v_ref[...].T
        zero = jnp.zeros((size, length), BF16)
        for head in range(heads):
            here = slice(head * size, (head + 1) * size)
            pair = slice(head // 2 * 2 * size, (head // 2 + 1) * 2 * size)
            own = [qt[here], zero] if head % 2 == 0 else [zero, qt[here]]
            scores = dot(k_ref[:, pair], jnp.concatenate(own, axis=0)) + bias_ref[...]
            expo = jnp.exp(scores - jnp.max(scores, axis=0, keepdims=True))
            share = 1.0 / jnp.sum(expo, axis=0, keepdims=True)
            expo = expo.astype(BF16)
            p_ref[0, head] = expo
            r_ref[0, 0, head : head + 1] = share
            ot_ref[here, :] = (dot(vt[here], expo) * share).astype(BF16)
        o_ref[...] = ot_ref[...].T

    spec = lambda part: pl.BlockSpec((length, block), lambda s, p: (s, part * blocks + p))
    return call(
        kernel,
        "attend",
        [qkv, qkv, qkv, row, col],
        [spec(0), spec(1), spec(2), pl.BlockSpec((1, 1, length), lambda s, p: (s, 0, 0)), pl.BlockSpec((1, length, 1), lambda s, p: (s, 0, 0))],
        (like((seqs * length, width)), like((width, seqs * length)), like((seqs, heads * blocks, length, length)), like((seqs, blocks, heads, length), F32)),
        (
            pl.BlockSpec((length, block), lambda s, p: (s, p)),
            pl.BlockSpec((block, length), lambda s, p: (p, s)),
            pl.BlockSpec((1, heads, length, length), lambda s, p: (s, p, 0, 0)),
            pl.BlockSpec((1, 1, heads, length), lambda s, p: (s, p, 0, 0)),
        ),
        grid=(seqs, blocks),
        scratch=[pltpu.VMEM((length, length), F32)],
        carry=carry,
        time=11,
    )


def attend_back(qkv, ot, probs, share, do, part, carry=()):
    seqs, blocks, heads, length = share.shape
    tokens, width = ot.shape[1], ot.shape[0]
    block = width // blocks
    size = block // heads

    def kernel(q_ref, k_ref, v_ref, ot_ref, p_ref, r_ref, do_ref, d_ref, bq_ref, bv_ref):
        dot_t = do_ref[...].T.astype(F32)
        shares = jnp.concatenate([jnp.broadcast_to(r_ref[0, 0, h : h + 1], (size, length)) for h in range(heads)], axis=0)
        dot_t = (dot_t * shares).astype(BF16)
        do = dot_t.T
        kt = k_ref[...].T
        product = dot_t.astype(F32) * ot_ref[...].astype(F32)
        zero = jnp.zeros((size, length), BF16)
        first = lax.broadcasted_iota(jnp.int32, (1, 2 * size), 1) < size
        dk, dv, dqt = [], [], []
        for head in range(heads):
            here = slice(head * size, (head + 1) * size)
            pair = slice(head // 2 * 2 * size, (head // 2 + 1) * 2 * size)
            delta = jnp.sum(product[here], axis=0, keepdims=True)
            own = [dot_t[here], zero] if head % 2 == 0 else [zero, dot_t[here]]
            expo = p_ref[0, head]
            ds = (expo.astype(F32) * (dot(v_ref[:, pair], jnp.concatenate(own, axis=0)) - delta)).astype(BF16)
            dv.append(dot(expo, do[:, pair]))
            dk.append(dot(ds, q_ref[:, pair]))
            dqt.append(dot(kt[here], ds))
        paired = lambda parts: jnp.concatenate([jnp.where(first, parts[i], parts[i + 1]) for i in range(0, heads, 2)], axis=1)
        dq = (jnp.concatenate(dqt, axis=0) * 0.125).astype(BF16).T
        dv = paired(dv).astype(BF16)
        d_ref[0] = dq
        d_ref[1] = (paired(dk) * 0.125).astype(BF16)
        d_ref[2] = dv
        bq_ref[0] = column_sum(dq)
        bv_ref[0] = column_sum(dv)

    spec = lambda which: pl.BlockSpec((length, block), lambda s, p: (s, which * blocks + p))
    sums = pl.BlockSpec((1, 1, block), lambda s, p: (s, 0, p))
    return call(
        kernel,
        "attend_back",
        [qkv, qkv, qkv, ot, probs, share, do],
        [
            spec(0),
            spec(1),
            spec(2),
            pl.BlockSpec((block, length), lambda s, p: (p, s)),
            pl.BlockSpec((1, heads, length, length), lambda s, p: (s, p, 0, 0)),
            pl.BlockSpec((1, 1, heads, length), lambda s, p: (s, p, 0, 0)),
            spec(part),
        ],
        (like((3, tokens, width)), like((seqs, 1, width), F32), like((seqs, 1, width), F32)),
        (pl.BlockSpec((3, length, block), lambda s, p: (0, s, p)), sums, sums),
        grid=(seqs, blocks),
        carry=carry,
        time=11,
    )


def normed(z):
    center = z - jnp.mean(z, axis=-1, keepdims=True)
    rstd = lax.rsqrt(jnp.mean(center * center, axis=-1, keepdims=True) + 1e-06)
    return center * rstd, rstd


def norm_back(dn, n, rstd):
    return rstd * (dn - jnp.mean(dn, axis=-1, keepdims=True) - n * jnp.mean(dn * n, axis=-1, keepdims=True))


def join(pieces, o0, o1, x, vec, tile=256, after=()):
    rows, width = x.shape
    count = len(pieces.buffers)

    def kernel(*refs):
        (cores_ref,), (o0_ref, o1_ref, x_ref, vec_ref), refs = refs[:1], refs[1 : 5], refs[5:]
        buffer_refs, (n_ref, r_ref, h_ref, ht_ref, whole_ref, held, arrived, left) = refs[:count], refs[count:]
        write = pltpu.make_async_copy(held, whole_ref, left)

        @pl.when(pl.program_id(0) == 0)
        def _():
            pieces.fetch(cores_ref, buffer_refs, held, arrived)
            write.start()

        half = o0_ref.shape[1]
        mixed = dot(o0_ref[...], held[:half]) + dot(o1_ref[...], held[half:])
        z = x_ref[...].astype(F32) + (mixed + vec_ref[BOUT : BOUT + 1])
        n, rstd = normed(z)
        n_ref[...] = n
        r_ref[...] = rstd
        h = (n * vec_ref[GAIN1 : GAIN1 + 1] + vec_ref[SHIFT1 : SHIFT1 + 1]).astype(BF16)
        h_ref[...] = h
        ht_ref[...] = h.T

        @pl.when(pl.program_id(0) == pl.num_programs(0) - 1)
        def _():
            write.wait()

    tok = pl.BlockSpec((tile, width), lambda i, *_: (i, 0))
    half = pl.BlockSpec((tile, width // 2), lambda i, *_: (i, 0))
    return call(
        kernel,
        "join",
        [o0, o1, x, vec] + list(pieces.buffers),
        [half, half, tok, whole(vec.shape)] + [ANY] * count,
        (like((rows, width), F32), like((rows, 1), F32), like((rows, width)), like((width, rows)), like((width, width))),
        (tok, pl.BlockSpec((tile, 1), lambda i, *_: (i, 0)), tok, pl.BlockSpec((width, tile), lambda i, *_: (0, i)), HBM),
        grid=(rows // tile,),
        scalars=[pieces.cores],
        scratch=pieces.scratch(),
        after=after,
        time=7,
    )


def inner(h, rest, bias, run=0, runs=1, into=(), tile=512):
    rows, depth = h.shape
    cols = bias.shape[1]
    steps = cols // tile // runs

    def kernel(h_ref, w_ref, b_ref, u_ref, g_ref):
        f = dot(h_ref[...], w_ref[...]) + b_ref[...]
        weight = 0.5 + 0.5 * lax.erf(f * math.sqrt(0.5))
        u_ref[...] = (f * weight).astype(BF16)
        bell = jnp.exp2((f * f) * (-0.5 * math.log2(math.e)))
        g_ref[...] = (weight + (f * (1.0 / math.sqrt(2.0 * math.pi))) * bell).astype(BF16)

    at = lambda i: (0, run * steps + i)
    out = pl.BlockSpec((rows, tile), at)
    return call(
        kernel,
        "inner",
        [h, rest, bias],
        [whole(h.shape), pl.BlockSpec((depth, tile), at), pl.BlockSpec((1, tile), at)],
        (like((rows, cols)), like((rows, cols))),
        (out, out),
        grid=(steps,),
        into=into,
        time=9,
    )


def outer(pieces, u, n1, cot, vec, tile=256, after=()):
    rows, depth = u.shape
    width = n1.shape[1]
    count = len(pieces.buffers)

    def kernel(*refs):
        (cores_ref,), (u_ref, n_ref, c_ref, vec_ref), refs = refs[:1], refs[1 : 5], refs[5:]
        buffer_refs, (out_ref, dz_ref, dm_ref, dmt_ref, sums_ref, whole_ref, held, arrived, left) = refs[:count], refs[count:]
        write = pltpu.make_async_copy(held, whole_ref, left)

        @pl.when(pl.program_id(0) == 0)
        def _():
            sums_ref[...] = jnp.zeros_like(sums_ref)
            pieces.fetch(cores_ref, buffer_refs, held, arrived)
            write.start()

        row = lambda i: vec_ref[i : i + 1]
        z = (n_ref[...] * row(GAIN1) + row(SHIFT1)) + (dot(u_ref[...], held[...]) + row(BOUTER))
        n, rstd = normed(z)
        out_ref[...] = (n * row(GAIN2) + row(SHIFT2)).astype(BF16)
        c = c_ref[...].astype(F32)
        dz = norm_back(c * row(GAIN2), n, rstd)
        dz_ref[...] = dz
        dm = dz.astype(BF16)
        dm_ref[...] = dm
        dmt_ref[...] = dm.T
        sums_ref[0:1, :] += column_sum(dm)
        sums_ref[1:2, :] += column_sum(c * n)
        sums_ref[2:3, :] += column_sum(c)

        @pl.when(pl.program_id(0) == pl.num_programs(0) - 1)
        def _():
            write.wait()

    tok = pl.BlockSpec((tile, width), lambda i, *_: (i, 0))
    return call(
        kernel,
        "outer",
        [u, n1, cot, vec] + list(pieces.buffers),
        [pl.BlockSpec((tile, depth), lambda i, *_: (i, 0)), tok, tok, whole(vec.shape)] + [ANY] * count,
        (like((rows, width)), like((rows, width), F32), like((rows, width)), like((width, rows)), like((8, width), F32), like((depth, width))),
        (tok, tok, tok, pl.BlockSpec((width, tile), lambda i, *_: (0, i)), whole((8, width)), HBM),
        grid=(rows // tile,),
        scalars=[pieces.cores],
        scratch=pieces.scratch(),
        after=after,
        time=19,
    )


def outer_grad(half, dmt, u, groups, after=()):
    width, rows = dmt.shape
    cols = u.shape[1]
    part = cols // groups
    blocks = 2048 // part

    def kernel(half_ref, left_ref, right_ref, out_ref):
        made = dot(left_ref[...], right_ref[...]).astype(BF16)
        for i in range(blocks):
            out_ref[:, i] = made[:, i * part : (i + 1) * part].reshape(2, width // 4, part)

    return call(
        kernel,
        "outer_grad",
        [dmt, u],
        [pl.BlockSpec((width // 2, rows), lambda i, half: (half[0], 0)), pl.BlockSpec((rows, blocks * part), lambda i, half: (0, i))],
        like((2, groups, width // 4, part)),
        pl.BlockSpec((2, blocks, width // 4, part), lambda i, half: (0, i, 0, 0)),
        grid=(groups // blocks,),
        scalars=[half],
        after=after,
        time=6,
    )


def inner_back(halves, dm, w2, slope, ht, w1, groups, tile=512, after=()):
    rows, width = dm.shape
    cols = slope.shape[1]
    steps = cols // 2 // tile
    per = steps // 2

    def kernel(halves_ref, dm_ref, w2_ref, g_ref, ht_ref, w1_ref, first_ref, second_ref, dh_ref, sum_ref):
        step = pl.program_id(0)

        @pl.when(step == 0)
        def _():
            dh_ref[...] = jnp.zeros_like(dh_ref)

        df = (dot_nt(dm_ref[...], w2_ref[...]) * g_ref[...].astype(F32)).astype(BF16)
        sum_ref[...] = column_sum(df)
        made = dot(ht_ref[...], df).astype(BF16).reshape(first_ref.shape)

        @pl.when(step < steps)
        def _():
            first_ref[...] = made

        @pl.when(step >= steps)
        def _():
            second_ref[...] = made

        dh_ref[...] += dot_nt(df, w1_ref[...])

    at = lambda i, halves: halves[i // steps] * steps + i % steps
    grad = like((2, groups, width // groups, cols // 4))
    block = (1, groups, width // groups, tile)
    kept = lambda step: (step // per, 0, 0, step % per)
    return call(
        kernel,
        "inner_back",
        [dm, w2, slope, ht, w1],
        [
            whole(dm.shape),
            pl.BlockSpec((tile, width), lambda i, halves: (at(i, halves), 0)),
            pl.BlockSpec((rows, tile), lambda i, halves: (0, at(i, halves))),
            whole(ht.shape),
            pl.BlockSpec((width, tile), lambda i, halves: (0, at(i, halves))),
        ],
        (grad, grad, like((rows, width), F32), like((1, cols), F32)),
        (
            pl.BlockSpec(block, lambda i, halves: kept(jnp.minimum(i, steps - 1))),
            pl.BlockSpec(block, lambda i, halves: kept(jnp.maximum(i - steps, 0))),
            whole((rows, width)),
            pl.BlockSpec((1, tile), lambda i, halves: (0, at(i, halves))),
        ),
        grid=(2 * steps,),
        scalars=[halves],
        after=after,
        time=35,
    )


def join_back(dz2, dh, n1, rstd, vec, w, tile=256, after=()):
    rows, width = dz2.shape

    def kernel(dz2_ref, dh_ref, n_ref, r_ref, vec_ref, w_ref, dz_ref, da_ref, do_ref, sums_ref):
        @pl.when(pl.program_id(0) == 0)
        def _():
            sums_ref[...] = jnp.zeros_like(sums_ref)

        dh = dz2_ref[...] + dh_ref[...]
        n = n_ref[...]
        dz = norm_back(dh * vec_ref[GAIN1 : GAIN1 + 1], n, r_ref[...])
        dz_ref[...] = dz
        da = dz.astype(BF16)
        da_ref[...] = da
        do_ref[...] = dot_nt(da, w_ref[...]).astype(BF16)
        sums_ref[0:1, :] += column_sum(da)
        sums_ref[1:2, :] += column_sum(dh * n)
        sums_ref[2:3, :] += column_sum(dh)

    tok = pl.BlockSpec((tile, width), lambda i: (i, 0))
    return call(
        kernel,
        "join_back",
        [dz2, dh, n1, rstd, vec, w],
        [tok, tok, tok, pl.BlockSpec((tile, 1), lambda i: (i, 0)), whole(vec.shape), whole(w.shape)],
        (like((rows, width), F32), like((rows, width)), like((rows, width)), like((8, width), F32)),
        (tok, tok, tok, whole((8, width))),
        grid=(rows // tile,),
        after=after,
        time=8,
    )


def token_weights_grad(halves, xt, d, groups, mixed=None, vectors=(), carry=()):
    width, rows = xt.shape
    part = d.shape[2] // 2
    size, last = part // 2, width // 4
    keep = width // groups
    mixed_at = -(-3 * size // last) * last
    cols = mixed_at + last if mixed else 3 * size
    more = 16 if vectors else 0
    arrays = [a for group, _ in vectors for a in group]

    def kernel(halves_ref, left_ref, d_ref, *refs):
        def put(out_ref):
            at, read = keep, list(refs)
            for group, row in vectors:
                here, read = read[: len(group)], read[len(group) :]
                values = [jnp.sum(ref[...], axis=0) if len(ref.shape) == 3 else ref[row : row + 1] for ref in here]
                wide = values[0].shape[1]
                many = wide * len(group) // groups
                for g in range(groups):
                    for i in range(many // keep):
                        start = g * many + i * keep
                        piece = values[start // wide][:, start % wide : start % wide + keep].astype(BF16)
                        for x in range(2):
                            out_ref[x, g, at + i : at + i + 1, :keep] = piece
                at += many // keep

        def store(out_ref, made, start, group, blocks):
            wide = made.shape[1] // 2
            for x in range(2):
                piece = made[:, x * wide : (x + 1) * wide].reshape(blocks, keep, wide)
                out_ref[x, group : group + blocks, :keep, start : start + wide] = piece

        for step, out_ref in enumerate(refs[-2:]):

            @pl.when(pl.program_id(0) == step)
            def _():
                for which in range(3):
                    store(out_ref, dot(left_ref[...], d_ref[which]).astype(BF16), which * size, 0, groups)
                if mixed:
                    for i in range(2):
                        made = dot(refs[i][...], refs[2][...]).astype(BF16)
                        store(out_ref, made, mixed_at, i * groups // 2, groups // 2)
                    if mixed_at > 3 * size:
                        out_ref[:, :, :, 3 * size : mixed_at] = jnp.zeros((2, groups, keep, mixed_at - 3 * size), BF16)
                if more:
                    out_ref[:, :, keep:, :] = jnp.zeros((2, groups, more, cols), BF16)
                    put(out_ref)

    operands = [xt, d] + list(mixed or ()) + arrays
    specs = [whole(xt.shape), pl.BlockSpec((3, rows, part), lambda i, halves: (0, 0, halves[i]))]
    if mixed:
        specs += [whole(mixed[0].shape), whole(mixed[1].shape), pl.BlockSpec((rows, width // 2), lambda i, halves: (0, halves[i]))]
    specs += [whole(a.shape) for a in arrays]
    shape = (2, groups, keep + more, cols)
    return call(
        kernel,
        "token_weights_grad",
        operands,
        specs,
        (like(shape), like(shape)),
        (whole(shape), whole(shape)),
        grid=(2,),
        scalars=[halves],
        carry=carry,
        time=8,
    )


def token_grad(base, d, w, dtype, tile=256, after=()):
    rows, width = base.shape
    part = d.shape[2]

    def kernel(base_ref, d_ref, w_ref, out_ref):
        total = base_ref[...]
        for i in range(3):
            total = total + dot_nt(d_ref[i], w_ref[:, i * part : (i + 1) * part])
        out_ref[...] = total.astype(dtype)

    tok = pl.BlockSpec((tile, width), lambda i: (i, 0))
    return call(
        kernel,
        "token_grad",
        [base, d, w],
        [tok, pl.BlockSpec((3, tile, part), lambda i: (0, i, 0)), whole(w.shape)],
        like((rows, width), dtype),
        tok,
        grid=(rows // tile,),
        after=after,
        time=6,
    )


def digits_of(axis, total, base):
    digits, stride = [], total
    while stride > 1:
        size = base if stride % base == 0 else 2
        stride //= size
        digits.append((axis, stride, size))
    return digits


def total_of(terms):
    total = terms[0].astype(F32)
    for term in terms[1:]:
        total = total + term.astype(F32)
    return total.astype(BF16)


class Layout:
    def __init__(self, mesh):
        self.replicas, self.groups = mesh.shape["replica"], mesh.shape["group"]
        self.group = digits_of("group", self.groups, 4)
        replica = digits_of("replica", self.replicas, 2)
        self.core, self.over = replica[-1], replica[:-1]
        self.sizes = {"replica": self.replicas, "group": self.groups}
        self.devices = self.replicas * self.groups
        cores = self.core[2]
        self.same_core = [
            [r * self.groups + g for r in range(c, self.replicas, cores) for g in range(self.groups)] for c in range(cores)
        ]

    def place(self, digit):
        axis, stride, size = digit
        return (lax.axis_index(axis) // stride) % size

    def send(self, value, digit, shift=1):
        axis, stride, size = digit
        pairs = []
        for i in range(self.sizes[axis]):
            own = (i // stride) % size
            pairs.append((i, i + ((own + shift) % size - own) * stride))
        return lax.ppermute(value, axis, pairs)

    def sends(self, value, digit):
        return [self.send(value, digit, k) for k in range(1, digit[2])]

    def pieces(self, parts, shape):
        core = self.place(self.core).astype(jnp.int32)
        cores = jnp.stack([core, 1 - core])
        buffers, spans, start = [], [], 0
        for chain, cols in parts:
            came = self.send(chain.value, self.core)
            blocks = math.prod(d[2] for d in self.over)
            for buffer in (chain.value, came):
                buffers.append(buffer.reshape(blocks, -1, buffer.shape[-1]))
                spans.append((0, cols, start))
            start += cols
        return Pieces(cores, buffers, spans, shape)

    def along(self, digit):
        axis, stride, size = digit
        stride *= self.groups if axis == "replica" else 1
        starts = [d for d in range(self.devices) if d // stride % size == 0]
        return [[d + k * stride for k in range(size)] for d in starts]


class Chain:
    def __init__(self, layout, value, order, done=()):
        self.layout, self.value, self.order, self.done = layout, value, list(order), list(done)
        self.came = layout.sends(value, self.order[0]) if self.order else []

    def job(self, first=0, cols=None):
        digits = self.layout.over + self.layout.group
        axis = sum(digits.index(d) < digits.index(self.order[0]) for d in self.done)
        place = self.layout.place(self.order[0]).astype(jnp.int32).reshape(1)
        return [self.value] + self.came, place, axis, first, self.value.shape[-1] if cols is None else cols

    def after(self, value, order=None):
        return Chain(self.layout, value, (self.order if order is None else order)[1:], self.done + self.order[:1])


def move(*chains, carry=()):
    values = stack([c.job() for c in chains], carry)
    values, carried = values if carry else (values, ())
    moved = [c.after(v) for c, v in zip(chains, values)]
    return moved + list(carried)


class Reduction:
    def __init__(self, layout, terms, order):
        self.layout, self.dims, self.terms, self.order = layout, layout.over + layout.group, terms, list(order)

    def job(self):
        digit = self.digit = self.order.pop(0)
        axis = self.dims.index(digit)
        count = lambda dims: math.prod(d[2] for d in dims)
        shape = (count(self.dims[:axis]), digit[2], count(self.dims[axis + 1 :]))
        self.dims = self.dims[:axis] + self.dims[axis + 1 :]
        terms = [(t.reshape(shape + t.shape[-2:]), block, cols) for t, block, cols in self.terms]
        return self.layout.place(digit).astype(jnp.int32).reshape(1), terms

    def take(self, made):
        came = [self.layout.send(s, self.digit, k + 1) for k, s in enumerate(made[:-1])]
        self.terms = [(t, (0, 0), t.shape[-2:]) for t in [made[-1]] + came]

    def came(self):
        return [t for t, _, _ in self.terms[1:]]

    def last(self):
        return [t.reshape((-1,) + t.shape[-2:]) for t, _, _ in self.terms]


def step(*reductions, carry=(), after=()):
    jobs = [r.job() for r in reductions]
    if len({r.digit[2] for r in reductions}) == 1:
        made, carry = combine(jobs, carry, after)
    else:
        made = []
        for job in jobs:
            one, carry = combine([job], carry, after)
            made += one
    for reduction, one in zip(reductions, made):
        reduction.take(one)
    return carry


def local(layout, tokens, segment_ids, w_query, b_query, w_key, w_value, b_value, w_out, b_out, gain_first, shift_first, w_inner, b_inner, w_outer, b_outer, gain_second, shift_second, cotangent):
    LAST.clear()
    groups, devices = layout.groups, layout.devices
    seqs, length = segment_ids.shape
    width = tokens.shape[1]
    hidden = w_inner.shape[1]
    each = b_query.shape[0]
    half = width // 2
    core = layout.place(layout.core).astype(jnp.int32)
    mine, theirs = core.reshape(1), (1 - core).reshape(1)
    halves = jnp.concatenate([theirs, mine])
    z_digit, y_digits = layout.group[:1], layout.group[1:]
    zxy, zyx = z_digit + layout.over + y_digits, z_digit + y_digits + layout.over
    xyz, yxz = layout.over + y_digits + z_digit, y_digits + layout.over + z_digit

    vectors = (b_query, b_value, b_out, gain_first, shift_first, b_outer, gain_second, shift_second, b_inner)
    lanes, cut, wide = 128, 3 * half // 2, (3 * half + width) // 2
    (first,) = pack([w_query, w_key, w_value], [[(0, 0, half), (1, 0, half), (2, 0, half)]], vectors)
    high = first.shape[0]
    first = Chain(layout, first, zxy)
    xt = transposed(tokens)
    a, b = stack([first.job(0, cut), first.job(cut, cut + lanes)])
    a, b = first.after(a), first.after(b, zyx)
    second, last, inner_rows = pack(
        [w_query, w_key, w_value, w_out, w_outer, w_inner],
        [[(0, half, half), (1, half, half), (2, half, half), (3, 0, width)], [(4, 0, width)], [(5, 0, hidden)]],
    )
    whole_winner = lax.all_gather(inner_rows, ("replica", "group"), axis=0, tiled=True)
    a, b, second = move(a, b, carry=[second])
    second = Chain(layout, second, zxy)
    while a.order[1:]:
        a, b = move(a, b)
    va, vb, c, d = stack([a.job(), b.job(), second.job(0, wide), second.job(wide, wide)])
    a, b = a.after(va), b.after(vb)
    pieces0 = layout.pieces([(a, cut), (b, cut)], (width, 3 * half))
    c, d = second.after(c), second.after(d, zyx)
    spots = vector_places(vectors, high)
    used = max(r for r, _ in spots) + 1
    both = [v.reshape(-1, groups, high, v.shape[-1])[:, :, :used, cut:].astype(F32) for v in pieces0.buffers[-2:]]
    small = jnp.stack([jnp.where(core == k, both[0], both[1]) for k in range(2)], axis=1).reshape(devices, used, lanes)
    vec = jnp.stack([small[:, r, l : l + each].reshape(width) for r, l in spots[:-1]])
    r, l = spots[-1]
    whole_binner = small[:, r, l : l + b_inner.shape[0]].reshape(1, -1)
    row, col = segment_ids.reshape(seqs, 1, length), segment_ids.reshape(seqs, length, 1)

    (qkv0, wqkv0), (last,) = project(pieces0, tokens, vec, 0, carry=[last])
    last = Chain(layout, last, zxy)
    while c.order[1:]:
        c, d = move(c, d)
    o0, ot0, probs0, share0 = attend(qkv0, row, col)
    c_value, d_value, e, f = stack([c.job(), d.job(), last.job(0, half), last.job(half, half)])
    c, d = c.after(c_value), d.after(d_value)
    pieces1 = layout.pieces([(c, wide), (d, wide)], (width, 3 * half + width))
    e, f = last.after(e), last.after(f, zyx)
    qkv1, wqkv1 = project(pieces1.part(0, 3 * half), tokens, vec, 1)
    o1, ot1, probs1, share1 = attend(qkv1, row, col)
    while len(e.order) > 1:
        e, f = move(e, f)
    n1, rstd1, h, ht, whole_wout = join(pieces1.part(3 * half, width), o0, o1, tokens, vec)
    made = inner(h, whole_winner, whole_binner, 0, 2)
    e, f = move(e, f)
    pieces2 = layout.pieces([(e, half), (f, half)], (w_outer.shape[0] * devices, width))
    u, slope = inner(h, whole_winner, whole_binner, 1, 2, made)
    out, dz2, dm, dmt, sums2, whole_wouter = outer(pieces2, u, n1, cotangent, vec)

    def reduction(other, own, *orders, by_rows=False, runs=None):
        came = layout.send(other, layout.core)
        rows, cols = own.shape[2:]
        if by_rows:
            parts = [((i, 0), (rows // len(orders), cols)) for i in range(len(orders))]
        else:
            runs = runs or [(i * cols // len(orders), cols // len(orders)) for i in range(len(orders))]
            parts = [((0, start // size), (rows, size)) for start, size in runs]
        return [Reduction(layout, [(own,) + part, (came,) + part], order) for part, order in zip(parts, orders)]

    def along_z(reductions, carry=()):
        sums = add_up([[t.reshape(-1, t.shape[-1]) for t in r.last()] for r in reductions], carry)
        sums, carry = sums if carry else (sums, ())
        sums = lax.psum_scatter(sums, ("replica", "group"), scatter_dimension=0, axis_index_groups=layout.along(z_digit[0]), tiled=True)
        return [sums] + list(carry)

    def across_z(reductions, carry=()):
        made = gather_sums(layout.place(z_digit[0]).astype(jnp.int32).reshape(1), [r.last() for r in reductions], carry)
        made, carry = made if carry else (made, ())
        return [[made[-1]] + [layout.send(s, z_digit[0], k + 1) for k, s in enumerate(made[:-1])]] + list(carry)

    spread = lambda block: lax.all_gather(block, "replica", axis=0, tiled=False)
    middle = range(len(xyz) - 2)
    cols = 3 * half // 4
    other = outer_grad(theirs, dmt, u, groups)
    own = outer_grad(mine, dmt, u, groups)
    outers = reduction(other, own, xyz, yxz, by_rows=True)
    step(*outers)
    other, own, dh, sum_inner = inner_back(halves, dm, whole_wouter, slope, ht, whole_winner, groups)
    for _ in middle:
        (other,) = step(*outers, carry=[other])
    inners = reduction(other, own, xyz, yxz)
    dz1, da, do, sums1 = join_back(dz2, dh, n1, rstd1, vec, whole_wout)
    (got_wouter,) = along_z(outers)
    step(*inners)
    d0, sq0, sv0 = attend_back(qkv0, ot0, probs0, share0, do, 0)
    other, own = token_weights_grad(halves, xt, d0, groups, mixed=(ot0, ot1, da))
    for _ in middle:
        (other,) = step(*inners, carry=[other])
    firsts = reduction(other, own, xyz, yxz, runs=((0, cols), (other.shape[3] - width // 4, width // 4)))
    d1, sq1, sv1 = attend_back(qkv1, ot1, probs1, share1, do, 1)
    (got_winner,) = along_z(inners)
    step(*firsts)
    partial = token_grad(dz1, d0, wqkv0, F32)
    vectors = [((sq0, sq1), 0), ((sv0, sv1), 0)] + [((sums,), i) for sums in (sums1, sums2) for i in range(3)] + [((sum_inner,), 0)]
    other, own = token_weights_grad(halves, xt, d1, groups, vectors=vectors)
    for _ in middle:
        other, got_wouter = step(*firsts, carry=[other, got_wouter])
    got_wouter = spread(got_wouter)
    seconds = reduction(other, own, xyz, yxz, runs=((0, 2 * cols // 3), (2 * cols // 3, cols // 3)))
    cores = layout.core[2]
    order = [r % cores * (layout.replicas // cores) + r // cores for r in range(layout.replicas)]
    step(*seconds)
    (first_sums,) = across_z(firsts)
    grad_tokens = token_grad(partial, d1, wqkv1, BF16)
    for _ in middle:
        (got_winner,) = step(*seconds, after=first_sums[1:], carry=[got_winner])
    got_winner = spread(got_winner)
    (second_sums,) = across_z(seconds)
    grad_wouter = outer_result(got_wouter, order)
    got = [add_up([first_sums, second_sums])]
    places = jnp.zeros((1,), jnp.int32)
    weight = 1
    for digit in layout.over[::-1] + [layout.core]:
        own = layout.place(digit).astype(jnp.int32)
        places = jnp.concatenate([places + own * weight, places + (1 - own) * weight])
        got = got + [layout.send(g, digit) for g in got]
        weight *= digit[2]
    grad_winner = inner_result(got_winner, order)
    keep = width // groups
    wq, wk, wv, grad_wout, sums = token_weights_result(got, places, keep, half // 4, width // 4)
    bq, bv, bout, gain1, shift1, bouter, gain2, shift2 = (sums[i, :keep] for i in range(8))
    binner = sums[8 : 8 + hidden // width, :keep].reshape(-1)
    return (out, grad_tokens, wq, bq, wk, wv, bv, grad_wout, bout, gain1, shift1, grad_winner, binner, grad_wouter, bouter, gain2, shift2)


def solution(mesh):
    layout = Layout(mesh)
    both = ("replica", "group")
    rows, vector = P(both, None), P(both)
    in_specs = (rows, rows, rows, vector, rows, rows, vector, rows, vector, vector, vector, rows, vector, rows, vector, vector, vector, rows)
    kept, kept_vector = P("group", None), P("group")
    out_specs = (rows, rows, kept, kept_vector, kept, kept, kept_vector, kept, kept_vector, kept_vector, kept_vector, kept, kept_vector, kept, kept_vector, kept_vector, kept_vector)
    return jax.shard_map(functools.partial(local, layout), mesh=mesh, in_specs=in_specs, out_specs=out_specs, check_vma=False)
```

```python
import functools
import math

import jax
import jax.numpy as jnp
from jax import lax
from jax.experimental import pallas as pl
from jax.experimental.pallas import tpu as pltpu
from jax.sharding import PartitionSpec as P

F32 = jnp.float32
BF16 = jnp.bfloat16
VMEM_LIMIT = 46 * 1024 * 1024
ANY = pl.BlockSpec(memory_space=pl.ANY)
ALL_VMEM = 62 * 1024 * 1024
HBM = pl.BlockSpec(memory_space=pltpu.HBM)
BQ, BV, BOUT, GAIN1, SHIFT1, BOUTER, GAIN2, SHIFT2 = range(8)


LAST = []


def call(kernel, name, operands, in_specs, out_shape, out_specs, *, grid=(1,), scalars=(), after=(), carry=(), into=(), scratch=(), time=0, room=None):
    single = not isinstance(out_shape, (tuple, list))
    shapes, specs = ([out_shape], [out_specs]) if single else (list(out_shape), list(out_specs))
    first, made = len(scalars) + len(operands), len(shapes)
    ends = made + len(carry)
    unread = list(carry) + list(into) + list(after) + LAST

    limit = VMEM_LIMIT
    if room is not None:
        pairs = list(zip(specs, shapes)) + list(zip(in_specs, operands))
        blocks = [math.prod(spec.block_shape) * array.dtype.itemsize for spec, array in pairs if spec.block_shape is not None]
        limit = ALL_VMEM if room < 0 else min(VMEM_LIMIT, 2 * sum(blocks) + room)

    def body(*refs):
        outs = first + len(unread)
        kernel(*refs[:first], *refs[outs : outs + made], *refs[outs + ends + 1 :])

    outs = pl.pallas_call(
        body,
        out_shape=shapes + [jax.ShapeDtypeStruct(c.shape, c.dtype) for c in carry] + [jax.ShapeDtypeStruct((8, 128), F32)],
        grid_spec=pltpu.PrefetchScalarGridSpec(
            num_scalar_prefetch=len(scalars),
            grid=grid,
            in_specs=list(in_specs) + [HBM] * len(carry) + [ANY] * (len(unread) - len(carry) - len(LAST)) + [HBM] * len(LAST),
            out_specs=specs + [HBM] * (len(carry) + 1),
            scratch_shapes=list(scratch),
        ),
        input_output_aliases={first + i: made + i for i in range(len(carry))} | {first + len(carry) + i: i for i in range(len(into))},
        compiler_params=pltpu.CompilerParams(dimension_semantics=("arbitrary",) * len(grid), vmem_limit_bytes=limit),
        cost_estimate=pl.CostEstimate(flops=int(1 + time * 1e9), bytes_accessed=int(1 + time * 1e6), transcendentals=0),
        name=name,
    )(*scalars, *operands, *unread)
    LAST[:] = outs[ends:]
    result = outs[0] if single else tuple(outs[:made])
    return (result, outs[made:ends]) if carry else result


def like(shape, dtype=BF16):
    return jax.ShapeDtypeStruct(shape, dtype)


def far(shape, dtype=BF16):
    return pltpu.HBM(shape, dtype)


def dot(left, right):
    return lax.dot_general(left, right, (((1,), (0,)), ((), ())), preferred_element_type=F32)


def dot_nt(left, right):
    return lax.dot_general(left, right, (((1,), (1,)), ((), ())), preferred_element_type=F32)


def whole(shape):
    return pl.BlockSpec(shape, lambda *i: (0,) * len(shape))


def column_sum(value):
    return jnp.sum(value.astype(F32), axis=0, keepdims=True)


def pack(operands, makes, vectors=()):
    lanes = 128 if vectors else 0

    def kernel(*refs):
        outs = refs[len(operands) + len(vectors) :]
        for out_ref, pieces in zip(outs, makes):
            at = 0
            for which, start, size in pieces:
                out_ref[:, at : at + size] = refs[which][:, start : start + size]
                at += size
        if vectors:
            rows, cols = outs[0].shape
            outs[0][:, cols - lanes :] = jnp.zeros((rows, lanes), BF16)
            for ref, (row, lane) in zip(refs[len(operands) :], vector_places(vectors, rows)):
                size = ref.shape[0]
                start = cols - lanes + lane
                outs[0][row : row + 1, start : start + size] = ref[...].astype(F32).reshape(1, size).astype(BF16)

    shapes = [(operands[pieces[0][0]].shape[0], sum(p[2] for p in pieces)) for pieces in makes]
    if vectors:
        shapes[0] = (shapes[0][0], shapes[0][1] + lanes)
    everything = list(operands) + list(vectors)
    return call(kernel, "pack", everything, [whole(o.shape) for o in everything], [like(s) for s in shapes], [whole(s) for s in shapes], room=-1)


def vector_places(vectors, rows):
    size = vectors[0].shape[0]
    places = [(i % rows, i // rows * size) for i in range(len(vectors) - 1)]
    return places + [(8, 0) if rows > 8 else (0, 64)]


def stack(jobs, carry=()):
    flat = [array for arrays, *_ in jobs for array in arrays]
    shapes = []
    for arrays, _, axis, _, cols in jobs:
        shape = arrays[0].shape
        shapes.append(shape[:axis] + (len(arrays),) + shape[axis:-1] + (cols,))

    def kernel(*refs):
        place_refs, refs = refs[: len(jobs)], refs[len(jobs) :]
        ins, outs, arrived = refs[: len(flat)], refs[len(flat) : -1], refs[-1]
        copies = []
        for (arrays, _, axis, first, cols), place_ref, out_ref in zip(jobs, place_refs, outs):
            count = len(arrays)
            for k in range(count):
                ref = ins[len(copies)]
                source = ref.at[(slice(None),) * (len(ref.shape) - 1) + (pl.ds(first, cols),)]
                target = out_ref.at[(slice(None),) * axis + (lax.rem(place_ref[0] + count - k, count),)]
                copies.append(pltpu.make_async_copy(source, target, arrived.at[len(copies)]))
        for copy in copies:
            copy.start()
        for copy in copies:
            copy.wait()

    return call(
        kernel,
        "stack",
        flat,
        [ANY] * len(flat),
        [like(shape) for shape in shapes],
        [whole(shape) for shape in shapes],
        scalars=[job[1] for job in jobs],
        carry=carry,
        scratch=[pltpu.SemaphoreType.DMA((len(flat),))],
        room=4 << 20,
    )


def combine(jobs, carry=(), after=()):
    n = jobs[0][1][0][0].shape[1]
    sizes = []
    for _, terms in jobs:
        before, _, behind, _, _ = terms[0][0].shape
        sizes.append((before, behind) + terms[0][2])
    flat = [t for _, terms in jobs for t in terms]

    def kernel(*refs):
        refs = refs[len(jobs) :]
        outs = refs[len(flat) :]
        i = 0
        for job, (_, terms) in enumerate(jobs):
            total = refs[i][:, 0].astype(F32)
            for ref in refs[i + 1 : i + len(terms)]:
                total = total + ref[:, 0].astype(F32)
            total = total.astype(BF16)
            i += len(terms)
            for j, out_ref in enumerate(outs[job * n : (job + 1) * n]):

                @pl.when(pl.program_id(0) == j)
                def _():
                    out_ref[...] = total

    def at(job, block):
        before, behind, rows, cols = sizes[job]
        return pl.BlockSpec((before, 1, behind, rows, cols), lambda i, *own: (0, lax.rem(own[job][0] + i + 1, n), 0) + block)

    made = call(
        kernel,
        "combine",
        [t[0] for t in flat],
        [at(job, t[1]) for job, (_, terms) in enumerate(jobs) for t in terms],
        [far(size) for size in sizes for _ in range(n)],
        [whole(size) for size in sizes for _ in range(n)],
        grid=(n,),
        scalars=[own for own, _ in jobs],
        carry=carry,
        after=after,
        room=12 << 20,
    )
    made, carried = made if carry else (made, ())
    return [made[job * n : (job + 1) * n] for job in range(len(jobs))], carried


def gather_sums(own, lists, carry=()):
    flat = [t for terms in lists for t in terms]
    n = flat[0].shape[0]
    rows = max(t.shape[1] for t in flat)
    cols = sum(terms[0].shape[2] for terms in lists)

    def kernel(own_ref, *refs):
        outs = refs[len(flat) :]
        parts, i = [], 0
        for terms in lists:
            total = refs[i][0].astype(F32)
            for ref in refs[i + 1 : i + len(terms)]:
                total = total + ref[0].astype(F32)
            parts.append(total.astype(BF16))
            i += len(terms)
        for j, out_ref in enumerate(outs):

            @pl.when(pl.program_id(0) == j)
            def _():
                at = 0
                for part in parts:
                    high, wide = part.shape
                    out_ref[:high, at : at + wide] = part
                    if high < rows:
                        out_ref[high:, at : at + wide] = jnp.zeros((rows - high, wide), BF16)
                    at += wide

    return call(
        kernel,
        "gather_sums",
        flat,
        [pl.BlockSpec((1,) + t.shape[1:], lambda i, own: (lax.rem(own[0] + i + 1, n), 0, 0)) for t in flat],
        [like((rows, cols))] * n,
        [whole((rows, cols))] * n,
        grid=(n,),
        scalars=[own],
        carry=carry,
        room=6 << 20,
    )


def add_up(lists, carry=()):
    flat = [a for arrays in lists for a in arrays]

    def kernel(*refs):
        at, i = 0, 0
        for arrays in lists:
            total = refs[i][...].astype(F32)
            for ref in refs[i + 1 : i + len(arrays)]:
                total = total + ref[...].astype(F32)
            rows, cols = total.shape
            refs[-1][:rows, at : at + cols] = total.astype(BF16)
            if rows < refs[-1].shape[0]:
                refs[-1][rows:, at : at + cols] = jnp.zeros((refs[-1].shape[0] - rows, cols), BF16)
            at += cols
            i += len(arrays)

    shape = (max(a.shape[0] for a in flat), sum(arrays[0].shape[1] for arrays in lists))
    return call(kernel, "add_up", flat, [whole(a.shape) for a in flat], like(shape), whole(shape), carry=carry, room=12 << 20)


def outer_result(got, order, runs=2):
    count, cols, rows = got.shape
    rows //= runs

    def kernel(got_ref, out_ref):
        for i, j in enumerate(order):
            for run in range(runs):
                at = (j * runs + run) * cols
                out_ref[:, at : at + cols] = got_ref[i, :, run * rows : (run + 1) * rows].astype(F32).T

    shape = (rows, count * runs * cols)
    return call(kernel, "outer_result", [got], [whole(got.shape)], like(shape, F32), whole(shape), room=8 << 20)


def inner_result(got, order):
    count, rows, cols = got.shape

    def kernel(got_ref, out_ref):
        for i, j in enumerate(order):
            out_ref[:, j * cols : (j + 1) * cols] = got_ref[i].astype(F32)

    shape = (rows, count * cols)
    return call(kernel, "inner_result", [got], [whole(got.shape)], like(shape, F32), whole(shape), room=8 << 20)


def wide_results(got, order, runs=2):
    count, rows, cols = got.shape
    high, wide = cols // 2 // runs, cols // 2

    def kernel(got_ref, first_ref, second_ref):
        for i, j in enumerate(order):
            for run in range(runs):
                at = (j * runs + run) * rows
                first_ref[:, at : at + rows] = got_ref[i, :, run * high : (run + 1) * high].astype(F32).T
            second_ref[:, j * wide : (j + 1) * wide] = got_ref[i, :, wide:].astype(F32)

    shapes = [(high, count * runs * rows), (rows, count * wide)]
    return call(kernel, "wide_results", [got], [whole(got.shape)], [like(s, F32) for s in shapes], [whole(s) for s in shapes], room=8 << 20)


def token_weights_result(pieces, places, keep, size, last):
    count = len(pieces)
    rows = pieces[0].shape[0]
    second = 3 * size + last

    def kernel(place_ref, *refs):
        outs = refs[count:]
        for i in range(count):
            at = lambda j, wide: pl.ds(pl.multiple_of(j * wide, wide), wide)
            piece = refs[i][:keep].astype(F32)
            for which in range(3):
                outs[which][:, at(place_ref[i], size)] = piece[:, which * size : (which + 1) * size]
                outs[which][:, at(count + place_ref[i], size)] = piece[:, second + which * size : second + (which + 1) * size]
            outs[3][:, at(place_ref[i], last)] = piece[:, 3 * size : second]
        outs[4][...] = refs[0][keep:, second:].astype(F32)

    shapes = [(keep, 2 * count * size)] * 3 + [(keep, count * last), (rows - keep, 3 * size)]
    return call(
        kernel,
        "token_weights_result",
        pieces,
        [whole(p.shape) for p in pieces],
        [like(s, F32) for s in shapes],
        [whole(s) for s in shapes],
        scalars=[places],
        room=8 << 20,
    )


def transposed(x, tile=256):
    rows, cols = x.shape

    def kernel(x_ref, out_ref):
        out_ref[...] = x_ref[...].T

    return call(
        kernel,
        "transposed",
        [x],
        [pl.BlockSpec((tile, cols), lambda i: (i, 0))],
        far((cols, rows)),
        pl.BlockSpec((cols, tile), lambda i: (0, i)),
        grid=(rows // tile,),
        time=3,
    )


class Pieces:
    def __init__(self, cores, buffers, spans, shape):
        self.cores, self.buffers, self.spans, self.shape = cores, buffers, spans, shape
        self.count = sum(b.shape[0] for b in buffers)

    def part(self, start, cols):
        kept = []
        for buffer, (first, size, to) in zip(self.buffers, self.spans):
            low, high = max(to, start), min(to + size, start + cols)
            kept.append((buffer, (first + low - to, high - low, low - start)))
        buffers, spans = zip(*(k for k in kept if k[1][1] > 0))
        return Pieces(self.cores, list(buffers), list(spans), (self.shape[0], cols))

    def scratch(self):
        return [pltpu.VMEM(self.shape, BF16), pltpu.SemaphoreType.DMA((self.count,)), pltpu.SemaphoreType.DMA]

    def fetch(self, cores_ref, refs, held, arrived):
        copies = []
        for i, (ref, (first, cols, to)) in enumerate(zip(refs, self.spans)):
            blocks, rows, _ = ref.shape
            for j in range(blocks):
                target = held.at[pl.ds(pl.multiple_of((2 * j + cores_ref[i % 2]) * rows, rows), rows), pl.ds(to, cols)]
                copies.append(pltpu.make_async_copy(ref.at[j, :, pl.ds(first, cols)], target, arrived.at[len(copies)]))
        for copy in copies:
            copy.start()
        for copy in copies:
            copy.wait()


def project(pieces, x, vec, half, carry=()):
    rows, depth = x.shape
    cols = pieces.shape[1]
    tile = cols // 3
    count = len(pieces.buffers)

    def kernel(*refs):
        (cores_ref,), (x_ref, vec_ref), refs = refs[:1], refs[1 : 3], refs[3:]
        buffer_refs, (out_ref, whole_ref, held, arrived, left) = refs[:count], refs[count:]
        step = pl.program_id(0)
        write = pltpu.make_async_copy(held, whole_ref, left)

        @pl.when(step == 0)
        def _():
            pieces.fetch(cores_ref, buffer_refs, held, arrived)
            write.start()

        at = slice(half * tile, (half + 1) * tile)
        for i, row in enumerate((BQ, None, BV)):

            @pl.when(step == i)
            def _():
                made = dot(x_ref[...], held[:, i * tile : (i + 1) * tile])
                out_ref[...] = (made if row is None else made + vec_ref[row : row + 1, at]).astype(BF16)

        @pl.when(step == 2)
        def _():
            write.wait()

    return call(
        kernel,
        "project",
        [x, vec] + list(pieces.buffers),
        [whole(x.shape), whole(vec.shape)] + [ANY] * count,
        (like((rows, cols)), like((depth, cols))),
        (pl.BlockSpec((rows, tile), lambda i, *_: (0, i)), HBM),
        grid=(3,),
        scalars=[pieces.cores],
        scratch=pieces.scratch(),
        carry=carry,
        time=6,
    )


def attend(qkv, row, col, heads=4, size=64, carry=()):
    seqs, _, length = row.shape
    width = qkv.shape[1] // 3
    block = heads * size
    blocks = width // block

    def kernel(q_ref, k_ref, v_ref, row_ref, col_ref, o_ref, ot_ref, p_ref, r_ref, bias_ref):
        @pl.when(pl.program_id(1) == 0)
        def _():
            bias_ref[...] = jnp.where(col_ref[0] == row_ref[0], 0.0, -1e9).astype(F32)

        qt = (q_ref[...] * jnp.asarray(0.125, BF16)).T
        vt = v_ref[...].T
        zero = jnp.zeros((size, length), BF16)
        for head in range(heads):
            here = slice(head * size, (head + 1) * size)
            pair = slice(head // 2 * 2 * size, (head // 2 + 1) * 2 * size)
            own = [qt[here], zero] if head % 2 == 0 else [zero, qt[here]]
            scores = dot(k_ref[:, pair], jnp.concatenate(own, axis=0)) + bias_ref[...]
            expo = jnp.exp(scores - jnp.max(scores, axis=0, keepdims=True))
            share = 1.0 / jnp.sum(expo, axis=0, keepdims=True)
            expo = expo.astype(BF16)
            p_ref[0, head] = expo
            r_ref[0, 0, head : head + 1] = share
            ot_ref[here, :] = (dot(vt[here], expo) * share).astype(BF16)
        o_ref[...] = ot_ref[...].T

    spec = lambda part: pl.BlockSpec((length, block), lambda s, p: (s, part * blocks + p))
    return call(
        kernel,
        "attend",
        [qkv, qkv, qkv, row, col],
        [spec(0), spec(1), spec(2), pl.BlockSpec((1, 1, length), lambda s, p: (s, 0, 0)), pl.BlockSpec((1, length, 1), lambda s, p: (s, 0, 0))],
        (like((seqs * length, width)), like((width, seqs * length)), like((seqs, heads * blocks, length, length)), like((seqs, blocks, heads, length), F32)),
        (
            pl.BlockSpec((length, block), lambda s, p: (s, p)),
            pl.BlockSpec((block, length), lambda s, p: (p, s)),
            pl.BlockSpec((1, heads, length, length), lambda s, p: (s, p, 0, 0)),
            pl.BlockSpec((1, 1, heads, length), lambda s, p: (s, p, 0, 0)),
        ),
        grid=(seqs, blocks),
        scratch=[pltpu.VMEM((length, length), F32)],
        carry=carry,
        time=11,
    )


def attend_back(qkv, ot, probs, share, do, part, carry=()):
    seqs, blocks, heads, length = share.shape
    tokens, width = ot.shape[1], ot.shape[0]
    block = width // blocks
    size = block // heads

    def kernel(q_ref, k_ref, v_ref, ot_ref, p_ref, r_ref, do_ref, d_ref, bq_ref, bv_ref):
        dot_t = do_ref[...].T.astype(F32)
        shares = jnp.concatenate([jnp.broadcast_to(r_ref[0, 0, h : h + 1], (size, length)) for h in range(heads)], axis=0)
        dot_t = (dot_t * shares).astype(BF16)
        do = dot_t.T
        kt = k_ref[...].T
        product = dot_t.astype(F32) * ot_ref[...].astype(F32)
        zero = jnp.zeros((size, length), BF16)
        first = lax.broadcasted_iota(jnp.int32, (1, 2 * size), 1) < size
        dk, dv, dqt = [], [], []
        for head in range(heads):
            here = slice(head * size, (head + 1) * size)
            pair = slice(head // 2 * 2 * size, (head // 2 + 1) * 2 * size)
            delta = jnp.sum(product[here], axis=0, keepdims=True)
            own = [dot_t[here], zero] if head % 2 == 0 else [zero, dot_t[here]]
            expo = p_ref[0, head]
            ds = (expo.astype(F32) * (dot(v_ref[:, pair], jnp.concatenate(own, axis=0)) - delta)).astype(BF16)
            dv.append(dot(expo, do[:, pair]))
            dk.append(dot(ds, q_ref[:, pair]))
            dqt.append(dot(kt[here], ds))
        paired = lambda parts: jnp.concatenate([jnp.where(first, parts[i], parts[i + 1]) for i in range(0, heads, 2)], axis=1)
        dq = (jnp.concatenate(dqt, axis=0) * 0.125).astype(BF16).T
        dv = paired(dv).astype(BF16)
        d_ref[0] = dq
        d_ref[1] = (paired(dk) * 0.125).astype(BF16)
        d_ref[2] = dv
        bq_ref[0] = column_sum(dq)
        bv_ref[0] = column_sum(dv)

    spec = lambda which: pl.BlockSpec((length, block), lambda s, p: (s, which * blocks + p))
    sums = pl.BlockSpec((1, 1, block), lambda s, p: (s, 0, p))
    return call(
        kernel,
        "attend_back",
        [qkv, qkv, qkv, ot, probs, share, do],
        [
            spec(0),
            spec(1),
            spec(2),
            pl.BlockSpec((block, length), lambda s, p: (p, s)),
            pl.BlockSpec((1, heads, length, length), lambda s, p: (s, p, 0, 0)),
            pl.BlockSpec((1, 1, heads, length), lambda s, p: (s, p, 0, 0)),
            spec(part),
        ],
        (far((3, tokens, width)), like((seqs, 1, width), F32), like((seqs, 1, width), F32)),
        (pl.BlockSpec((3, length, block), lambda s, p: (0, s, p)), sums, sums),
        grid=(seqs, blocks),
        carry=carry,
        time=11,
    )


def normed(z):
    center = z - jnp.mean(z, axis=-1, keepdims=True)
    rstd = lax.rsqrt(jnp.mean(center * center, axis=-1, keepdims=True) + 1e-06)
    return center * rstd, rstd


def norm_back(dn, n, rstd):
    return rstd * (dn - jnp.mean(dn, axis=-1, keepdims=True) - n * jnp.mean(dn * n, axis=-1, keepdims=True))


def join(pieces, o0, o1, x, vec, tile=256, after=()):
    rows, width = x.shape
    count = len(pieces.buffers)

    def kernel(*refs):
        (cores_ref,), (o0_ref, o1_ref, x_ref, vec_ref), refs = refs[:1], refs[1 : 5], refs[5:]
        buffer_refs, (n_ref, r_ref, h_ref, ht_ref, whole_ref, held, arrived, left) = refs[:count], refs[count:]
        write = pltpu.make_async_copy(held, whole_ref, left)

        @pl.when(pl.program_id(0) == 0)
        def _():
            pieces.fetch(cores_ref, buffer_refs, held, arrived)
            write.start()

        half = o0_ref.shape[1]
        mixed = dot(o0_ref[...], held[:half]) + dot(o1_ref[...], held[half:])
        z = x_ref[...].astype(F32) + (mixed + vec_ref[BOUT : BOUT + 1])
        n, rstd = normed(z)
        n_ref[...] = n
        r_ref[...] = rstd
        h = (n * vec_ref[GAIN1 : GAIN1 + 1] + vec_ref[SHIFT1 : SHIFT1 + 1]).astype(BF16)
        h_ref[...] = h
        ht_ref[...] = h.T

        @pl.when(pl.program_id(0) == pl.num_programs(0) - 1)
        def _():
            write.wait()

    tok = pl.BlockSpec((tile, width), lambda i, *_: (i, 0))
    half = pl.BlockSpec((tile, width // 2), lambda i, *_: (i, 0))
    return call(
        kernel,
        "join",
        [o0, o1, x, vec] + list(pieces.buffers),
        [half, half, tok, whole(vec.shape)] + [ANY] * count,
        (far((rows, width), F32), far((rows, 1), F32), like((rows, width)), far((width, rows)), like((width, width))),
        (tok, pl.BlockSpec((tile, 1), lambda i, *_: (i, 0)), tok, pl.BlockSpec((width, tile), lambda i, *_: (0, i)), HBM),
        grid=(rows // tile,),
        scalars=[pieces.cores],
        scratch=pieces.scratch(),
        after=after,
        time=7,
    )


def inner(h, rest, bias, run=0, runs=1, into=(), tile=512):
    rows, depth = h.shape
    cols = bias.shape[1]
    steps = cols // tile // runs

    def kernel(h_ref, w_ref, b_ref, u_ref, g_ref):
        f = dot(h_ref[...], w_ref[...]) + b_ref[...]
        weight = 0.5 + 0.5 * lax.erf(f * math.sqrt(0.5))
        u_ref[...] = (f * weight).astype(BF16)
        bell = jnp.exp2((f * f) * (-0.5 * math.log2(math.e)))
        g_ref[...] = (weight + (f * (1.0 / math.sqrt(2.0 * math.pi))) * bell).astype(BF16)

    at = lambda i: (0, run * steps + i)
    out = pl.BlockSpec((rows, tile), at)
    return call(
        kernel,
        "inner",
        [h, rest, bias],
        [whole(h.shape), pl.BlockSpec((depth, tile), at), pl.BlockSpec((1, tile), at)],
        (like((rows, cols)), like((rows, cols))),
        (out, out),
        grid=(steps,),
        into=into,
        time=9,
    )


def outer(pieces, u, n1, cot, vec, tile=256, after=()):
    rows, depth = u.shape
    width = n1.shape[1]
    count = len(pieces.buffers)

    def kernel(*refs):
        (cores_ref,), (u_ref, n_ref, c_ref, vec_ref), refs = refs[:1], refs[1 : 5], refs[5:]
        buffer_refs, (out_ref, dz_ref, dm_ref, dmt_ref, sums_ref, whole_ref, held, arrived, left) = refs[:count], refs[count:]
        write = pltpu.make_async_copy(held, whole_ref, left)

        @pl.when(pl.program_id(0) == 0)
        def _():
            sums_ref[...] = jnp.zeros_like(sums_ref)
            pieces.fetch(cores_ref, buffer_refs, held, arrived)
            write.start()

        row = lambda i: vec_ref[i : i + 1]
        z = (n_ref[...] * row(GAIN1) + row(SHIFT1)) + (dot(u_ref[...], held[...]) + row(BOUTER))
        n, rstd = normed(z)
        out_ref[...] = (n * row(GAIN2) + row(SHIFT2)).astype(BF16)
        c = c_ref[...].astype(F32)
        dz = norm_back(c * row(GAIN2), n, rstd)
        dz_ref[...] = dz
        dm = dz.astype(BF16)
        dm_ref[...] = dm
        dmt_ref[...] = dm.T
        sums_ref[0:1, :] += column_sum(dm)
        sums_ref[1:2, :] += column_sum(c * n)
        sums_ref[2:3, :] += column_sum(c)

        @pl.when(pl.program_id(0) == pl.num_programs(0) - 1)
        def _():
            write.wait()

    tok = pl.BlockSpec((tile, width), lambda i, *_: (i, 0))
    return call(
        kernel,
        "outer",
        [u, n1, cot, vec] + list(pieces.buffers),
        [pl.BlockSpec((tile, depth), lambda i, *_: (i, 0)), tok, tok, whole(vec.shape)] + [ANY] * count,
        (far((rows, width)), far((rows, width), F32), far((rows, width)), like((width, rows)), like((8, width), F32), like((depth, width))),
        (tok, tok, tok, pl.BlockSpec((width, tile), lambda i, *_: (0, i)), whole((8, width)), HBM),
        grid=(rows // tile,),
        scalars=[pieces.cores],
        scratch=pieces.scratch(),
        after=after,
        time=19,
    )


def outer_grad(half, dmt, u, groups, after=()):
    width, rows = dmt.shape
    cols = u.shape[1]
    part = cols // groups
    blocks = 2048 // part

    def kernel(half_ref, left_ref, right_ref, out_ref):
        made = dot(left_ref[...], right_ref[...]).astype(BF16)
        for i in range(blocks):
            out_ref[:, i] = made[:, i * part : (i + 1) * part].reshape(2, width // 4, part)

    return call(
        kernel,
        "outer_grad",
        [dmt, u],
        [pl.BlockSpec((width // 2, rows), lambda i, half: (half[0], 0)), pl.BlockSpec((rows, blocks * part), lambda i, half: (0, i))],
        like((2, groups, width // 4, part)),
        pl.BlockSpec((2, blocks, width // 4, part), lambda i, half: (0, i, 0, 0)),
        grid=(groups // blocks,),
        scalars=[half],
        after=after,
        time=6,
    )


def inner_back(halves, dm, w2, slope, ht, w1, groups, tile=512, after=()):
    rows, width = dm.shape
    cols = slope.shape[1]
    steps = cols // 2 // tile
    per = steps // 2

    def kernel(halves_ref, dm_ref, w2_ref, g_ref, ht_ref, w1_ref, first_ref, second_ref, dh_ref, sum_ref):
        step = pl.program_id(0)

        @pl.when(step == 0)
        def _():
            dh_ref[...] = jnp.zeros_like(dh_ref)

        df = (dot_nt(dm_ref[...], w2_ref[...]) * g_ref[...].astype(F32)).astype(BF16)
        sum_ref[...] = column_sum(df)
        made = dot(ht_ref[...], df).astype(BF16).reshape(first_ref.shape)

        @pl.when(step < steps)
        def _():
            first_ref[...] = made

        @pl.when(step >= steps)
        def _():
            second_ref[...] = made

        dh_ref[...] += dot_nt(df, w1_ref[...])

    at = lambda i, halves: halves[i // steps] * steps + i % steps
    grad = like((2, groups, width // groups, cols // 4))
    block = (1, groups, width // groups, tile)
    kept = lambda step: (step // per, 0, 0, step % per)
    return call(
        kernel,
        "inner_back",
        [dm, w2, slope, ht, w1],
        [
            whole(dm.shape),
            pl.BlockSpec((tile, width), lambda i, halves: (at(i, halves), 0)),
            pl.BlockSpec((rows, tile), lambda i, halves: (0, at(i, halves))),
            whole(ht.shape),
            pl.BlockSpec((width, tile), lambda i, halves: (0, at(i, halves))),
        ],
        (grad, grad, like((rows, width), F32), like((1, cols), F32)),
        (
            pl.BlockSpec(block, lambda i, halves: kept(jnp.minimum(i, steps - 1))),
            pl.BlockSpec(block, lambda i, halves: kept(jnp.maximum(i - steps, 0))),
            whole((rows, width)),
            pl.BlockSpec((1, tile), lambda i, halves: (0, at(i, halves))),
        ),
        grid=(2 * steps,),
        scalars=[halves],
        after=after,
        time=35,
    )


def join_back(dz2, dh, n1, rstd, vec, w, tile=256, after=()):
    rows, width = dz2.shape

    def kernel(dz2_ref, dh_ref, n_ref, r_ref, vec_ref, w_ref, dz_ref, da_ref, do_ref, sums_ref):
        @pl.when(pl.program_id(0) == 0)
        def _():
            sums_ref[...] = jnp.zeros_like(sums_ref)

        dh = dz2_ref[...] + dh_ref[...]
        n = n_ref[...]
        dz = norm_back(dh * vec_ref[GAIN1 : GAIN1 + 1], n, r_ref[...])
        dz_ref[...] = dz
        da = dz.astype(BF16)
        da_ref[...] = da
        do_ref[...] = dot_nt(da, w_ref[...]).astype(BF16)
        sums_ref[0:1, :] += column_sum(da)
        sums_ref[1:2, :] += column_sum(dh * n)
        sums_ref[2:3, :] += column_sum(dh)

    tok = pl.BlockSpec((tile, width), lambda i: (i, 0))
    return call(
        kernel,
        "join_back",
        [dz2, dh, n1, rstd, vec, w],
        [tok, tok, tok, pl.BlockSpec((tile, 1), lambda i: (i, 0)), whole(vec.shape), whole(w.shape)],
        (far((rows, width), F32), far((rows, width)), far((rows, width)), like((8, width), F32)),
        (tok, tok, tok, whole((8, width))),
        grid=(rows // tile,),
        after=after,
        time=8,
    )


def token_weights_grad(halves, xt, d, groups, mixed=None, vectors=(), carry=()):
    width, rows = xt.shape
    part = d.shape[2] // 2
    size, last = part // 2, width // 4
    keep = width // groups
    mixed_at = -(-3 * size // last) * last
    cols = mixed_at + last if mixed else 3 * size
    more = 16 if vectors else 0
    arrays = [a for group, _ in vectors for a in group]

    def kernel(halves_ref, left_ref, d_ref, *refs):
        def put(out_ref):
            at, read = keep, list(refs)
            for group, row in vectors:
                here, read = read[: len(group)], read[len(group) :]
                values = [jnp.sum(ref[...], axis=0) if len(ref.shape) == 3 else ref[row : row + 1] for ref in here]
                wide = values[0].shape[1]
                many = wide * len(group) // groups
                for g in range(groups):
                    for i in range(many // keep):
                        start = g * many + i * keep
                        piece = values[start // wide][:, start % wide : start % wide + keep].astype(BF16)
                        for x in range(2):
                            out_ref[x, g, at + i : at + i + 1, :keep] = piece
                at += many // keep

        def store(out_ref, made, start, group, blocks):
            wide = made.shape[1] // 2
            for x in range(2):
                piece = made[:, x * wide : (x + 1) * wide].reshape(blocks, keep, wide)
                out_ref[x, group : group + blocks, :keep, start : start + wide] = piece

        for step, out_ref in enumerate(refs[-2:]):

            @pl.when(pl.program_id(0) == step)
            def _():
                for which in range(3):
                    store(out_ref, dot(left_ref[...], d_ref[which]).astype(BF16), which * size, 0, groups)
                if mixed:
                    for i in range(2):
                        made = dot(refs[i][...], refs[2][...]).astype(BF16)
                        store(out_ref, made, mixed_at, i * groups // 2, groups // 2)
                    if mixed_at > 3 * size:
                        out_ref[:, :, :, 3 * size : mixed_at] = jnp.zeros((2, groups, keep, mixed_at - 3 * size), BF16)
                if more:
                    out_ref[:, :, keep:, :] = jnp.zeros((2, groups, more, cols), BF16)
                    put(out_ref)

    operands = [xt, d] + list(mixed or ()) + arrays
    specs = [whole(xt.shape), pl.BlockSpec((3, rows, part), lambda i, halves: (0, 0, halves[i]))]
    if mixed:
        specs += [whole(mixed[0].shape), whole(mixed[1].shape), pl.BlockSpec((rows, width // 2), lambda i, halves: (0, halves[i]))]
    specs += [whole(a.shape) for a in arrays]
    shape = (2, groups, keep + more, cols)
    return call(
        kernel,
        "token_weights_grad",
        operands,
        specs,
        (like(shape), like(shape)),
        (whole(shape), whole(shape)),
        grid=(2,),
        scalars=[halves],
        carry=carry,
        time=8,
    )


def token_grad(base, d, w, dtype, tile=256, after=()):
    rows, width = base.shape
    part = d.shape[2]

    def kernel(base_ref, d_ref, w_ref, out_ref):
        total = base_ref[...]
        for i in range(3):
            total = total + dot_nt(d_ref[i], w_ref[:, i * part : (i + 1) * part])
        out_ref[...] = total.astype(dtype)

    tok = pl.BlockSpec((tile, width), lambda i: (i, 0))
    return call(
        kernel,
        "token_grad",
        [base, d, w],
        [tok, pl.BlockSpec((3, tile, part), lambda i: (0, i, 0)), whole(w.shape)],
        like((rows, width), dtype),
        tok,
        grid=(rows // tile,),
        after=after,
        time=6,
    )


def digits_of(axis, total, base):
    digits, stride = [], total
    while stride > 1:
        size = base if stride % base == 0 else 2
        stride //= size
        digits.append((axis, stride, size))
    return digits


def total_of(terms):
    total = terms[0].astype(F32)
    for term in terms[1:]:
        total = total + term.astype(F32)
    return total.astype(BF16)


class Layout:
    def __init__(self, mesh):
        self.replicas, self.groups = mesh.shape["replica"], mesh.shape["group"]
        self.group = digits_of("group", self.groups, 4)
        replica = digits_of("replica", self.replicas, 2)
        self.core, self.over = replica[-1], replica[:-1]
        self.sizes = {"replica": self.replicas, "group": self.groups}
        self.devices = self.replicas * self.groups
        cores = self.core[2]
        self.same_core = [
            [r * self.groups + g for r in range(c, self.replicas, cores) for g in range(self.groups)] for c in range(cores)
        ]

    def place(self, digit):
        axis, stride, size = digit
        return (lax.axis_index(axis) // stride) % size

    def send(self, value, digit, shift=1):
        axis, stride, size = digit
        pairs = []
        for i in range(self.sizes[axis]):
            own = (i // stride) % size
            pairs.append((i, i + ((own + shift) % size - own) * stride))
        return lax.ppermute(value, axis, pairs)

    def sends(self, value, digit):
        return [self.send(value, digit, k) for k in range(1, digit[2])]

    def pieces(self, parts, shape):
        core = self.place(self.core).astype(jnp.int32)
        cores = jnp.stack([core, 1 - core])
        buffers, spans, start = [], [], 0
        for chain, cols in parts:
            came = self.send(chain.value, self.core)
            blocks = math.prod(d[2] for d in self.over)
            for buffer in (chain.value, came):
                buffers.append(buffer.reshape(blocks, -1, buffer.shape[-1]))
                spans.append((0, cols, start))
            start += cols
        return Pieces(cores, buffers, spans, shape)

    def along(self, digit):
        axis, stride, size = digit
        stride *= self.groups if axis == "replica" else 1
        starts = [d for d in range(self.devices) if d // stride % size == 0]
        return [[d + k * stride for k in range(size)] for d in starts]


class Chain:
    def __init__(self, layout, value, order, done=()):
        self.layout, self.value, self.order, self.done = layout, value, list(order), list(done)
        self.came = layout.sends(value, self.order[0]) if self.order else []

    def job(self, first=0, cols=None):
        digits = self.layout.over + self.layout.group
        axis = sum(digits.index(d) < digits.index(self.order[0]) for d in self.done)
        place = self.layout.place(self.order[0]).astype(jnp.int32).reshape(1)
        return [self.value] + self.came, place, axis, first, self.value.shape[-1] if cols is None else cols

    def after(self, value, order=None):
        return Chain(self.layout, value, (self.order if order is None else order)[1:], self.done + self.order[:1])


def move(*chains, carry=()):
    values = stack([c.job() for c in chains], carry)
    values, carried = values if carry else (values, ())
    moved = [c.after(v) for c, v in zip(chains, values)]
    return moved + list(carried)


class Reduction:
    def __init__(self, layout, terms, order):
        self.layout, self.dims, self.terms, self.order = layout, layout.over + layout.group, terms, list(order)

    def job(self):
        digit = self.digit = self.order.pop(0)
        axis = self.dims.index(digit)
        count = lambda dims: math.prod(d[2] for d in dims)
        shape = (count(self.dims[:axis]), digit[2], count(self.dims[axis + 1 :]))
        self.dims = self.dims[:axis] + self.dims[axis + 1 :]
        terms = [(t.reshape(shape + t.shape[-2:]), block, cols) for t, block, cols in self.terms]
        return self.layout.place(digit).astype(jnp.int32).reshape(1), terms

    def take(self, made):
        came = [self.layout.send(s, self.digit, k + 1) for k, s in enumerate(made[:-1])]
        self.terms = [(t, (0, 0), t.shape[-2:]) for t in [made[-1]] + came]

    def came(self):
        return [t for t, _, _ in self.terms[1:]]

    def last(self):
        return [t.reshape((-1,) + t.shape[-2:]) for t, _, _ in self.terms]


def step(*reductions, carry=(), after=()):
    jobs = [r.job() for r in reductions]
    if len({r.digit[2] for r in reductions}) == 1:
        made, carry = combine(jobs, carry, after)
    else:
        made = []
        for job in jobs:
            one, carry = combine([job], carry, after)
            made += one
    for reduction, one in zip(reductions, made):
        reduction.take(one)
    return carry


def local(layout, tokens, segment_ids, w_query, b_query, w_key, w_value, b_value, w_out, b_out, gain_first, shift_first, w_inner, b_inner, w_outer, b_outer, gain_second, shift_second, cotangent):
    LAST.clear()
    groups, devices = layout.groups, layout.devices
    seqs, length = segment_ids.shape
    width = tokens.shape[1]
    hidden = w_inner.shape[1]
    each = b_query.shape[0]
    half = width // 2
    core = layout.place(layout.core).astype(jnp.int32)
    mine, theirs = core.reshape(1), (1 - core).reshape(1)
    halves = jnp.concatenate([theirs, mine])
    z_digit, y_digits = layout.group[:1], layout.group[1:]
    zxy, zyx = z_digit + layout.over + y_digits, z_digit + y_digits + layout.over
    xyz, yxz = layout.over + y_digits + z_digit, y_digits + layout.over + z_digit

    vectors = (b_query, b_value, b_out, gain_first, shift_first, b_outer, gain_second, shift_second, b_inner)
    lanes, cut, wide = 128, 3 * half // 2, (3 * half + width) // 2
    (first,) = pack([w_query, w_key, w_value], [[(0, 0, half), (1, 0, half), (2, 0, half)]], vectors)
    high = first.shape[0]
    first = Chain(layout, first, zxy)
    xt = transposed(tokens)
    a, b = stack([first.job(0, cut), first.job(cut, cut + lanes)])
    a, b = first.after(a), first.after(b, zyx)
    second, last, inner_rows = pack(
        [w_query, w_key, w_value, w_out, w_outer, w_inner],
        [[(0, half, half), (1, half, half), (2, half, half), (3, 0, width)], [(4, 0, width)], [(5, 0, hidden)]],
    )
    whole_winner = lax.all_gather(inner_rows, ("replica", "group"), axis=0, tiled=True)
    a, b, second = move(a, b, carry=[second])
    second = Chain(layout, second, zxy)
    while a.order[1:]:
        a, b = move(a, b)
    va, vb, c, d = stack([a.job(), b.job(), second.job(0, wide), second.job(wide, wide)])
    a, b = a.after(va), b.after(vb)
    pieces0 = layout.pieces([(a, cut), (b, cut)], (width, 3 * half))
    c, d = second.after(c), second.after(d, zyx)
    spots = vector_places(vectors, high)
    used = max(r for r, _ in spots) + 1
    both = [v.reshape(-1, groups, high, v.shape[-1])[:, :, :used, cut:].astype(F32) for v in pieces0.buffers[-2:]]
    small = jnp.stack([jnp.where(core == k, both[0], both[1]) for k in range(2)], axis=1).reshape(devices, used, lanes)
    vec = jnp.stack([small[:, r, l : l + each].reshape(width) for r, l in spots[:-1]])
    r, l = spots[-1]
    whole_binner = small[:, r, l : l + b_inner.shape[0]].reshape(1, -1)
    row, col = segment_ids.reshape(seqs, 1, length), segment_ids.reshape(seqs, length, 1)

    (qkv0, wqkv0), (last,) = project(pieces0, tokens, vec, 0, carry=[last])
    last = Chain(layout, last, zxy)
    while c.order[1:]:
        c, d = move(c, d)
    o0, ot0, probs0, share0 = attend(qkv0, row, col)
    c_value, d_value, e, f = stack([c.job(), d.job(), last.job(0, half), last.job(half, half)])
    c, d = c.after(c_value), d.after(d_value)
    pieces1 = layout.pieces([(c, wide), (d, wide)], (width, 3 * half + width))
    e, f = last.after(e), last.after(f, zyx)
    qkv1, wqkv1 = project(pieces1.part(0, 3 * half), tokens, vec, 1)
    o1, ot1, probs1, share1 = attend(qkv1, row, col)
    while len(e.order) > 1:
        e, f = move(e, f)
    n1, rstd1, h, ht, whole_wout = join(pieces1.part(3 * half, width), o0, o1, tokens, vec)
    made = inner(h, whole_winner, whole_binner, 0, 2)
    e, f = move(e, f)
    pieces2 = layout.pieces([(e, half), (f, half)], (w_outer.shape[0] * devices, width))
    u, slope = inner(h, whole_winner, whole_binner, 1, 2, made)
    out, dz2, dm, dmt, sums2, whole_wouter = outer(pieces2, u, n1, cotangent, vec)

    def reduction(other, own, *orders, by_rows=False, runs=None):
        came = layout.send(other, layout.core)
        rows, cols = own.shape[2:]
        if by_rows:
            parts = [((i, 0), (rows // len(orders), cols)) for i in range(len(orders))]
        else:
            runs = runs or [(i * cols // len(orders), cols // len(orders)) for i in range(len(orders))]
            parts = [((0, start // size), (rows, size)) for start, size in runs]
        return [Reduction(layout, [(own,) + part, (came,) + part], order) for part, order in zip(parts, orders)]

    def along_z(reductions, carry=()):
        sums = add_up([[t.reshape(-1, t.shape[-1]) for t in r.last()] for r in reductions], carry)
        sums, carry = sums if carry else (sums, ())
        sums = lax.psum_scatter(sums, ("replica", "group"), scatter_dimension=0, axis_index_groups=layout.along(z_digit[0]), tiled=True)
        return [sums] + list(carry)

    def across_z(reductions, carry=()):
        made = gather_sums(layout.place(z_digit[0]).astype(jnp.int32).reshape(1), [r.last() for r in reductions], carry)
        made, carry = made if carry else (made, ())
        return [[made[-1]] + [layout.send(s, z_digit[0], k + 1) for k, s in enumerate(made[:-1])]] + list(carry)

    spread = lambda block: lax.all_gather(block, "replica", axis=0, tiled=False)
    middle = range(len(xyz) - 2)
    cols = 3 * half // 4
    other = outer_grad(theirs, dmt, u, groups)
    own = outer_grad(mine, dmt, u, groups)
    outers = reduction(other, own, xyz, yxz, by_rows=True)
    step(*outers)
    other, own, dh, sum_inner = inner_back(halves, dm, whole_wouter, slope, ht, whole_winner, groups)
    for _ in middle:
        (other,) = step(*outers, carry=[other])
    inners = reduction(other, own, xyz, yxz)
    dz1, da, do, sums1 = join_back(dz2, dh, n1, rstd1, vec, whole_wout)
    (got_wouter,) = along_z(outers)
    step(*inners)
    d0, sq0, sv0 = attend_back(qkv0, ot0, probs0, share0, do, 0)
    other, own = token_weights_grad(halves, xt, d0, groups, mixed=(ot0, ot1, da))
    for _ in middle:
        (other,) = step(*inners, carry=[other])
    firsts = reduction(other, own, xyz, yxz, runs=((0, cols), (other.shape[3] - width // 4, width // 4)))
    d1, sq1, sv1 = attend_back(qkv1, ot1, probs1, share1, do, 1)
    (got_winner,) = along_z(inners)
    step(*firsts)
    partial = token_grad(dz1, d0, wqkv0, F32)
    vectors = [((sq0, sq1), 0), ((sv0, sv1), 0)] + [((sums,), i) for sums in (sums1, sums2) for i in range(3)] + [((sum_inner,), 0)]
    other, own = token_weights_grad(halves, xt, d1, groups, vectors=vectors)
    for _ in middle:
        (other,) = step(*firsts, carry=[other])
    seconds = reduction(other, own, xyz, yxz, runs=((0, 2 * cols // 3), (2 * cols // 3, cols // 3)))
    cores = layout.core[2]
    order = [r % cores * (layout.replicas // cores) + r // cores for r in range(layout.replicas)]
    step(*seconds)
    (first_sums,) = across_z(firsts)
    together = got_wouter.shape[0] == got_winner.shape[0]
    if together:
        (got,) = pack([got_wouter, got_winner], [[(0, 0, got_wouter.shape[1]), (1, 0, got_winner.shape[1])]])
        got = spread(got)
    else:
        got_wouter, got_winner = spread(got_wouter), spread(got_winner)
    grad_tokens = token_grad(partial, d1, wqkv1, BF16)
    for _ in middle:
        step(*seconds, after=first_sums[1:])
    (second_sums,) = across_z(seconds)
    if together:
        grad_wouter, grad_winner = wide_results(got, order)
    else:
        grad_wouter, grad_winner = outer_result(got_wouter, order), inner_result(got_winner, order)
    got = [add_up([first_sums, second_sums])]
    places = jnp.zeros((1,), jnp.int32)
    weight = 1
    for digit in layout.over[::-1] + [layout.core]:
        own = layout.place(digit).astype(jnp.int32)
        places = jnp.concatenate([places + own * weight, places + (1 - own) * weight])
        got = got + [layout.send(g, digit) for g in got]
        weight *= digit[2]
    keep = width // groups
    wq, wk, wv, grad_wout, sums = token_weights_result(got, places, keep, half // 4, width // 4)
    bq, bv, bout, gain1, shift1, bouter, gain2, shift2 = (sums[i, :keep] for i in range(8))
    binner = sums[8 : 8 + hidden // width, :keep].reshape(-1)
    return (out, grad_tokens, wq, bq, wk, wv, bv, grad_wout, bout, gain1, shift1, grad_winner, binner, grad_wouter, bouter, gain2, shift2)


def solution(mesh):
    layout = Layout(mesh)
    both = ("replica", "group")
    rows, vector = P(both, None), P(both)
    in_specs = (rows, rows, rows, vector, rows, rows, vector, rows, vector, vector, vector, rows, vector, rows, vector, vector, vector, rows)
    kept, kept_vector = P("group", None), P("group")
    out_specs = (rows, rows, kept, kept_vector, kept, kept, kept_vector, kept, kept_vector, kept_vector, kept_vector, kept, kept_vector, kept, kept_vector, kept_vector, kept_vector)
    return jax.shard_map(functools.partial(local, layout), mesh=mesh, in_specs=in_specs, out_specs=out_specs, check_vma=False)
```

```python
import functools
import math

import jax
import jax.numpy as jnp
from jax import lax
from jax.experimental import pallas as pl
from jax.experimental.pallas import tpu as pltpu
from jax.sharding import PartitionSpec as P

F32 = jnp.float32
BF16 = jnp.bfloat16
VMEM_LIMIT = 46 * 1024 * 1024
ANY = pl.BlockSpec(memory_space=pl.ANY)
ALL_VMEM = 62 * 1024 * 1024
HBM = pl.BlockSpec(memory_space=pltpu.HBM)
BQ, BV, BOUT, GAIN1, SHIFT1, BOUTER, GAIN2, SHIFT2 = range(8)


LAST = []


def call(kernel, name, operands, in_specs, out_shape, out_specs, *, grid=(1,), scalars=(), after=(), carry=(), into=(), scratch=(), time=0, room=None):
    single = not isinstance(out_shape, (tuple, list))
    shapes, specs = ([out_shape], [out_specs]) if single else (list(out_shape), list(out_specs))
    first, made = len(scalars) + len(operands), len(shapes)
    ends = made + len(carry)
    unread = list(carry) + list(into) + list(after) + LAST

    limit = VMEM_LIMIT
    if room is not None:
        pairs = list(zip(specs, shapes)) + list(zip(in_specs, operands))
        blocks = [math.prod(spec.block_shape) * array.dtype.itemsize for spec, array in pairs if spec.block_shape is not None]
        limit = ALL_VMEM if room < 0 else min(VMEM_LIMIT, 2 * sum(blocks) + room)

    def body(*refs):
        outs = first + len(unread)
        kernel(*refs[:first], *refs[outs : outs + made], *refs[outs + ends + 1 :])

    outs = pl.pallas_call(
        body,
        out_shape=shapes + [jax.ShapeDtypeStruct(c.shape, c.dtype) for c in carry] + [jax.ShapeDtypeStruct((8, 128), F32)],
        grid_spec=pltpu.PrefetchScalarGridSpec(
            num_scalar_prefetch=len(scalars),
            grid=grid,
            in_specs=list(in_specs) + [HBM] * len(carry) + [ANY] * (len(unread) - len(carry) - len(LAST)) + [HBM] * len(LAST),
            out_specs=specs + [HBM] * (len(carry) + 1),
            scratch_shapes=list(scratch),
        ),
        input_output_aliases={first + i: made + i for i in range(len(carry))} | {first + len(carry) + i: i for i in range(len(into))},
        compiler_params=pltpu.CompilerParams(dimension_semantics=("arbitrary",) * len(grid), vmem_limit_bytes=limit),
        cost_estimate=pl.CostEstimate(flops=int(1 + time * 1e9), bytes_accessed=int(1 + time * 1e6), transcendentals=0),
        name=name,
    )(*scalars, *operands, *unread)
    LAST[:] = outs[ends:]
    result = outs[0] if single else tuple(outs[:made])
    return (result, outs[made:ends]) if carry else result


def like(shape, dtype=BF16):
    return jax.ShapeDtypeStruct(shape, dtype)


def far(shape, dtype=BF16):
    return pltpu.HBM(shape, dtype)


def dot(left, right):
    return lax.dot_general(left, right, (((1,), (0,)), ((), ())), preferred_element_type=F32)


def dot_nt(left, right):
    return lax.dot_general(left, right, (((1,), (1,)), ((), ())), preferred_element_type=F32)


def whole(shape):
    return pl.BlockSpec(shape, lambda *i: (0,) * len(shape))


def column_sum(value):
    return jnp.sum(value.astype(F32), axis=0, keepdims=True)


def pack(operands, makes, vectors=()):
    lanes = 128 if vectors else 0

    def kernel(*refs):
        outs = refs[len(operands) + len(vectors) :]
        for out_ref, pieces in zip(outs, makes):
            at = 0
            for which, start, size in pieces:
                out_ref[:, at : at + size] = refs[which][:, start : start + size]
                at += size
        if vectors:
            rows, cols = outs[0].shape
            outs[0][:, cols - lanes :] = jnp.zeros((rows, lanes), BF16)
            for ref, (row, lane) in zip(refs[len(operands) :], vector_places(vectors, rows)):
                size = ref.shape[0]
                start = cols - lanes + lane
                outs[0][row : row + 1, start : start + size] = ref[...].astype(F32).reshape(1, size).astype(BF16)

    shapes = [(operands[pieces[0][0]].shape[0], sum(p[2] for p in pieces)) for pieces in makes]
    if vectors:
        shapes[0] = (shapes[0][0], shapes[0][1] + lanes)
    everything = list(operands) + list(vectors)
    return call(kernel, "pack", everything, [whole(o.shape) for o in everything], [like(s) for s in shapes], [whole(s) for s in shapes], room=-1)


def vector_places(vectors, rows):
    size = vectors[0].shape[0]
    places = [(i % rows, i // rows * size) for i in range(len(vectors) - 1)]
    return places + [(8, 0) if rows > 8 else (0, 64)]


def stack(jobs, carry=()):
    flat = [array for arrays, *_ in jobs for array in arrays]
    shapes = []
    for arrays, _, axis, _, cols in jobs:
        shape = arrays[0].shape
        shapes.append(shape[:axis] + (len(arrays),) + shape[axis:-1] + (cols,))

    def kernel(*refs):
        place_refs, refs = refs[: len(jobs)], refs[len(jobs) :]
        ins, outs, arrived = refs[: len(flat)], refs[len(flat) : -1], refs[-1]
        copies = []
        for (arrays, _, axis, first, cols), place_ref, out_ref in zip(jobs, place_refs, outs):
            count = len(arrays)
            for k in range(count):
                ref = ins[len(copies)]
                source = ref.at[(slice(None),) * (len(ref.shape) - 1) + (pl.ds(first, cols),)]
                target = out_ref.at[(slice(None),) * axis + (lax.rem(place_ref[0] + count - k, count),)]
                copies.append(pltpu.make_async_copy(source, target, arrived.at[len(copies)]))
        for copy in copies:
            copy.start()
        for copy in copies:
            copy.wait()

    return call(
        kernel,
        "stack",
        flat,
        [ANY] * len(flat),
        [like(shape) for shape in shapes],
        [whole(shape) for shape in shapes],
        scalars=[job[1] for job in jobs],
        carry=carry,
        scratch=[pltpu.SemaphoreType.DMA((len(flat),))],
        room=4 << 20,
    )


def combine(jobs, carry=(), after=(), also=()):
    n = jobs[0][1][0][0].shape[1]
    sizes = []
    for _, terms in jobs:
        before, _, behind, _, _ = terms[0][0].shape
        sizes.append((before, behind) + terms[0][2])
    flat = [t for _, terms in jobs for t in terms]
    done = [a for arrays in also for a in arrays]

    def kernel(*refs):
        refs = refs[len(jobs) :]
        outs = refs[len(flat) + len(done) :]
        if also:

            @pl.when(pl.program_id(0) == 0)
            def _():
                add_side_by_side(also, refs[len(flat) : len(flat) + len(done)], outs[-1])

        i = 0
        for job, (_, terms) in enumerate(jobs):
            total = refs[i][:, 0].astype(F32)
            for ref in refs[i + 1 : i + len(terms)]:
                total = total + ref[:, 0].astype(F32)
            total = total.astype(BF16)
            i += len(terms)
            for j, out_ref in enumerate(outs[job * n : (job + 1) * n]):

                @pl.when(pl.program_id(0) == j)
                def _():
                    out_ref[...] = total

    def at(job, block):
        before, behind, rows, cols = sizes[job]
        return pl.BlockSpec((before, 1, behind, rows, cols), lambda i, *own: (0, lax.rem(own[job][0] + i + 1, n), 0) + block)

    joined = [(done[0].shape[0], sum(arrays[0].shape[1] for arrays in also))] if also else []
    made = call(
        kernel,
        "combine",
        [t[0] for t in flat] + done,
        [at(job, t[1]) for job, (_, terms) in enumerate(jobs) for t in terms] + [whole(a.shape) for a in done],
        [far(size) for size in sizes for _ in range(n)] + [like(shape) for shape in joined],
        [whole(size) for size in sizes for _ in range(n)] + [whole(shape) for shape in joined],
        grid=(n,),
        scalars=[own for own, _ in jobs],
        carry=carry,
        after=after,
        room=12 << 20,
    )
    made, carried = made if carry else (made, ())
    return [made[job * n : (job + 1) * n] for job in range(len(jobs))], carried, made[-1]


def add_side_by_side(lists, refs, out_ref):
    at, i = 0, 0
    for arrays in lists:
        total = refs[i][...].astype(F32)
        for ref in refs[i + 1 : i + len(arrays)]:
            total = total + ref[...].astype(F32)
        out_ref[:, at : at + total.shape[1]] = total.astype(BF16)
        at += total.shape[1]
        i += len(arrays)


def gather_sums(own, lists, carry=()):
    flat = [t for terms in lists for t in terms]
    n = flat[0].shape[0]
    rows = max(t.shape[1] for t in flat)
    cols = sum(terms[0].shape[2] for terms in lists)

    def kernel(own_ref, *refs):
        outs = refs[len(flat) :]
        parts, i = [], 0
        for terms in lists:
            total = refs[i][0].astype(F32)
            for ref in refs[i + 1 : i + len(terms)]:
                total = total + ref[0].astype(F32)
            parts.append(total.astype(BF16))
            i += len(terms)
        for j, out_ref in enumerate(outs):

            @pl.when(pl.program_id(0) == j)
            def _():
                at = 0
                for part in parts:
                    high, wide = part.shape
                    out_ref[:high, at : at + wide] = part
                    if high < rows:
                        out_ref[high:, at : at + wide] = jnp.zeros((rows - high, wide), BF16)
                    at += wide

    return call(
        kernel,
        "gather_sums",
        flat,
        [pl.BlockSpec((1,) + t.shape[1:], lambda i, own: (lax.rem(own[0] + i + 1, n), 0, 0)) for t in flat],
        [like((rows, cols))] * n,
        [whole((rows, cols))] * n,
        grid=(n,),
        scalars=[own],
        carry=carry,
        room=6 << 20,
    )


def add_up(lists, carry=()):
    flat = [a for arrays in lists for a in arrays]

    def kernel(*refs):
        at, i = 0, 0
        for arrays in lists:
            total = refs[i][...].astype(F32)
            for ref in refs[i + 1 : i + len(arrays)]:
                total = total + ref[...].astype(F32)
            rows, cols = total.shape
            refs[-1][:rows, at : at + cols] = total.astype(BF16)
            if rows < refs[-1].shape[0]:
                refs[-1][rows:, at : at + cols] = jnp.zeros((refs[-1].shape[0] - rows, cols), BF16)
            at += cols
            i += len(arrays)

    shape = (max(a.shape[0] for a in flat), sum(arrays[0].shape[1] for arrays in lists))
    return call(kernel, "add_up", flat, [whole(a.shape) for a in flat], like(shape), whole(shape), carry=carry, room=12 << 20)


def outer_result(got, order, runs=2):
    count, cols, rows = got.shape
    rows //= runs

    def kernel(got_ref, out_ref):
        for i, j in enumerate(order):
            for run in range(runs):
                at = (j * runs + run) * cols
                out_ref[:, at : at + cols] = got_ref[i, :, run * rows : (run + 1) * rows].astype(F32).T

    shape = (rows, count * runs * cols)
    return call(kernel, "outer_result", [got], [whole(got.shape)], like(shape, F32), whole(shape), room=8 << 20)


def inner_result(got, order):
    count, rows, cols = got.shape

    def kernel(got_ref, out_ref):
        for i, j in enumerate(order):
            out_ref[:, j * cols : (j + 1) * cols] = got_ref[i].astype(F32)

    shape = (rows, count * cols)
    return call(kernel, "inner_result", [got], [whole(got.shape)], like(shape, F32), whole(shape), room=8 << 20)


def wide_results(got, order, runs=2):
    count, rows, cols = got.shape
    high, wide = cols // 2 // runs, cols // 2

    def kernel(got_ref, first_ref, second_ref):
        for i, j in enumerate(order):
            for run in range(runs):
                at = (j * runs + run) * rows
                first_ref[:, at : at + rows] = got_ref[i, :, run * high : (run + 1) * high].astype(F32).T
            second_ref[:, j * wide : (j + 1) * wide] = got_ref[i, :, wide:].astype(F32)

    shapes = [(high, count * runs * rows), (rows, count * wide)]
    return call(kernel, "wide_results", [got], [whole(got.shape)], [like(s, F32) for s in shapes], [whole(s) for s in shapes], room=8 << 20)


def token_weights_result(pieces, places, keep, size, last):
    count = len(pieces)
    rows = pieces[0].shape[0]
    second = 3 * size + last

    def kernel(place_ref, *refs):
        outs = refs[count:]
        for i in range(count):
            at = lambda j, wide: pl.ds(pl.multiple_of(j * wide, wide), wide)
            piece = refs[i][:keep].astype(F32)
            for which in range(3):
                outs[which][:, at(place_ref[i], size)] = piece[:, which * size : (which + 1) * size]
                outs[which][:, at(count + place_ref[i], size)] = piece[:, second + which * size : second + (which + 1) * size]
            outs[3][:, at(place_ref[i], last)] = piece[:, 3 * size : second]
        outs[4][...] = refs[0][keep:, second:].astype(F32)

    shapes = [(keep, 2 * count * size)] * 3 + [(keep, count * last), (rows - keep, 3 * size)]
    return call(
        kernel,
        "token_weights_result",
        pieces,
        [whole(p.shape) for p in pieces],
        [like(s, F32) for s in shapes],
        [whole(s) for s in shapes],
        scalars=[places],
        room=8 << 20,
    )


def transposed(x, tile=256):
    rows, cols = x.shape

    def kernel(x_ref, out_ref):
        out_ref[...] = x_ref[...].T

    return call(
        kernel,
        "transposed",
        [x],
        [pl.BlockSpec((tile, cols), lambda i: (i, 0))],
        far((cols, rows)),
        pl.BlockSpec((cols, tile), lambda i: (0, i)),
        grid=(rows // tile,),
        time=3,
    )


class Pieces:
    def __init__(self, cores, buffers, spans, shape):
        self.cores, self.buffers, self.spans, self.shape = cores, buffers, spans, shape
        self.count = sum(b.shape[0] for b in buffers)

    def part(self, start, cols):
        kept = []
        for buffer, (first, size, to) in zip(self.buffers, self.spans):
            low, high = max(to, start), min(to + size, start + cols)
            kept.append((buffer, (first + low - to, high - low, low - start)))
        buffers, spans = zip(*(k for k in kept if k[1][1] > 0))
        return Pieces(self.cores, list(buffers), list(spans), (self.shape[0], cols))

    def scratch(self):
        return [pltpu.VMEM(self.shape, BF16), pltpu.SemaphoreType.DMA((self.count,)), pltpu.SemaphoreType.DMA]

    def fetch(self, cores_ref, refs, held, arrived):
        copies = []
        for i, (ref, (first, cols, to)) in enumerate(zip(refs, self.spans)):
            blocks, rows, _ = ref.shape
            for j in range(blocks):
                target = held.at[pl.ds(pl.multiple_of((2 * j + cores_ref[i % 2]) * rows, rows), rows), pl.ds(to, cols)]
                copies.append(pltpu.make_async_copy(ref.at[j, :, pl.ds(first, cols)], target, arrived.at[len(copies)]))
        for copy in copies:
            copy.start()
        for copy in copies:
            copy.wait()


def project(pieces, x, vec, half, carry=()):
    rows, depth = x.shape
    cols = pieces.shape[1]
    tile = cols // 3
    count = len(pieces.buffers)

    def kernel(*refs):
        (cores_ref,), (x_ref, vec_ref), refs = refs[:1], refs[1 : 3], refs[3:]
        buffer_refs, (out_ref, whole_ref, held, arrived, left) = refs[:count], refs[count:]
        step = pl.program_id(0)
        write = pltpu.make_async_copy(held, whole_ref, left)

        @pl.when(step == 0)
        def _():
            pieces.fetch(cores_ref, buffer_refs, held, arrived)
            write.start()

        at = slice(half * tile, (half + 1) * tile)
        for i, row in enumerate((BQ, None, BV)):

            @pl.when(step == i)
            def _():
                made = dot(x_ref[...], held[:, i * tile : (i + 1) * tile])
                out_ref[...] = (made if row is None else made + vec_ref[row : row + 1, at]).astype(BF16)

        @pl.when(step == 2)
        def _():
            write.wait()

    return call(
        kernel,
        "project",
        [x, vec] + list(pieces.buffers),
        [whole(x.shape), whole(vec.shape)] + [ANY] * count,
        (like((rows, cols)), like((depth, cols))),
        (pl.BlockSpec((rows, tile), lambda i, *_: (0, i)), HBM),
        grid=(3,),
        scalars=[pieces.cores],
        scratch=pieces.scratch(),
        carry=carry,
        time=6,
    )


def attend(qkv, row, col, heads=4, size=64, carry=()):
    seqs, _, length = row.shape
    width = qkv.shape[1] // 3
    block = heads * size
    blocks = width // block

    def kernel(q_ref, k_ref, v_ref, row_ref, col_ref, o_ref, ot_ref, p_ref, r_ref, bias_ref):
        @pl.when(pl.program_id(1) == 0)
        def _():
            bias_ref[...] = jnp.where(col_ref[0] == row_ref[0], 0.0, -1e9).astype(F32)

        qt = (q_ref[...] * jnp.asarray(0.125, BF16)).T
        vt = v_ref[...].T
        zero = jnp.zeros((size, length), BF16)
        for head in range(heads):
            here = slice(head * size, (head + 1) * size)
            pair = slice(head // 2 * 2 * size, (head // 2 + 1) * 2 * size)
            own = [qt[here], zero] if head % 2 == 0 else [zero, qt[here]]
            scores = dot(k_ref[:, pair], jnp.concatenate(own, axis=0)) + bias_ref[...]
            expo = jnp.exp(scores - jnp.max(scores, axis=0, keepdims=True))
            share = 1.0 / jnp.sum(expo, axis=0, keepdims=True)
            expo = expo.astype(BF16)
            p_ref[0, head] = expo
            r_ref[0, 0, head : head + 1] = share
            ot_ref[here, :] = (dot(vt[here], expo) * share).astype(BF16)
        o_ref[...] = ot_ref[...].T

    spec = lambda part: pl.BlockSpec((length, block), lambda s, p: (s, part * blocks + p))
    return call(
        kernel,
        "attend",
        [qkv, qkv, qkv, row, col],
        [spec(0), spec(1), spec(2), pl.BlockSpec((1, 1, length), lambda s, p: (s, 0, 0)), pl.BlockSpec((1, length, 1), lambda s, p: (s, 0, 0))],
        (like((seqs * length, width)), like((width, seqs * length)), like((seqs, heads * blocks, length, length)), like((seqs, blocks, heads, length), F32)),
        (
            pl.BlockSpec((length, block), lambda s, p: (s, p)),
            pl.BlockSpec((block, length), lambda s, p: (p, s)),
            pl.BlockSpec((1, heads, length, length), lambda s, p: (s, p, 0, 0)),
            pl.BlockSpec((1, 1, heads, length), lambda s, p: (s, p, 0, 0)),
        ),
        grid=(seqs, blocks),
        scratch=[pltpu.VMEM((length, length), F32)],
        carry=carry,
        time=11,
    )


def attend_back(qkv, ot, probs, share, do, part, carry=()):
    seqs, blocks, heads, length = share.shape
    tokens, width = ot.shape[1], ot.shape[0]
    block = width // blocks
    size = block // heads

    def kernel(q_ref, k_ref, v_ref, ot_ref, p_ref, r_ref, do_ref, d_ref, bq_ref, bv_ref):
        dot_t = do_ref[...].T.astype(F32)
        shares = jnp.concatenate([jnp.broadcast_to(r_ref[0, 0, h : h + 1], (size, length)) for h in range(heads)], axis=0)
        dot_t = (dot_t * shares).astype(BF16)
        do = dot_t.T
        kt = k_ref[...].T
        product = dot_t.astype(F32) * ot_ref[...].astype(F32)
        zero = jnp.zeros((size, length), BF16)
        first = lax.broadcasted_iota(jnp.int32, (1, 2 * size), 1) < size
        dk, dv, dqt = [], [], []
        for head in range(heads):
            here = slice(head * size, (head + 1) * size)
            pair = slice(head // 2 * 2 * size, (head // 2 + 1) * 2 * size)
            delta = jnp.sum(product[here], axis=0, keepdims=True)
            own = [dot_t[here], zero] if head % 2 == 0 else [zero, dot_t[here]]
            expo = p_ref[0, head]
            ds = (expo.astype(F32) * (dot(v_ref[:, pair], jnp.concatenate(own, axis=0)) - delta)).astype(BF16)
            dv.append(dot(expo, do[:, pair]))
            dk.append(dot(ds, q_ref[:, pair]))
            dqt.append(dot(kt[here], ds))
        paired = lambda parts: jnp.concatenate([jnp.where(first, parts[i], parts[i + 1]) for i in range(0, heads, 2)], axis=1)
        dq = (jnp.concatenate(dqt, axis=0) * 0.125).astype(BF16).T
        dv = paired(dv).astype(BF16)
        d_ref[0] = dq
        d_ref[1] = (paired(dk) * 0.125).astype(BF16)
        d_ref[2] = dv
        bq_ref[0] = column_sum(dq)
        bv_ref[0] = column_sum(dv)

    spec = lambda which: pl.BlockSpec((length, block), lambda s, p: (s, which * blocks + p))
    sums = pl.BlockSpec((1, 1, block), lambda s, p: (s, 0, p))
    return call(
        kernel,
        "attend_back",
        [qkv, qkv, qkv, ot, probs, share, do],
        [
            spec(0),
            spec(1),
            spec(2),
            pl.BlockSpec((block, length), lambda s, p: (p, s)),
            pl.BlockSpec((1, heads, length, length), lambda s, p: (s, p, 0, 0)),
            pl.BlockSpec((1, 1, heads, length), lambda s, p: (s, p, 0, 0)),
            spec(part),
        ],
        (far((3, tokens, width)), like((seqs, 1, width), F32), like((seqs, 1, width), F32)),
        (pl.BlockSpec((3, length, block), lambda s, p: (0, s, p)), sums, sums),
        grid=(seqs, blocks),
        carry=carry,
        time=11,
    )


def normed(z):
    center = z - jnp.mean(z, axis=-1, keepdims=True)
    rstd = lax.rsqrt(jnp.mean(center * center, axis=-1, keepdims=True) + 1e-06)
    return center * rstd, rstd


def norm_back(dn, n, rstd):
    return rstd * (dn - jnp.mean(dn, axis=-1, keepdims=True) - n * jnp.mean(dn * n, axis=-1, keepdims=True))


def join(pieces, o0, o1, x, vec, tile=256, after=()):
    rows, width = x.shape
    count = len(pieces.buffers)

    def kernel(*refs):
        (cores_ref,), (o0_ref, o1_ref, x_ref, vec_ref), refs = refs[:1], refs[1 : 5], refs[5:]
        buffer_refs, (n_ref, r_ref, h_ref, ht_ref, whole_ref, held, arrived, left) = refs[:count], refs[count:]
        write = pltpu.make_async_copy(held, whole_ref, left)

        @pl.when(pl.program_id(0) == 0)
        def _():
            pieces.fetch(cores_ref, buffer_refs, held, arrived)
            write.start()

        half = o0_ref.shape[1]
        mixed = dot(o0_ref[...], held[:half]) + dot(o1_ref[...], held[half:])
        z = x_ref[...].astype(F32) + (mixed + vec_ref[BOUT : BOUT + 1])
        n, rstd = normed(z)
        n_ref[...] = n
        r_ref[...] = rstd
        h = (n * vec_ref[GAIN1 : GAIN1 + 1] + vec_ref[SHIFT1 : SHIFT1 + 1]).astype(BF16)
        h_ref[...] = h
        ht_ref[...] = h.T

        @pl.when(pl.program_id(0) == pl.num_programs(0) - 1)
        def _():
            write.wait()

    tok = pl.BlockSpec((tile, width), lambda i, *_: (i, 0))
    half = pl.BlockSpec((tile, width // 2), lambda i, *_: (i, 0))
    return call(
        kernel,
        "join",
        [o0, o1, x, vec] + list(pieces.buffers),
        [half, half, tok, whole(vec.shape)] + [ANY] * count,
        (far((rows, width), F32), far((rows, 1), F32), like((rows, width)), far((width, rows)), like((width, width))),
        (tok, pl.BlockSpec((tile, 1), lambda i, *_: (i, 0)), tok, pl.BlockSpec((width, tile), lambda i, *_: (0, i)), HBM),
        grid=(rows // tile,),
        scalars=[pieces.cores],
        scratch=pieces.scratch(),
        after=after,
        time=7,
    )


def inner(h, rest, bias, run=0, runs=1, into=(), tile=512):
    rows, depth = h.shape
    cols = bias.shape[1]
    steps = cols // tile // runs

    def kernel(h_ref, w_ref, b_ref, u_ref, g_ref):
        f = dot(h_ref[...], w_ref[...]) + b_ref[...]
        weight = 0.5 + 0.5 * lax.erf(f * math.sqrt(0.5))
        u_ref[...] = (f * weight).astype(BF16)
        bell = jnp.exp2((f * f) * (-0.5 * math.log2(math.e)))
        g_ref[...] = (weight + (f * (1.0 / math.sqrt(2.0 * math.pi))) * bell).astype(BF16)

    at = lambda i: (0, run * steps + i)
    out = pl.BlockSpec((rows, tile), at)
    return call(
        kernel,
        "inner",
        [h, rest, bias],
        [whole(h.shape), pl.BlockSpec((depth, tile), at), pl.BlockSpec((1, tile), at)],
        (like((rows, cols)), like((rows, cols))),
        (out, out),
        grid=(steps,),
        into=into,
        time=9,
    )


def outer(pieces, u, n1, cot, vec, tile=256, after=()):
    rows, depth = u.shape
    width = n1.shape[1]
    count = len(pieces.buffers)

    def kernel(*refs):
        (cores_ref,), (u_ref, n_ref, c_ref, vec_ref), refs = refs[:1], refs[1 : 5], refs[5:]
        buffer_refs, (out_ref, dz_ref, dm_ref, dmt_ref, sums_ref, whole_ref, held, arrived, left) = refs[:count], refs[count:]
        write = pltpu.make_async_copy(held, whole_ref, left)

        @pl.when(pl.program_id(0) == 0)
        def _():
            sums_ref[...] = jnp.zeros_like(sums_ref)
            pieces.fetch(cores_ref, buffer_refs, held, arrived)
            write.start()

        row = lambda i: vec_ref[i : i + 1]
        z = (n_ref[...] * row(GAIN1) + row(SHIFT1)) + (dot(u_ref[...], held[...]) + row(BOUTER))
        n, rstd = normed(z)
        out_ref[...] = (n * row(GAIN2) + row(SHIFT2)).astype(BF16)
        c = c_ref[...].astype(F32)
        dz = norm_back(c * row(GAIN2), n, rstd)
        dz_ref[...] = dz
        dm = dz.astype(BF16)
        dm_ref[...] = dm
        dmt_ref[...] = dm.T
        sums_ref[0:1, :] += column_sum(dm)
        sums_ref[1:2, :] += column_sum(c * n)
        sums_ref[2:3, :] += column_sum(c)

        @pl.when(pl.program_id(0) == pl.num_programs(0) - 1)
        def _():
            write.wait()

    tok = pl.BlockSpec((tile, width), lambda i, *_: (i, 0))
    return call(
        kernel,
        "outer",
        [u, n1, cot, vec] + list(pieces.buffers),
        [pl.BlockSpec((tile, depth), lambda i, *_: (i, 0)), tok, tok, whole(vec.shape)] + [ANY] * count,
        (far((rows, width)), far((rows, width), F32), far((rows, width)), like((width, rows)), like((8, width), F32), like((depth, width))),
        (tok, tok, tok, pl.BlockSpec((width, tile), lambda i, *_: (0, i)), whole((8, width)), HBM),
        grid=(rows // tile,),
        scalars=[pieces.cores],
        scratch=pieces.scratch(),
        after=after,
        time=19,
    )


def outer_grad(half, dmt, u, groups, after=()):
    width, rows = dmt.shape
    cols = u.shape[1]
    part = cols // groups
    blocks = 2048 // part

    def kernel(half_ref, left_ref, right_ref, out_ref):
        made = dot(left_ref[...], right_ref[...]).astype(BF16)
        for i in range(blocks):
            out_ref[:, i] = made[:, i * part : (i + 1) * part].reshape(2, width // 4, part)

    return call(
        kernel,
        "outer_grad",
        [dmt, u],
        [pl.BlockSpec((width // 2, rows), lambda i, half: (half[0], 0)), pl.BlockSpec((rows, blocks * part), lambda i, half: (0, i))],
        like((2, groups, width // 4, part)),
        pl.BlockSpec((2, blocks, width // 4, part), lambda i, half: (0, i, 0, 0)),
        grid=(groups // blocks,),
        scalars=[half],
        after=after,
        time=6,
    )


def inner_back(halves, dm, w2, slope, ht, w1, groups, tile=512, after=()):
    rows, width = dm.shape
    cols = slope.shape[1]
    steps = cols // 2 // tile
    per = steps // 2

    def kernel(halves_ref, dm_ref, w2_ref, g_ref, ht_ref, w1_ref, first_ref, second_ref, dh_ref, sum_ref):
        step = pl.program_id(0)

        @pl.when(step == 0)
        def _():
            dh_ref[...] = jnp.zeros_like(dh_ref)

        df = (dot_nt(dm_ref[...], w2_ref[...]) * g_ref[...].astype(F32)).astype(BF16)
        sum_ref[...] = column_sum(df)
        made = dot(ht_ref[...], df).astype(BF16).reshape(first_ref.shape)

        @pl.when(step < steps)
        def _():
            first_ref[...] = made

        @pl.when(step >= steps)
        def _():
            second_ref[...] = made

        dh_ref[...] += dot_nt(df, w1_ref[...])

    at = lambda i, halves: halves[i // steps] * steps + i % steps
    grad = like((2, groups, width // groups, cols // 4))
    block = (1, groups, width // groups, tile)
    kept = lambda step: (step // per, 0, 0, step % per)
    return call(
        kernel,
        "inner_back",
        [dm, w2, slope, ht, w1],
        [
            whole(dm.shape),
            pl.BlockSpec((tile, width), lambda i, halves: (at(i, halves), 0)),
            pl.BlockSpec((rows, tile), lambda i, halves: (0, at(i, halves))),
            whole(ht.shape),
            pl.BlockSpec((width, tile), lambda i, halves: (0, at(i, halves))),
        ],
        (grad, grad, like((rows, width), F32), like((1, cols), F32)),
        (
            pl.BlockSpec(block, lambda i, halves: kept(jnp.minimum(i, steps - 1))),
            pl.BlockSpec(block, lambda i, halves: kept(jnp.maximum(i - steps, 0))),
            whole((rows, width)),
            pl.BlockSpec((1, tile), lambda i, halves: (0, at(i, halves))),
        ),
        grid=(2 * steps,),
        scalars=[halves],
        after=after,
        time=35,
    )


def join_back(dz2, dh, n1, rstd, vec, w, tile=256, after=()):
    rows, width = dz2.shape

    def kernel(dz2_ref, dh_ref, n_ref, r_ref, vec_ref, w_ref, dz_ref, da_ref, do_ref, sums_ref):
        @pl.when(pl.program_id(0) == 0)
        def _():
            sums_ref[...] = jnp.zeros_like(sums_ref)

        dh = dz2_ref[...] + dh_ref[...]
        n = n_ref[...]
        dz = norm_back(dh * vec_ref[GAIN1 : GAIN1 + 1], n, r_ref[...])
        dz_ref[...] = dz
        da = dz.astype(BF16)
        da_ref[...] = da
        do_ref[...] = dot_nt(da, w_ref[...]).astype(BF16)
        sums_ref[0:1, :] += column_sum(da)
        sums_ref[1:2, :] += column_sum(dh * n)
        sums_ref[2:3, :] += column_sum(dh)

    tok = pl.BlockSpec((tile, width), lambda i: (i, 0))
    return call(
        kernel,
        "join_back",
        [dz2, dh, n1, rstd, vec, w],
        [tok, tok, tok, pl.BlockSpec((tile, 1), lambda i: (i, 0)), whole(vec.shape), whole(w.shape)],
        (far((rows, width), F32), far((rows, width)), far((rows, width)), like((8, width), F32)),
        (tok, tok, tok, whole((8, width))),
        grid=(rows // tile,),
        after=after,
        time=8,
    )


def token_weights_grad(halves, xt, d, groups, mixed=None, vectors=(), carry=()):
    width, rows = xt.shape
    part = d.shape[2] // 2
    size, last = part // 2, width // 4
    keep = width // groups
    mixed_at = -(-3 * size // last) * last
    cols = mixed_at + last if mixed else 3 * size
    more = 16 if vectors else 0
    arrays = [a for group, _ in vectors for a in group]

    def kernel(halves_ref, left_ref, d_ref, *refs):
        def put(out_ref):
            at, read = keep, list(refs)
            for group, row in vectors:
                here, read = read[: len(group)], read[len(group) :]
                values = [jnp.sum(ref[...], axis=0) if len(ref.shape) == 3 else ref[row : row + 1] for ref in here]
                wide = values[0].shape[1]
                many = wide * len(group) // groups
                for g in range(groups):
                    for i in range(many // keep):
                        start = g * many + i * keep
                        piece = values[start // wide][:, start % wide : start % wide + keep].astype(BF16)
                        for x in range(2):
                            out_ref[x, g, at + i : at + i + 1, :keep] = piece
                at += many // keep

        def store(out_ref, made, start, group, blocks):
            wide = made.shape[1] // 2
            for x in range(2):
                piece = made[:, x * wide : (x + 1) * wide].reshape(blocks, keep, wide)
                out_ref[x, group : group + blocks, :keep, start : start + wide] = piece

        for step, out_ref in enumerate(refs[-2:]):

            @pl.when(pl.program_id(0) == step)
            def _():
                for which in range(3):
                    store(out_ref, dot(left_ref[...], d_ref[which]).astype(BF16), which * size, 0, groups)
                if mixed:
                    for i in range(2):
                        made = dot(refs[i][...], refs[2][...]).astype(BF16)
                        store(out_ref, made, mixed_at, i * groups // 2, groups // 2)
                    if mixed_at > 3 * size:
                        out_ref[:, :, :, 3 * size : mixed_at] = jnp.zeros((2, groups, keep, mixed_at - 3 * size), BF16)
                if more:
                    out_ref[:, :, keep:, :] = jnp.zeros((2, groups, more, cols), BF16)
                    put(out_ref)

    operands = [xt, d] + list(mixed or ()) + arrays
    specs = [whole(xt.shape), pl.BlockSpec((3, rows, part), lambda i, halves: (0, 0, halves[i]))]
    if mixed:
        specs += [whole(mixed[0].shape), whole(mixed[1].shape), pl.BlockSpec((rows, width // 2), lambda i, halves: (0, halves[i]))]
    specs += [whole(a.shape) for a in arrays]
    shape = (2, groups, keep + more, cols)
    return call(
        kernel,
        "token_weights_grad",
        operands,
        specs,
        (like(shape), like(shape)),
        (whole(shape), whole(shape)),
        grid=(2,),
        scalars=[halves],
        carry=carry,
        time=8,
    )


def token_grad(base, d, w, dtype, tile=256, after=()):
    rows, width = base.shape
    part = d.shape[2]

    def kernel(base_ref, d_ref, w_ref, out_ref):
        total = base_ref[...]
        for i in range(3):
            total = total + dot_nt(d_ref[i], w_ref[:, i * part : (i + 1) * part])
        out_ref[...] = total.astype(dtype)

    tok = pl.BlockSpec((tile, width), lambda i: (i, 0))
    return call(
        kernel,
        "token_grad",
        [base, d, w],
        [tok, pl.BlockSpec((3, tile, part), lambda i: (0, i, 0)), whole(w.shape)],
        like((rows, width), dtype),
        tok,
        grid=(rows // tile,),
        after=after,
        time=6,
    )


def digits_of(axis, total, base):
    digits, stride = [], total
    while stride > 1:
        size = base if stride % base == 0 else 2
        stride //= size
        digits.append((axis, stride, size))
    return digits


def total_of(terms):
    total = terms[0].astype(F32)
    for term in terms[1:]:
        total = total + term.astype(F32)
    return total.astype(BF16)


class Layout:
    def __init__(self, mesh):
        self.replicas, self.groups = mesh.shape["replica"], mesh.shape["group"]
        self.group = digits_of("group", self.groups, 4)
        replica = digits_of("replica", self.replicas, 2)
        self.core, self.over = replica[-1], replica[:-1]
        self.sizes = {"replica": self.replicas, "group": self.groups}
        self.devices = self.replicas * self.groups
        cores = self.core[2]
        self.same_core = [
            [r * self.groups + g for r in range(c, self.replicas, cores) for g in range(self.groups)] for c in range(cores)
        ]

    def place(self, digit):
        axis, stride, size = digit
        return (lax.axis_index(axis) // stride) % size

    def send(self, value, digit, shift=1):
        axis, stride, size = digit
        pairs = []
        for i in range(self.sizes[axis]):
            own = (i // stride) % size
            pairs.append((i, i + ((own + shift) % size - own) * stride))
        return lax.ppermute(value, axis, pairs)

    def sends(self, value, digit):
        return [self.send(value, digit, k) for k in range(1, digit[2])]

    def pieces(self, parts, shape):
        core = self.place(self.core).astype(jnp.int32)
        cores = jnp.stack([core, 1 - core])
        buffers, spans, start = [], [], 0
        for chain, cols in parts:
            came = self.send(chain.value, self.core)
            blocks = math.prod(d[2] for d in self.over)
            for buffer in (chain.value, came):
                buffers.append(buffer.reshape(blocks, -1, buffer.shape[-1]))
                spans.append((0, cols, start))
            start += cols
        return Pieces(cores, buffers, spans, shape)

    def along(self, digit):
        axis, stride, size = digit
        stride *= self.groups if axis == "replica" else 1
        starts = [d for d in range(self.devices) if d // stride % size == 0]
        return [[d + k * stride for k in range(size)] for d in starts]


class Chain:
    def __init__(self, layout, value, order, done=()):
        self.layout, self.value, self.order, self.done = layout, value, list(order), list(done)
        self.came = layout.sends(value, self.order[0]) if self.order else []

    def job(self, first=0, cols=None):
        digits = self.layout.over + self.layout.group
        axis = sum(digits.index(d) < digits.index(self.order[0]) for d in self.done)
        place = self.layout.place(self.order[0]).astype(jnp.int32).reshape(1)
        return [self.value] + self.came, place, axis, first, self.value.shape[-1] if cols is None else cols

    def after(self, value, order=None):
        return Chain(self.layout, value, (self.order if order is None else order)[1:], self.done + self.order[:1])


def move(*chains, carry=()):
    values = stack([c.job() for c in chains], carry)
    values, carried = values if carry else (values, ())
    moved = [c.after(v) for c, v in zip(chains, values)]
    return moved + list(carried)


class Reduction:
    def __init__(self, layout, terms, order):
        self.layout, self.dims, self.terms, self.order = layout, layout.over + layout.group, terms, list(order)

    def job(self):
        digit = self.digit = self.order.pop(0)
        axis = self.dims.index(digit)
        count = lambda dims: math.prod(d[2] for d in dims)
        shape = (count(self.dims[:axis]), digit[2], count(self.dims[axis + 1 :]))
        self.dims = self.dims[:axis] + self.dims[axis + 1 :]
        terms = [(t.reshape(shape + t.shape[-2:]), block, cols) for t, block, cols in self.terms]
        return self.layout.place(digit).astype(jnp.int32).reshape(1), terms

    def take(self, made):
        came = [self.layout.send(s, self.digit, k + 1) for k, s in enumerate(made[:-1])]
        self.terms = [(t, (0, 0), t.shape[-2:]) for t in [made[-1]] + came]

    def came(self):
        return [t for t, _, _ in self.terms[1:]]

    def last(self):
        return [t.reshape((-1,) + t.shape[-2:]) for t, _, _ in self.terms]


def step(*reductions, carry=(), after=(), also=()):
    jobs = [r.job() for r in reductions]
    if len({r.digit[2] for r in reductions}) == 1:
        made, carry, total = combine(jobs, carry, after, also)
    else:
        made, total = [], add_up(also) if also else None
        for job in jobs:
            one, carry, _ = combine([job], carry, after)
            made += one
    for reduction, one in zip(reductions, made):
        reduction.take(one)
    return total if also else carry


def local(layout, tokens, segment_ids, w_query, b_query, w_key, w_value, b_value, w_out, b_out, gain_first, shift_first, w_inner, b_inner, w_outer, b_outer, gain_second, shift_second, cotangent):
    LAST.clear()
    groups, devices = layout.groups, layout.devices
    seqs, length = segment_ids.shape
    width = tokens.shape[1]
    hidden = w_inner.shape[1]
    each = b_query.shape[0]
    half = width // 2
    core = layout.place(layout.core).astype(jnp.int32)
    mine, theirs = core.reshape(1), (1 - core).reshape(1)
    halves = jnp.concatenate([theirs, mine])
    z_digit, y_digits = layout.group[:1], layout.group[1:]
    zxy, zyx = z_digit + layout.over + y_digits, z_digit + y_digits + layout.over
    xyz, yxz = layout.over + y_digits + z_digit, y_digits + layout.over + z_digit

    vectors = (b_query, b_value, b_out, gain_first, shift_first, b_outer, gain_second, shift_second, b_inner)
    lanes, cut, wide = 128, 3 * half // 2, (3 * half + width) // 2
    (first,) = pack([w_query, w_key, w_value], [[(0, 0, half), (1, 0, half), (2, 0, half)]], vectors)
    high = first.shape[0]
    first = Chain(layout, first, zxy)
    xt = transposed(tokens)
    a, b = stack([first.job(0, cut), first.job(cut, cut + lanes)])
    a, b = first.after(a), first.after(b, zyx)
    second, last, inner_rows = pack(
        [w_query, w_key, w_value, w_out, w_outer, w_inner],
        [[(0, half, half), (1, half, half), (2, half, half), (3, 0, width)], [(4, 0, width)], [(5, 0, hidden)]],
    )
    whole_winner = lax.all_gather(inner_rows, ("replica", "group"), axis=0, tiled=True)
    a, b, second = move(a, b, carry=[second])
    second = Chain(layout, second, zxy)
    while a.order[1:]:
        a, b = move(a, b)
    va, vb, c, d = stack([a.job(), b.job(), second.job(0, wide), second.job(wide, wide)])
    a, b = a.after(va), b.after(vb)
    pieces0 = layout.pieces([(a, cut), (b, cut)], (width, 3 * half))
    c, d = second.after(c), second.after(d, zyx)
    spots = vector_places(vectors, high)
    used = max(r for r, _ in spots) + 1
    both = [v.reshape(-1, groups, high, v.shape[-1])[:, :, :used, cut:].astype(F32) for v in pieces0.buffers[-2:]]
    small = jnp.stack([jnp.where(core == k, both[0], both[1]) for k in range(2)], axis=1).reshape(devices, used, lanes)
    vec = jnp.stack([small[:, r, l : l + each].reshape(width) for r, l in spots[:-1]])
    r, l = spots[-1]
    whole_binner = small[:, r, l : l + b_inner.shape[0]].reshape(1, -1)
    row, col = segment_ids.reshape(seqs, 1, length), segment_ids.reshape(seqs, length, 1)

    (qkv0, wqkv0), (last,) = project(pieces0, tokens, vec, 0, carry=[last])
    last = Chain(layout, last, zxy)
    while c.order[1:]:
        c, d = move(c, d)
    o0, ot0, probs0, share0 = attend(qkv0, row, col)
    c_value, d_value, e, f = stack([c.job(), d.job(), last.job(0, half), last.job(half, half)])
    c, d = c.after(c_value), d.after(d_value)
    pieces1 = layout.pieces([(c, wide), (d, wide)], (width, 3 * half + width))
    e, f = last.after(e), last.after(f, zyx)
    qkv1, wqkv1 = project(pieces1.part(0, 3 * half), tokens, vec, 1)
    o1, ot1, probs1, share1 = attend(qkv1, row, col)
    while len(e.order) > 1:
        e, f = move(e, f)
    n1, rstd1, h, ht, whole_wout = join(pieces1.part(3 * half, width), o0, o1, tokens, vec)
    made = inner(h, whole_winner, whole_binner, 0, 2)
    e, f = move(e, f)
    pieces2 = layout.pieces([(e, half), (f, half)], (w_outer.shape[0] * devices, width))
    u, slope = inner(h, whole_winner, whole_binner, 1, 2, made)
    out, dz2, dm, dmt, sums2, whole_wouter = outer(pieces2, u, n1, cotangent, vec)

    def reduction(other, own, *orders, by_rows=False, runs=None):
        came = layout.send(other, layout.core)
        rows, cols = own.shape[2:]
        if by_rows:
            parts = [((i, 0), (rows // len(orders), cols)) for i in range(len(orders))]
        else:
            runs = runs or [(i * cols // len(orders), cols // len(orders)) for i in range(len(orders))]
            parts = [((0, start // size), (rows, size)) for start, size in runs]
        return [Reduction(layout, [(own,) + part, (came,) + part], order) for part, order in zip(parts, orders)]

    def flat(reductions):
        return [[t.reshape(-1, t.shape[-1]) for t in r.last()] for r in reductions]

    def along_z(sums):
        return lax.psum_scatter(sums, ("replica", "group"), scatter_dimension=0, axis_index_groups=layout.along(z_digit[0]), tiled=True)

    def across_z(reductions, carry=()):
        made = gather_sums(layout.place(z_digit[0]).astype(jnp.int32).reshape(1), [r.last() for r in reductions], carry)
        made, carry = made if carry else (made, ())
        return [[made[-1]] + [layout.send(s, z_digit[0], k + 1) for k, s in enumerate(made[:-1])]] + list(carry)

    spread = lambda block: lax.all_gather(block, "replica", axis=0, tiled=False)
    middle = range(len(xyz) - 2)
    cols = 3 * half // 4
    other = outer_grad(theirs, dmt, u, groups)
    own = outer_grad(mine, dmt, u, groups)
    outers = reduction(other, own, xyz, yxz, by_rows=True)
    step(*outers)
    other, own, dh, sum_inner = inner_back(halves, dm, whole_wouter, slope, ht, whole_winner, groups)
    for _ in middle:
        (other,) = step(*outers, carry=[other])
    inners = reduction(other, own, xyz, yxz)
    dz1, da, do, sums1 = join_back(dz2, dh, n1, rstd1, vec, whole_wout)
    got_wouter = along_z(step(*inners, also=flat(outers)))
    d0, sq0, sv0 = attend_back(qkv0, ot0, probs0, share0, do, 0)
    other, own = token_weights_grad(halves, xt, d0, groups, mixed=(ot0, ot1, da))
    for _ in middle:
        (other,) = step(*inners, carry=[other])
    firsts = reduction(other, own, xyz, yxz, runs=((0, cols), (other.shape[3] - width // 4, width // 4)))
    d1, sq1, sv1 = attend_back(qkv1, ot1, probs1, share1, do, 1)
    got_winner = along_z(step(*firsts, also=flat(inners)))
    partial = token_grad(dz1, d0, wqkv0, F32)
    vectors = [((sq0, sq1), 0), ((sv0, sv1), 0)] + [((sums,), i) for sums in (sums1, sums2) for i in range(3)] + [((sum_inner,), 0)]
    other, own = token_weights_grad(halves, xt, d1, groups, vectors=vectors)
    for _ in middle:
        (other,) = step(*firsts, carry=[other])
    seconds = reduction(other, own, xyz, yxz, runs=((0, 2 * cols // 3), (2 * cols // 3, cols // 3)))
    cores = layout.core[2]
    order = [r % cores * (layout.replicas // cores) + r // cores for r in range(layout.replicas)]
    step(*seconds)
    (first_sums,) = across_z(firsts)
    together = got_wouter.shape[0] == got_winner.shape[0]
    if together:
        (got,) = pack([got_wouter, got_winner], [[(0, 0, got_wouter.shape[1]), (1, 0, got_winner.shape[1])]])
        got = spread(got)
    else:
        got_wouter, got_winner = spread(got_wouter), spread(got_winner)
    grad_tokens = token_grad(partial, d1, wqkv1, BF16)
    for _ in middle:
        step(*seconds, after=first_sums[1:])
    (second_sums,) = across_z(seconds)
    if together:
        grad_wouter, grad_winner = wide_results(got, order)
    else:
        grad_wouter, grad_winner = outer_result(got_wouter, order), inner_result(got_winner, order)
    got = [add_up([first_sums, second_sums])]
    places = jnp.zeros((1,), jnp.int32)
    weight = 1
    for digit in layout.over[::-1] + [layout.core]:
        own = layout.place(digit).astype(jnp.int32)
        places = jnp.concatenate([places + own * weight, places + (1 - own) * weight])
        got = got + [layout.send(g, digit) for g in got]
        weight *= digit[2]
    keep = width // groups
    wq, wk, wv, grad_wout, sums = token_weights_result(got, places, keep, half // 4, width // 4)
    bq, bv, bout, gain1, shift1, bouter, gain2, shift2 = (sums[i, :keep] for i in range(8))
    binner = sums[8 : 8 + hidden // width, :keep].reshape(-1)
    return (out, grad_tokens, wq, bq, wk, wv, bv, grad_wout, bout, gain1, shift1, grad_winner, binner, grad_wouter, bouter, gain2, shift2)


def solution(mesh):
    layout = Layout(mesh)
    both = ("replica", "group")
    rows, vector = P(both, None), P(both)
    in_specs = (rows, rows, rows, vector, rows, rows, vector, rows, vector, vector, vector, rows, vector, rows, vector, vector, vector, rows)
    kept, kept_vector = P("group", None), P("group")
    out_specs = (rows, rows, kept, kept_vector, kept, kept, kept_vector, kept, kept_vector, kept_vector, kept_vector, kept, kept_vector, kept, kept_vector, kept_vector, kept_vector)
    return jax.shard_map(functools.partial(local, layout), mesh=mesh, in_specs=in_specs, out_specs=out_specs, check_vma=False)
```
